32 devices in a mesh: obs: 4 (over z), lat: 8 (over y, x, core).
Axes of the slice: x: 2, y: 2, z: 4, core: 2. Of those that a mesh axis runs over, the one named last changes fastest.
Arguments:
- footprints: bfloat16 [4, 8, 384, 128, 128], P('obs', 'lat'), may hold values from -0.078125 to 0.078125
- block_rows: int32 [4, 8, 384], P('obs', 'lat'), may hold values from 0 to 31
- block_cols: int32 [4, 8, 384], P('obs', 'lat'), may hold values from 0 to 639
- block_scale: int32 [4, 8, 384], P('obs', 'lat'), may hold values from 0 to 3
- lat_width: int32 [256], replicated, may hold values from 1 to 32, as said below
- lon_width: int32 [256], replicated, may hold values from 1 to 80
- obs_weight: float32 [16384], P('obs'), may hold values from 0.3 to 3
- solution: float32 [8, 4, 256, 640], P(None, None, 'lat'), may hold values from -6 to 6
- residual: float32 [8, 4, 256, 640], P(None, None, 'lat'), may hold values from -6 to 6
- direction: float32 [8, 4, 256, 640], P(None, None, 'lat'), may hold values from -6 to 6
Outputs:
- next_solution: float32 [8, 4, 256, 640], P(None, None, 'lat')
- next_residual: float32 [8, 4, 256, 640], P(None, None, 'lat')
- next_direction: float32 [8, 4, 256, 640], P(None, None, 'lat')
The draws below stay inside these ranges and needn't reach their ends.
Inputs may be any that keep to these rules, and one draw needn't show every extreme that they name: `lat_width`: some latitude row has band width exactly 32.
All inputs are finite; a program needn't handle non-finite values.
Results may differ from the reference program's by a relative error of at most 0.00039.
Values may be sent and summed in bfloat16 or wider, within the bound.
No kernel may reach another device: no remote copies, remote signals or barrier semaphores. Data moves between devices by JAX's collectives and lax.ppermute only.
A program may use at most 128 MiB of HBM per device.

```python
import math
import jax
import jax.numpy as jnp
from jax import lax

K = 8
BLOCK = 128
RB_DEV = 32
LAT_DEV = 32
NLON = 640
WEEKS = 4
NBLK = 384
OBS_DEV = 4096
SOUNDINGS = 16384
NLAT = 256
CB_DEV = 640
N_OBS = 4
N_LAT = 8


def draw_lat_width(key, part):
    first_key = jax.random.fold_in(key, 11)
    second_key = jax.random.fold_in(key, 23)
    widths = jax.random.randint(first_key, (NLAT,), 1, LAT_DEV + 1)
    chosen = jax.random.randint(second_key, (), 0, NLAT)
    widths = widths.at[chosen].set(LAT_DEV)
    return widths.astype(jnp.int32)


def with_ends(result, own_key, least, top_value):
    dims = result.shape
    spot = [jax.random.randint(jax.random.fold_in(own_key, axis), (), 0, dims[axis]) for axis in range(len(dims))]
    result = result.at[tuple(spot)].set(least)
    longest = dims.index(max(dims))
    spot[longest] = (spot[longest] + 1) % dims[longest]
    return result.at[tuple(spot)].set(top_value)


def block_levels(key, extent, pieces, low, high):
    loudness, own = 1.0, jax.random.fold_in(key, 6)
    for dim, shards_of in pieces:
        steps = jnp.exp(jax.random.uniform(jax.random.fold_in(own, dim), (shards_of,), jnp.float32, low / len(pieces), high / len(pieces)))
        loudness = loudness * jnp.repeat(steps, extent[dim] // shards_of).reshape([-1 if axis == dim else 1 for axis in range(len(extent))])
    return loudness


def gaussian(rng, extent, scale, limit, cuts=(), held_as=jnp.bfloat16):
    drawn = scale * jax.random.normal(rng, extent, jnp.float32)
    if cuts:
        drawn = drawn * block_levels(rng, extent, cuts, -0.22, 0.18)
    return jnp.clip(drawn, -limit, limit).astype(held_as)


def setup_inputs(seed: int = 0) -> dict:
    key_list = jax.random.split(jax.random.key(seed), 11)
    return {
        "footprints": gaussian(key_list[0], (N_OBS, N_LAT, NBLK, BLOCK, BLOCK), (BLOCK * NBLK * N_LAT // (2 * RB_DEV)) ** -0.5, 0.078125, ((0, 4), (1, 8))),
        "block_rows": with_ends(jax.random.randint(key_list[1], (N_OBS, N_LAT, NBLK), 0, RB_DEV), jax.random.fold_in(key_list[1], 1), 0, RB_DEV - 1).astype(jnp.int32),
        "block_cols": with_ends(jax.random.randint(key_list[2], (N_OBS, N_LAT, NBLK), 0, CB_DEV), jax.random.fold_in(key_list[2], 1), 0, CB_DEV - 1).astype(jnp.int32),
        "block_scale": with_ends(jax.random.randint(key_list[3], (N_OBS, N_LAT, NBLK), 0, 4), jax.random.fold_in(key_list[3], 1), 0, 3).astype(jnp.int32),
        "lat_width": draw_lat_width(jax.random.fold_in(key_list[10], 71), 0),
        "lon_width": with_ends(jax.random.randint(key_list[5], (NLAT,), 1, NLON // 8 + 1), jax.random.fold_in(key_list[5], 1), 1, (NLON // 8 + 1) - 1).astype(jnp.int32),
        "obs_weight": jnp.clip(jnp.exp(math.log(3.0) - 2.3025851 * jax.random.uniform(key_list[6], (SOUNDINGS,), jnp.float32) ** block_levels(key_list[6], (SOUNDINGS,), ((0, 4),), -0.2, 0.2)), 0.3, 3.0),
        "solution": gaussian(key_list[7], (K, WEEKS, NLAT, NLON), 1.0, 6.0, ((2, 8),), jnp.float32),
        "residual": gaussian(key_list[8], (K, WEEKS, NLAT, NLON), 1.0, 6.0, ((2, 8),), jnp.float32),
        "direction": gaussian(key_list[9], (K, WEEKS, NLAT, NLON), 1.0, 6.0, ((2, 8),), jnp.float32),
    }


def lat_matrix(index_out, width_out, index_in, row_reach):
    decay_rows = row_reach / 2.0
    distance = jnp.abs(index_out[:, None] - index_in[None, :]).astype(jnp.float32)
    offsets = jnp.abs(jnp.arange(-row_reach, row_reach + 1)).astype(jnp.float32)
    limits = width_out.astype(jnp.float32)[:, None]
    weights = jnp.where(offsets[None, :] <= limits, jnp.exp(-2.0 * offsets / decay_rows)[None, :], 0.0)
    normal = jnp.sqrt(lax.optimization_barrier(jnp.sum(weights, axis=1)))
    return jnp.where(distance <= limits, jnp.exp(-distance / decay_rows), 0.0) / normal[:, None]

def lon_matrix(row_width, lon_points):
    lon_decay = lon_points / 32.0
    lon_reach = lon_points // 8
    lon_grid = jnp.arange(lon_points)
    apart_cells = jnp.abs(lon_grid[:, None] - lon_grid[None, :])
    apart_cells = jnp.minimum(apart_cells, lon_points - apart_cells).astype(jnp.float32)
    offsets = jnp.abs(jnp.arange(-lon_reach, lon_reach + 1)).astype(jnp.float32)
    limit_cells = row_width.astype(jnp.float32)
    normal = jnp.sqrt(jnp.sum(jnp.where(offsets <= limit_cells, jnp.exp(-2.0 * offsets / lon_decay), 0.0)))
    return jnp.where(apart_cells <= limit_cells, jnp.exp(-apart_cells / lon_decay), 0.0) / normal

def lon_apply(field_in, widths):
    lon_points = field_in.shape[3]

    def one_row(packed):
        slab_row, row_width = packed
        return jnp.einsum('kwa,ab->kwb', slab_row, lon_matrix(row_width, lon_points), precision=lax.Precision.HIGHEST)
    mixed_rows = lax.map(one_row, (jnp.moveaxis(field_in, 2, 0), widths))
    return jnp.moveaxis(mixed_rows, 0, 2)

def inner_gram(left_field, right_field):
    left_rows = left_field.reshape(left_field.shape[0], -1)
    right_rows = right_field.reshape(right_field.shape[0], -1)
    return jnp.einsum('kx,jx->kj', left_rows, right_rows, precision=lax.Precision.HIGHEST)

def combine_columns(coeffs, field_in):
    return jnp.einsum('ba,bwix->awix', coeffs, field_in, precision=lax.Precision.HIGHEST)

def reference(footprints, block_rows, block_cols, block_scale, lat_width, lon_width, obs_weight, solution, residual, direction):
    highest = lax.Precision.HIGHEST
    lat_index = jnp.arange(NLAT)
    lat_full = lat_matrix(lat_index, lat_width, lat_index, LAT_DEV)
    spread = jnp.einsum('ij,kwjl->kwil', lat_full, lon_apply(direction, lon_width), precision=highest)
    band_cells = spread.astype(jnp.bfloat16).reshape(K, WEEKS, N_LAT, LAT_DEV, NLON)
    band_cells = jnp.moveaxis(band_cells, 2, 0).reshape(N_LAT, K, CB_DEV, BLOCK)
    flat_blocks = footprints.reshape(N_OBS * N_LAT, NBLK, BLOCK, BLOCK)
    flat_rows = block_rows.reshape(N_OBS * N_LAT, NBLK)
    flat_cols = block_cols.reshape(N_OBS * N_LAT, NBLK)
    flat_scale = jnp.exp2(-block_scale.reshape(N_OBS * N_LAT, NBLK).astype(jnp.float32))
    row_slots = jnp.arange(RB_DEV)
    col_slots = jnp.arange(CB_DEV)

    def forward_one(device_slot):
        blocks = flat_blocks[device_slot].astype(jnp.float32)
        picked = jnp.take(band_cells[device_slot % N_LAT], flat_cols[device_slot], axis=1).astype(jnp.float32)
        partial_value = jnp.einsum('nrc,knc->knr', blocks, picked) * flat_scale[device_slot][None, :, None]
        row_hot = (flat_rows[device_slot][:, None] == row_slots[None, :]).astype(jnp.float32)
        return jnp.einsum('knr,nb->kbr', partial_value, row_hot, precision=highest).reshape(K, OBS_DEV)
    partials = lax.map(forward_one, jnp.arange(N_OBS * N_LAT))
    obs_sums = lax.optimization_barrier(jnp.sum(partials.reshape(N_OBS, N_LAT, K, OBS_DEV), axis=1))
    obs_values = (obs_sums * obs_weight.reshape(N_OBS, 1, OBS_DEV)).astype(jnp.bfloat16)

    def adjoint_one(device_slot):
        blocks = flat_blocks[device_slot].astype(jnp.float32)
        slab_values = obs_values[device_slot // N_LAT].reshape(K, RB_DEV, BLOCK)
        pulled = jnp.take(slab_values, flat_rows[device_slot], axis=1).astype(jnp.float32)
        adjoint_terms = jnp.einsum('nrc,knr->knc', blocks, pulled) * flat_scale[device_slot][None, :, None]
        col_hot = (flat_cols[device_slot][:, None] == col_slots[None, :]).astype(jnp.float32)
        return jnp.einsum('knc,nb->kbc', adjoint_terms, col_hot, precision=highest)
    adjoints = lax.map(adjoint_one, jnp.arange(N_OBS * N_LAT)).reshape(N_OBS, N_LAT, K, CB_DEV, BLOCK)
    adjoint = lax.optimization_barrier(jnp.sum(adjoints, axis=0)).reshape(N_LAT, K, WEEKS, LAT_DEV, NLON)
    adjoint = jnp.moveaxis(adjoint, 0, 2).reshape(K, WEEKS, NLAT, NLON)
    pulled_back = jnp.einsum('ji,kwjl->kwil', lat_full, adjoint, precision=highest)
    image = direction + lon_apply(pulled_back, lon_width)
    gram_old = inner_gram(residual, residual)
    curvature = inner_gram(direction, image)
    step_coef = jax.scipy.linalg.cho_solve((jnp.linalg.cholesky(curvature), True), gram_old)
    next_solution = solution + combine_columns(step_coef, direction)
    next_residual = residual - combine_columns(step_coef, image)
    gram_new = inner_gram(next_residual, next_residual)
    turn_coef = jax.scipy.linalg.cho_solve((jnp.linalg.cholesky(gram_old), True), gram_new)
    next_direction = next_residual + combine_columns(turn_coef, direction)
    return (next_solution, next_residual, next_direction)
```

```python
import functools
import math

import jax
import jax.numpy as jnp
from jax import lax
from jax.experimental import pallas as pl
from jax.experimental.pallas import tpu as pltpu
from jax.sharding import PartitionSpec as P

LANES = 128
SUBLANES = 8
VMEM_BYTES = 40 * 1024 * 1024
HIGHEST = lax.Precision.HIGHEST


def params():
    return pltpu.CompilerParams(vmem_limit_bytes=VMEM_BYTES)


def cost(flops, nbytes):
    return pl.CostEstimate(flops=int(flops), bytes_accessed=int(nbytes), transcendentals=0)


def whole(shape):
    return pl.BlockSpec(shape, lambda *_: (0,) * len(shape))


def pow2(exponent):
    size = jnp.abs(exponent)
    up = jnp.ones(exponent.shape, jnp.float32)
    down = up
    for bit in range(7):
        on = ((size >> bit) & 1) == 1
        up = up * jnp.where(on, 2.0 ** (2**bit), 1.0)
        down = down * jnp.where(on, 2.0 ** -(2**bit), 1.0)
    return jnp.where(exponent < 0, down, up)


def exponent_of(peak):
    logs = jnp.log(jnp.maximum(peak, 1e-28)) * (1.0 / math.log(2.0))
    return jnp.ceil(logs + 1e-3).astype(jnp.int32)


def to_int(values, factor):
    return jnp.clip(jnp.round(values * factor), -32767.0, 32767.0).astype(jnp.int32)


def pack(high, low):
    return (high << 16) | (low & 0xFFFF)


def high_of(word):
    return word >> 16


def low_of(word):
    return (word << 16) >> 16


def pack_field(field_ref, word_ref, peak):
    weeks, rows, lon = field_ref.shape
    half = rows // 2
    exponent = exponent_of(jnp.max(peak, axis=0, keepdims=True))
    exponent = jnp.broadcast_to(exponent, (SUBLANES, lon))
    factor = pow2(15 - exponent)
    word_ref[weeks * half :, :] = exponent

    def one_week(week, carry):
        for start in range(0, half, SUBLANES):
            high = to_int(field_ref[week, start : start + SUBLANES, :], factor)
            low = to_int(field_ref[week, half + start : half + start + SUBLANES, :], factor)
            at = pl.multiple_of(week * half + start, SUBLANES)
            word_ref[pl.ds(at, SUBLANES), :] = pack(high, low)
        return carry

    lax.fori_loop(0, weeks, one_week, 0)


def word_scale(word_ref, half_rows):
    return pow2(word_ref[half_rows : half_rows + SUBLANES, :] - 15)


def lon_setup(lon):
    return lon / 32.0, (lon // 8 + 1).bit_length()


def lon_rows(rows, count, norm, lon):
    decay, bits = lon_setup(lon)
    total = -rows
    for side in (1, -1):
        window = rows
        taken = jnp.zeros_like(rows)
        for bit in range(bits):
            reach = 2**bit
            fade = math.exp(-reach / decay)
            shift = reach if side == 1 else lon - reach
            moved = window if bit == 0 else window + fade * pltpu.roll(taken, shift, 1)
            taken = jnp.where(((count >> bit) & 1) == 1, moved, taken)
            if bit + 1 < bits:
                window = window + fade * pltpu.roll(window, shift, 1)
        total = total + taken
    return total * norm


def lon_norm(count, lon):
    decay, _ = lon_setup(lon)
    ratio = math.exp(-2.0 / decay)
    ends = jnp.exp(count.astype(jnp.float32) * (-2.0 / decay))
    return 1.0 / jnp.sqrt(1.0 + (2.0 / (1.0 - ratio)) * (ratio - ends))


def lon_field(source_ref, count_ref, norm_ref, out_ref):
    weeks, rows, lon = source_ref.shape

    def one_group(group, peak):
        at = pl.multiple_of(group * SUBLANES, SUBLANES)
        count = count_ref[pl.ds(at, SUBLANES), :]
        norm = norm_ref[pl.ds(at, SUBLANES), :]

        def one_week(week, peak):
            rows_in = source_ref[week, pl.ds(at, SUBLANES), :]
            result = lon_rows(rows_in, count, norm, lon)
            out_ref[week, pl.ds(at, SUBLANES), :] = result
            return jnp.maximum(peak, jnp.abs(result))

        return lax.fori_loop(0, weeks, one_week, peak)

    return lax.fori_loop(0, rows // SUBLANES, one_group, jnp.zeros((SUBLANES, lon), jnp.float32))


def spread_lon_kernel(_, field_ref, count_ref, out_ref, word_ref, norm_ref):
    norm_ref[...] = lon_norm(count_ref[...], count_ref.shape[1])
    peak = lon_field(field_ref.at[0], count_ref, norm_ref, out_ref.at[0])
    pack_field(out_ref.at[0], word_ref.at[0], peak)


def spread_lon(direction, first, rhs, counts):
    _, weeks, rows, lon = direction.shape
    words = weeks * rows // 2 + SUBLANES
    return pl.pallas_call(
        spread_lon_kernel,
        grid_spec=pltpu.PrefetchScalarGridSpec(
            num_scalar_prefetch=1,
            grid=(rhs,),
            in_specs=[
                pl.BlockSpec((1, weeks, rows, lon), lambda k, first: (first[0] + k, 0, 0, 0)),
                whole((rows, lon)),
            ],
            out_specs=[
                pl.BlockSpec((1, weeks, rows, lon), lambda k, first: (k, 0, 0, 0)),
                pl.BlockSpec((1, words, lon), lambda k, first: (k, 0, 0)),
            ],
            scratch_shapes=[pltpu.VMEM((rows, lon), jnp.float32)],
        ),
        out_shape=[
            jax.ShapeDtypeStruct((rhs, weeks, rows, lon), jnp.float32),
            jax.ShapeDtypeStruct((rhs, words, lon), jnp.int32),
        ],
        compiler_params=params(),
        cost_estimate=cost(rhs * weeks * rows * lon * 100, rhs * weeks * rows * lon * 10),
        name="spread_lon",
    )(first, direction, counts)


def fill_window(window_ref, week, before_ref, own_ref, after_ref, scale_before, scale_after):
    _, rows, lon = own_ref.shape
    half = rows // 2
    for base, ref, scale in ((0, before_ref, scale_before), (2 * rows, after_ref, scale_after)):
        for start in range(0, half, SUBLANES):
            at = pl.multiple_of(week * half + start, SUBLANES)
            word = ref[pl.ds(at, SUBLANES), :]
            window_ref[base + start : base + start + SUBLANES, :] = (
                high_of(word).astype(jnp.float32) * scale
            )
            window_ref[base + half + start : base + half + start + SUBLANES, :] = (
                low_of(word).astype(jnp.float32) * scale
            )
    window_ref[rows : 2 * rows, :] = own_ref[week]


def spread_lat_kernel(slots, own_ref, before_ref, after_ref, weights_ref, hot_ref, *rest):
    picks, (window_ref, cells_ref) = rest[:slots], rest[slots:]
    _, weeks, rows, lon = own_ref.shape
    half_rows = weeks * rows // 2
    scale_before = word_scale(before_ref.at[0], half_rows)
    scale_after = word_scale(after_ref.at[0], half_rows)
    for week in range(weeks):
        fill_window(
            window_ref,
            week,
            before_ref.at[0],
            own_ref.at[0],
            after_ref.at[0],
            scale_before,
            scale_after,
        )
        mixed = jnp.dot(
            weights_ref[...],
            window_ref[...],
            precision=HIGHEST,
            preferred_element_type=jnp.float32,
        )
        for part in range(lon // LANES):
            at = (week * (lon // LANES) + part) * rows
            cells_ref[at : at + rows, :] = mixed[:, part * LANES : (part + 1) * LANES].astype(
                jnp.bfloat16
            )
    for slot in range(slots):
        picks[slot][0] = jnp.dot(
            hot_ref[slot], cells_ref[...], preferred_element_type=jnp.float32
        ).astype(jnp.bfloat16)


def spread_lat(own, before, after, weights, hot):
    rhs, weeks, rows, lon = own.shape
    slots, blocks, cols = hot.shape
    words = before.shape[1]
    word_spec = pl.BlockSpec((1, words, lon), lambda k: (k, 0, 0))
    return pl.pallas_call(
        functools.partial(spread_lat_kernel, slots),
        grid=(rhs,),
        in_specs=[
            pl.BlockSpec((1, weeks, rows, lon), lambda k: (k, 0, 0, 0)),
            word_spec,
            word_spec,
            whole(weights.shape),
            whole(hot.shape),
        ],
        out_specs=[pl.BlockSpec((1, blocks, LANES), lambda k: (k, 0, 0))] * slots,
        out_shape=[jax.ShapeDtypeStruct((rhs, blocks, LANES), jnp.bfloat16)] * slots,
        scratch_shapes=[
            pltpu.VMEM((3 * rows, lon), jnp.float32),
            pltpu.VMEM((cols, LANES), jnp.bfloat16),
        ],
        compiler_params=params(),
        cost_estimate=cost(rhs * slots * blocks * cols * LANES * 2, rhs * weeks * rows * lon * 10),
        name="spread_lat",
    )(own, before, after, weights, hot)


CHUNK = 32


def forward_kernel(slots, row_ref, scale_ref, blocks_ref, *rest):
    picks, (out_ref, cells_ref) = rest[:slots], rest[slots:]
    step = pl.program_id(0)
    chunk = blocks_ref.shape[0]
    rhs, count, _ = picks[0].shape
    lines = slots * rhs

    @pl.when(step == 0)
    def _():
        out_ref[...] = jnp.zeros_like(out_ref)
        for slot in range(slots):
            for k in range(rhs):
                cells_ref[pl.ds(slot * rhs + k, count, stride=lines), :] = picks[slot][k].astype(
                    jnp.float32
                )

    values = []
    for n in range(chunk):
        at = pl.multiple_of((step * chunk + n) * lines, lines)
        cells = cells_ref[pl.ds(at, lines), :].astype(jnp.bfloat16)
        values.append(
            lax.dot_general(
                cells,
                blocks_ref[n],
                (((1,), (1,)), ((), ())),
                preferred_element_type=jnp.float32,
            )
        )
    for n in range(chunk):
        index = step * chunk + n
        at = pl.multiple_of(row_ref[index] * lines, lines)
        out_ref[pl.ds(at, lines), :] += values[n] * scale_ref[index]


def forward(row_list, scales, blocks, picks, row_blocks):
    slots = len(picks)
    rhs, count, _ = picks[0].shape
    lines = slots * rhs
    edge = blocks.shape[1]
    return pl.pallas_call(
        functools.partial(forward_kernel, slots),
        grid_spec=pltpu.PrefetchScalarGridSpec(
            num_scalar_prefetch=2,
            grid=(count // CHUNK,),
            in_specs=[pl.BlockSpec((CHUNK, edge, edge), lambda n, *_: (n, 0, 0))]
            + [whole((rhs, count, edge))] * slots,
            out_specs=whole((row_blocks * lines, edge)),
            scratch_shapes=[pltpu.VMEM((count * lines, edge), jnp.float32)],
        ),
        out_shape=jax.ShapeDtypeStruct((row_blocks * lines, edge), jnp.float32),
        compiler_params=params(),
        cost_estimate=cost(blocks.size * 2 * lines, blocks.size * 2),
        name="forward",
    )(row_list, scales, blocks, *picks)


def adjoint_kernel(slots, rhs, row_ref, scale_ref, blocks_ref, values_ref, *rest):
    outs, (terms_ref,) = rest[:slots], rest[slots:]
    step = pl.program_id(0)
    chunk = blocks_ref.shape[0]
    lines = slots * rhs
    for n in range(chunk):
        index = step * chunk + n
        at = pl.multiple_of(row_ref[index] * lines, lines)
        pulled = values_ref[pl.ds(at, lines), :].astype(jnp.bfloat16)
        term = jnp.dot(pulled, blocks_ref[n], preferred_element_type=jnp.float32)
        to = pl.multiple_of(index * lines, lines)
        terms_ref[pl.ds(to, lines), :] = term * scale_ref[index]

    @pl.when(step == pl.num_programs(0) - 1)
    def _():
        count = terms_ref.shape[0] // lines
        half = count // 2
        for slot in range(slots):
            for k in range(rhs):
                terms = terms_ref[pl.ds(slot * rhs + k, count, stride=lines), :]
                peak = jnp.max(jnp.abs(terms), axis=0, keepdims=True)
                exponent = jnp.broadcast_to(exponent_of(peak), (SUBLANES, LANES))
                number = to_int(terms, pow2(15 - exponent)[:1])
                outs[slot][k, :half, :] = pack(number[:half], number[half:])
                outs[slot][k, half:, :] = exponent


def adjoint_terms(row_list, scales, blocks, values, slots, rhs):
    count, edge, _ = blocks.shape
    lines = slots * rhs
    words = count // 2 + SUBLANES
    return pl.pallas_call(
        functools.partial(adjoint_kernel, slots, rhs),
        grid_spec=pltpu.PrefetchScalarGridSpec(
            num_scalar_prefetch=2,
            grid=(count // CHUNK,),
            in_specs=[
                pl.BlockSpec((CHUNK, edge, edge), lambda n, *_: (n, 0, 0)),
                whole(values.shape),
            ],
            out_specs=[whole((rhs, words, edge))] * slots,
            scratch_shapes=[pltpu.VMEM((count * lines, edge), jnp.float32)],
        ),
        out_shape=[jax.ShapeDtypeStruct((rhs, words, edge), jnp.int32)] * slots,
        compiler_params=params(),
        cost_estimate=cost(blocks.size * 2 * lines, blocks.size * 2),
        name="adjoint",
    )(row_list, scales, blocks, values)


def gather_cells_kernel(slots, hot_ref, *rest):
    terms, (field_ref, word_ref, split_ref) = rest[:slots], rest[slots:]
    _, weeks, rows, lon = field_ref.shape
    count = hot_ref.shape[1] // slots
    half = count // 2
    for slot in range(slots):
        scale = word_scale(terms[slot].at[0], half)[:1]
        word = terms[slot][0, :half, :]
        for base, number in ((0, high_of(word)), (half, low_of(word))):
            coarse = (number + 128) >> 8
            fine = number - (coarse << 8)
            at = slot * count + base
            split_ref[at : at + half, :LANES] = (
                (coarse << 8).astype(jnp.float32) * scale
            ).astype(jnp.bfloat16)
            split_ref[at : at + half, LANES:] = (fine.astype(jnp.float32) * scale).astype(
                jnp.bfloat16
            )
    peak = jnp.zeros((SUBLANES, lon), jnp.float32)
    parts = lon // LANES
    for week in range(weeks):
        at = week * parts * rows
        both = jnp.dot(
            hot_ref[at : at + parts * rows, :],
            split_ref[...],
            preferred_element_type=jnp.float32,
        )
        cells = both[:, :LANES] + both[:, LANES:]
        for part in range(parts):
            field_ref[0, week, :, part * LANES : (part + 1) * LANES] = cells[
                part * rows : (part + 1) * rows
            ]
        for start in range(0, rows, SUBLANES):
            peak = jnp.maximum(peak, jnp.abs(field_ref[0, week, start : start + SUBLANES, :]))
    pack_field(field_ref.at[0], word_ref.at[0], peak)


def gather_cells(hot_turned, terms, weeks, rows, lon):
    slots = len(terms)
    rhs, words_in, edge = terms[0].shape
    words = weeks * rows // 2 + SUBLANES
    return pl.pallas_call(
        functools.partial(gather_cells_kernel, slots),
        grid=(rhs,),
        in_specs=[whole(hot_turned.shape)]
        + [pl.BlockSpec((1, words_in, edge), lambda k: (k, 0, 0))] * slots,
        out_specs=[
            pl.BlockSpec((1, weeks, rows, lon), lambda k: (k, 0, 0, 0)),
            pl.BlockSpec((1, words, lon), lambda k: (k, 0, 0)),
        ],
        out_shape=[
            jax.ShapeDtypeStruct((rhs, weeks, rows, lon), jnp.float32),
            jax.ShapeDtypeStruct((rhs, words, lon), jnp.int32),
        ],
        scratch_shapes=[pltpu.VMEM((hot_turned.shape[1], 2 * LANES), jnp.bfloat16)],
        compiler_params=params(),
        cost_estimate=cost(rhs * hot_turned.size * 4 * LANES, rhs * weeks * rows * lon * 10),
        name="gather_cells",
    )(hot_turned, *terms)


def pull_back_kernel(
    own_ref, before_ref, after_ref, weights_ref, count_ref, word_ref, window_ref, norm_ref, field_ref
):
    _, weeks, rows, lon = own_ref.shape
    half_rows = weeks * rows // 2
    norm_ref[...] = lon_norm(count_ref[...], lon)
    scale_before = word_scale(before_ref.at[0], half_rows)
    scale_after = word_scale(after_ref.at[0], half_rows)
    for week in range(weeks):
        fill_window(
            window_ref,
            week,
            before_ref.at[0],
            own_ref.at[0],
            after_ref.at[0],
            scale_before,
            scale_after,
        )
        field_ref[week] = jnp.dot(
            weights_ref[...],
            window_ref[...],
            precision=HIGHEST,
            preferred_element_type=jnp.float32,
        )
    peak = lon_field(field_ref, count_ref, norm_ref, field_ref)
    pack_field(field_ref, word_ref.at[0], peak)


def pull_back(own, before, after, weights, counts):
    rhs, weeks, rows, lon = own.shape
    words = before.shape[1]
    word_spec = pl.BlockSpec((1, words, lon), lambda k: (k, 0, 0))
    return pl.pallas_call(
        pull_back_kernel,
        grid=(rhs,),
        in_specs=[
            pl.BlockSpec((1, weeks, rows, lon), lambda k: (k, 0, 0, 0)),
            word_spec,
            word_spec,
            whole(weights.shape),
            whole(counts.shape),
        ],
        out_specs=word_spec,
        out_shape=jax.ShapeDtypeStruct((rhs, words, lon), jnp.int32),
        scratch_shapes=[
            pltpu.VMEM((3 * rows, lon), jnp.float32),
            pltpu.VMEM((rows, lon), jnp.float32),
            pltpu.VMEM((weeks, rows, lon), jnp.float32),
        ],
        compiler_params=params(),
        cost_estimate=cost(rhs * weeks * rows * lon * 300, rhs * weeks * rows * lon * 10),
        name="pull_back",
    )(own, before, after, weights, counts)


TILE = 4


def gram_kernel(slots, order_ref, residual_ref, direction_ref, *rest):
    words, (image_ref, gram_ref) = rest[:slots], rest[slots:]
    week = pl.program_id(0)
    rhs_count, _, rows, lon = direction_ref.shape
    rhs = words[0].shape[0]
    half = rows // 2
    half_rows = words[0].shape[1] - SUBLANES

    @pl.when(week == 0)
    def _():
        gram_ref[...] = jnp.zeros_like(gram_ref)

    for slot in range(slots):
        for k in range(rhs):
            index = order_ref[slot] + k
            scale = word_scale(words[slot].at[k], half_rows)
            for start in range(0, half, SUBLANES):
                at = pl.multiple_of(week * half + start, SUBLANES)
                word = words[slot][k, pl.ds(at, SUBLANES), :]
                for base, number in ((start, high_of(word)), (half + start, low_of(word))):
                    image_ref[index, 0, base : base + SUBLANES, :] = (
                        direction_ref[index, 0, base : base + SUBLANES, :]
                        + number.astype(jnp.float32) * scale
                    )

    pairs = (
        (residual_ref, residual_ref),
        (direction_ref, image_ref),
        (residual_ref, image_ref),
        (image_ref, image_ref),
    )
    for place, (left_ref, right_ref) in enumerate(pairs):
        for a0 in range(0, rhs_count, TILE):
            for b0 in range(0, rhs_count, TILE):
                if left_ref is right_ref and b0 < a0:
                    continue

                def one_group(group, sums):
                    at = pl.multiple_of(group * SUBLANES, SUBLANES)
                    sums = list(sums)
                    for lane in range(0, lon, LANES):
                        left = [
                            left_ref[a0 + a, 0, pl.ds(at, SUBLANES), lane : lane + LANES]
                            for a in range(TILE)
                        ]
                        right = [
                            right_ref[b0 + b, 0, pl.ds(at, SUBLANES), lane : lane + LANES]
                            for b in range(TILE)
                        ]
                        for a in range(TILE):
                            for b in range(TILE):
                                sums[a * TILE + b] = sums[a * TILE + b] + left[a] * right[b]
                    return tuple(sums)

                zero = jnp.zeros((SUBLANES, LANES), jnp.float32)
                sums = lax.fori_loop(0, rows // SUBLANES, one_group, (zero,) * TILE**2)
                for a in range(TILE):
                    for b in range(TILE):
                        at = (place * rhs_count + a0 + a) * rhs_count + b0 + b
                        gram_ref[at] += sums[a * TILE + b]


def grams(order, residual, direction, words):
    slots = len(words)
    rhs_count, weeks, rows, lon = direction.shape
    field = pl.BlockSpec((rhs_count, 1, rows, lon), lambda w, *_: (0, w, 0, 0))
    return pl.pallas_call(
        functools.partial(gram_kernel, slots),
        grid_spec=pltpu.PrefetchScalarGridSpec(
            num_scalar_prefetch=1,
            grid=(weeks,),
            in_specs=[field, field] + [whole(words[0].shape)] * slots,
            out_specs=[field, whole((4 * rhs_count**2, SUBLANES, LANES))],
        ),
        out_shape=[
            jax.ShapeDtypeStruct(direction.shape, jnp.float32),
            jax.ShapeDtypeStruct((4 * rhs_count**2, SUBLANES, LANES), jnp.float32),
        ],
        compiler_params=params(),
        cost_estimate=cost(8 * rhs_count * direction.size, 16 * direction.size),
        name="grams",
    )(order, residual, direction, *words)


def update_kernel(
    step_ref, turn_ref, solution_ref, residual_ref, direction_ref, image_ref, sol_out, res_out, dir_out
):
    rhs_count, _, rows, lon = direction_ref.shape

    def one_group(group, carry):
        at = pl.multiple_of(group * SUBLANES, SUBLANES)
        spot = pl.ds(at, SUBLANES)
        for a in range(rhs_count):
            moved = solution_ref[a, 0, spot, :]
            left = residual_ref[a, 0, spot, :]
            for b in range(rhs_count):
                coef = step_ref[b, a]
                moved = moved + coef * direction_ref[b, 0, spot, :]
                left = left - coef * image_ref[b, 0, spot, :]
            sol_out[a, 0, spot, :] = moved
            res_out[a, 0, spot, :] = left
            turned = left
            for b in range(rhs_count):
                turned = turned + turn_ref[b, a] * direction_ref[b, 0, spot, :]
            dir_out[a, 0, spot, :] = turned
        return carry

    lax.fori_loop(0, rows // SUBLANES, one_group, 0)


def update(step_coef, turn_coef, solution, residual, direction, image):
    rhs_count, weeks, rows, lon = direction.shape
    field = pl.BlockSpec((rhs_count, 1, rows, lon), lambda w, *_: (0, w, 0, 0))
    shape = jax.ShapeDtypeStruct(direction.shape, jnp.float32)
    return pl.pallas_call(
        update_kernel,
        grid_spec=pltpu.PrefetchScalarGridSpec(
            num_scalar_prefetch=2,
            grid=(weeks,),
            in_specs=[field] * 4,
            out_specs=[field] * 3,
        ),
        out_shape=[shape] * 3,
        compiler_params=params(),
        cost_estimate=cost(6 * rhs_count * direction.size, 28 * direction.size),
        name="update",
    )(step_coef, turn_coef, solution, residual, direction, image)


def shifted(value, axis, by):
    size = lax.axis_size(axis)
    return lax.ppermute(value, axis, [(i, (i + by) % size) for i in range(size)])


def neighbours(value, axis):
    size = lax.axis_size(axis)
    before = lax.ppermute(value, axis, [(i, i + 1) for i in range(size - 1)])
    after = lax.ppermute(value, axis, [(i + 1, i) for i in range(size - 1)])
    return before, after


def summed_over(value, axis):
    size = lax.axis_size(axis)
    if size & (size - 1):
        return lax.psum(value, axis)
    reach = 1
    while reach < size:
        value = value + lax.ppermute(value, axis, [(i, i ^ reach) for i in range(size)])
        reach *= 2
    return value


def lat_windows(lat_width, band, rows):
    decay = rows / 2.0
    total = lat_width.shape[0]
    offsets = jnp.abs(jnp.arange(-rows, rows + 1)).astype(jnp.float32)
    limits = lat_width.astype(jnp.float32)
    normal = jnp.sqrt(
        jnp.sum(
            jnp.where(
                offsets[None, :] <= limits[:, None], jnp.exp(-2.0 * offsets / decay)[None, :], 0.0
            ),
            axis=1,
        )
    )
    padded_limits = jnp.pad(limits, (rows, rows), constant_values=-1.0)
    padded_normal = jnp.pad(normal, (rows, rows), constant_values=1.0)
    near_limits = lax.dynamic_slice_in_dim(padded_limits, band * rows, 3 * rows)
    near_normal = lax.dynamic_slice_in_dim(padded_normal, band * rows, 3 * rows)
    distance = jnp.abs(
        jnp.arange(rows)[:, None] + rows - jnp.arange(3 * rows)[None, :]
    ).astype(jnp.float32)
    fade = jnp.exp(-distance / decay)
    own_limits, own_normal = near_limits[rows : 2 * rows, None], near_normal[rows : 2 * rows, None]
    spread = jnp.where(distance <= own_limits, fade, 0.0) / own_normal
    pulled = jnp.where(distance <= near_limits[None, :], fade, 0.0) / near_normal[None, :]
    return spread, pulled


def product(left, right):
    return jnp.dot(left, right, precision=HIGHEST)


def shards(
    footprints,
    block_rows,
    block_cols,
    block_scale,
    lat_width,
    lon_width,
    obs_weight,
    solution,
    residual,
    direction,
):
    rhs_count, weeks, rows, lon = direction.shape
    blocks = footprints[0, 0]
    count, edge, _ = blocks.shape
    row_list, col_list = block_rows[0, 0], block_cols[0, 0]
    scales = jnp.exp2(-block_scale[0, 0].astype(jnp.float32))
    row_blocks = obs_weight.shape[0] // edge
    slots = lax.axis_size("obs")
    rhs = rhs_count // slots
    slab, band = lax.axis_index("obs"), lax.axis_index("lat")
    parts = lon // edge
    cols = weeks * rows * parts

    own_width = lax.dynamic_slice_in_dim(lon_width, band * rows, rows)
    counts = jnp.broadcast_to(own_width[:, None] + 1, (rows, lon))
    lat_spread, lat_pulled = lat_windows(lat_width, band, rows)

    line, part = col_list // parts, col_list % parts
    place = ((line // rows) * parts + part) * rows + line % rows
    places = [place] + [shifted(place, "obs", -d) for d in range(1, slots)]
    places = jnp.stack(places)
    hot = (places[:, :, None] == jnp.arange(cols)[None, None, :]).astype(jnp.bfloat16)
    hot_turned = (jnp.arange(cols)[:, None] == places.reshape(1, -1)).astype(jnp.bfloat16)

    first = (slab * rhs).astype(jnp.int32).reshape(1)
    lon_own, lon_words = spread_lon(direction, first, rhs, counts)
    before, after = neighbours(lon_words, "lat")
    picks = spread_lat(lon_own, before, after, lat_spread, hot)
    cells = [picks[0]] + [shifted(picks[d], "obs", d) for d in range(1, slots)]
    sums = summed_over(forward(row_list, scales, blocks, cells, row_blocks), "lat")
    weighted = sums.reshape(row_blocks, slots * rhs, edge) * obs_weight.reshape(row_blocks, 1, edge)
    terms = adjoint_terms(
        row_list, scales, blocks, weighted.reshape(-1, edge), slots, rhs
    )
    terms = [terms[0]] + [shifted(terms[d], "obs", -d) for d in range(1, slots)]
    field, field_words = gather_cells(hot_turned, terms, weeks, rows, lon)
    before, after = neighbours(field_words, "lat")
    image_words = pull_back(field, before, after, lat_pulled, counts)
    image_words = [image_words] + [shifted(image_words, "obs", d) for d in range(1, slots)]
    order = (((slab - jnp.arange(slots)) % slots) * rhs).astype(jnp.int32)
    image, products = grams(order, residual, direction, image_words)

    sums = summed_over(jnp.sum(products, axis=(1, 2)), "lat")
    gram_old, curvature, mixed, gram_image = sums.reshape(4, rhs_count, rhs_count)
    upper = jnp.arange(rhs_count)[:, None] <= jnp.arange(rhs_count)[None, :]
    gram_old = jnp.where(upper, gram_old, gram_old.T)
    gram_image = jnp.where(upper, gram_image, gram_image.T)
    step_coef = jax.scipy.linalg.cho_solve((jnp.linalg.cholesky(curvature), True), gram_old)
    cross = product(mixed, step_coef)
    gram_new = gram_old - cross - cross.T + product(step_coef.T, product(gram_image, step_coef))
    turn_coef = jax.scipy.linalg.cho_solve((jnp.linalg.cholesky(gram_old), True), gram_new)
    return tuple(update(step_coef, turn_coef, solution, residual, direction, image))


def solution(mesh):
    return jax.shard_map(
        shards,
        mesh=mesh,
        in_specs=(
            P("obs", "lat", None, None, None),
            P("obs", "lat", None),
            P("obs", "lat", None),
            P("obs", "lat", None),
            P(),
            P(),
            P("obs"),
            P(None, None, "lat", None),
            P(None, None, "lat", None),
            P(None, None, "lat", None),
        ),
        out_specs=(
            P(None, None, "lat", None),
            P(None, None, "lat", None),
            P(None, None, "lat", None),
        ),
        check_vma=False,
    )
```

```python
import functools
import math

import jax
import jax.numpy as jnp
from jax import lax
from jax.experimental import pallas as pl
from jax.experimental.pallas import tpu as pltpu
from jax.sharding import PartitionSpec as P

LANES = 128
CHUNK = 96
COPIES = 12
GROUP_RHS = 2
SUBLANES = 8
MIB = 1024 * 1024
HIGHEST = lax.Precision.HIGHEST


def params(mib):
    return pltpu.CompilerParams(vmem_limit_bytes=mib * MIB)


def cost(flops, nbytes):
    return pl.CostEstimate(flops=int(flops), bytes_accessed=int(nbytes), transcendentals=0)


def whole(shape):
    return pl.BlockSpec(shape, lambda *_: (0,) * len(shape), pipeline_mode=pl.Buffered(1))


def in_vmem(count):
    return [pl.BlockSpec(memory_space=pltpu.VMEM)] * count


def pow2(exponent):
    size = jnp.abs(exponent)
    up = jnp.ones(exponent.shape, jnp.float32)
    down = up
    for bit in range(7):
        on = ((size >> bit) & 1) == 1
        up = up * jnp.where(on, 2.0 ** (2**bit), 1.0)
        down = down * jnp.where(on, 2.0 ** -(2**bit), 1.0)
    return jnp.where(exponent < 0, down, up)


def exponent_of(peak):
    logs = jnp.log(jnp.maximum(peak, 1e-28)) * (1.0 / math.log(2.0))
    return jnp.ceil(logs + 1e-3).astype(jnp.int32)


def to_int(values, factor):
    return jnp.clip(jnp.round(values * factor), -32767.0, 32767.0).astype(jnp.int32)


def pack(high, low):
    return (high << 16) | (low & 0xFFFF)


def high_of(word):
    return word >> 16


def low_of(word):
    return (word << 16) >> 16


def words_of(rhs, weeks, rows):
    return rhs * weeks * rows // 2 + SUBLANES


def exponent_rows(peaks):
    line = lax.broadcasted_iota(jnp.int32, (SUBLANES, peaks[0].shape[1]), 0)
    found = jnp.zeros(line.shape, jnp.int32)
    for k, peak in enumerate(peaks):
        found = jnp.where(line == k, exponent_of(jnp.max(peak, axis=0, keepdims=True)), found)
    return found


def pack_field(field_ref, word_ref, peaks):
    rhs, weeks, rows, lon = field_ref.shape
    half = rows // 2
    exponents = exponent_rows(peaks)
    word_ref[rhs * weeks * half :, :] = exponents
    for k in range(rhs):
        factor = pow2(15 - jnp.broadcast_to(exponents[k : k + 1], (SUBLANES, lon)))

        def one_week(week, carry):
            for start in range(0, half, SUBLANES):
                high = to_int(field_ref[k, week, start : start + SUBLANES, :], factor)
                low = to_int(field_ref[k, week, half + start : half + start + SUBLANES, :], factor)
                at = pl.multiple_of((k * weeks + week) * half + start, SUBLANES)
                word_ref[pl.ds(at, SUBLANES), :] = pack(high, low)
            return carry

        lax.fori_loop(0, weeks, one_week, 0)


def word_scale(word_ref, body, k):
    row = word_ref[body + k : body + k + 1, :] - 15
    return pow2(jnp.broadcast_to(row, (SUBLANES, row.shape[1])))


def lon_setup(lon):
    return lon / 32.0, (lon // 8 + 1).bit_length()


def lon_rows(rows, count, norm, lon):
    decay, bits = lon_setup(lon)
    fields = rows.shape[0] // SUBLANES
    count = jnp.concatenate([count] * fields, axis=0)
    windows = [rows, rows]
    taken = [jnp.zeros_like(rows)] * 2
    for bit in range(bits):
        reach = 2**bit
        fade = math.exp(-reach / decay)
        chosen = ((count >> bit) & 1) == 1
        for side in range(2):
            shift = reach if side == 0 else lon - reach
            moved = windows[side]
            if bit:
                moved = moved + fade * pltpu.roll(taken[side], shift, 1)
            taken[side] = jnp.where(chosen, moved, taken[side])
            if bit + 1 < bits:
                windows[side] = windows[side] + fade * pltpu.roll(windows[side], shift, 1)
    return (taken[0] + taken[1] - rows) * jnp.concatenate([norm] * fields, axis=0)


def lon_norm(count, lon):
    decay, _ = lon_setup(lon)
    ratio = math.exp(-2.0 / decay)
    ends = jnp.exp(count.astype(jnp.float32) * (-2.0 / decay))
    return 1.0 / jnp.sqrt(1.0 + (2.0 / (1.0 - ratio)) * (ratio - ends))


def lon_field(source_ref, count_ref, out_ref):
    rhs, weeks, rows, lon = out_ref.shape

    def one_group(group, peaks):
        at = pl.multiple_of(group * SUBLANES, SUBLANES)
        count = count_ref[pl.ds(at, SUBLANES), :]
        norm = lon_norm(count, lon)
        fields = [source_ref[k, w, pl.ds(at, SUBLANES), :] for k in range(rhs) for w in range(weeks)]
        result = lon_rows(jnp.concatenate(fields, axis=0), count, norm, lon)
        peaks = list(peaks)
        for k in range(rhs):
            for w in range(weeks):
                start = (k * weeks + w) * SUBLANES
                part = result[start : start + SUBLANES]
                out_ref[k, w, pl.ds(at, SUBLANES), :] = part
                peaks[k] = jnp.maximum(peaks[k], jnp.abs(part))
        return tuple(peaks)

    zero = jnp.zeros((SUBLANES, lon), jnp.float32)
    return lax.fori_loop(0, rows // SUBLANES, one_group, (zero,) * rhs)


def spread_lon_kernel(_, field_ref, count_ref, out_ref, word_ref):
    pack_field(out_ref, word_ref, lon_field(field_ref, count_ref, out_ref))


def spread_lon(direction, first, rhs, counts):
    _, weeks, rows, lon = direction.shape
    words = words_of(rhs, weeks, rows)
    return pl.pallas_call(
        spread_lon_kernel,
        grid_spec=pltpu.PrefetchScalarGridSpec(
            num_scalar_prefetch=1,
            grid=(1,),
            in_specs=[
                pl.BlockSpec(
                    (rhs, weeks, rows, lon),
                    lambda _, first: (first[0], 0, 0, 0),
                    pipeline_mode=pl.Buffered(1),
                ),
                whole((rows, lon)),
            ],
            out_specs=[whole((rhs, weeks, rows, lon)), whole((words, lon))],
        ),
        out_shape=[
            jax.ShapeDtypeStruct((rhs, weeks, rows, lon), jnp.float32),
            jax.ShapeDtypeStruct((words, lon), jnp.int32),
        ],
        compiler_params=params(6),
        cost_estimate=cost(rhs * weeks * rows * lon * 100, rhs * weeks * rows * lon * 10),
        name="spread_lon",
    )(first, direction, counts)


def lat_mix(weights_ref, window_ref, k, week, before_ref, own_ref, after_ref, scales):
    rhs, weeks, rows, lon = own_ref.shape
    half = rows // 2
    for base, ref, scale in ((0, before_ref, scales[0]), (2 * rows, after_ref, scales[1])):
        for start in range(0, half, SUBLANES):
            at = (k * weeks + week) * half + start
            word = ref[at : at + SUBLANES, :]
            window_ref[base + start : base + start + SUBLANES, :] = (
                high_of(word).astype(jnp.float32) * scale
            )
            window_ref[base + half + start : base + half + start + SUBLANES, :] = (
                low_of(word).astype(jnp.float32) * scale
            )
    window_ref[rows : 2 * rows, :] = own_ref[k, week]
    return jnp.dot(
        weights_ref[...],
        window_ref[...],
        precision=HIGHEST,
        preferred_element_type=jnp.float32,
    )


def spread_lat_kernel(slots, own_ref, before_ref, after_ref, weights_ref, hot_ref, *rest):
    picks, (window_ref, cells_ref) = rest[:slots], rest[slots:]
    rhs, weeks, rows, lon = own_ref.shape
    body = before_ref.shape[0] - SUBLANES
    parts = lon // LANES
    for k in range(rhs):
        scales = word_scale(before_ref, body, k), word_scale(after_ref, body, k)
        for week in range(weeks):
            mixed = lat_mix(
                weights_ref, window_ref, k, week, before_ref, own_ref, after_ref, scales
            )
            for part in range(parts):
                at = (week * parts + part) * rows
                cells_ref[at : at + rows, k * LANES : (k + 1) * LANES] = mixed[
                    :, part * LANES : (part + 1) * LANES
                ].astype(jnp.bfloat16)
    for slot in range(slots):
        found = jnp.dot(
            hot_ref[slot], cells_ref[...], preferred_element_type=jnp.float32
        ).astype(jnp.bfloat16)
        for k in range(rhs):
            picks[slot][k] = found[:, k * LANES : (k + 1) * LANES]


def spread_lat(own, before, after, weights, hot):
    rhs, weeks, rows, lon = own.shape
    slots, blocks, cols = hot.shape
    return pl.pallas_call(
        functools.partial(spread_lat_kernel, slots),
        in_specs=in_vmem(5),
        out_specs=in_vmem(slots),
        out_shape=[jax.ShapeDtypeStruct((rhs, blocks, LANES), jnp.bfloat16)] * slots,
        scratch_shapes=[
            pltpu.VMEM((3 * rows, lon), jnp.float32),
            pltpu.VMEM((cols, rhs * LANES), jnp.bfloat16),
        ],
        compiler_params=params(10),
        cost_estimate=cost(rhs * slots * blocks * cols * LANES * 2, rhs * weeks * rows * lon * 10),
        name="spread_lat",
    )(own, before, after, weights, hot)


def chunk_of(count, most):
    return max(size for size in range(1, most + 1) if count % size == 0)


def preload_kernel(after_ref, blocks_ref, out_ref, done):
    del after_ref
    parts = done.shape[0]
    size = blocks_ref.shape[0] // parts
    copies = [
        pltpu.make_async_copy(
            blocks_ref.at[pl.ds(part * size, size)],
            out_ref.at[pl.ds(part * size, size)],
            done.at[part],
        )
        for part in range(parts)
    ]
    for copy in copies:
        copy.start()
    for copy in copies:
        copy.wait()


def preload(blocks, after):
    parts = chunk_of(blocks.shape[0], COPIES)
    return pl.pallas_call(
        preload_kernel,
        in_specs=[pl.BlockSpec(memory_space=pl.ANY)] * 2,
        out_specs=pl.BlockSpec(memory_space=pltpu.VMEM),
        out_shape=jax.ShapeDtypeStruct(blocks.shape, blocks.dtype),
        scratch_shapes=[pltpu.SemaphoreType.DMA((parts,))],
        compiler_params=params(13),
        cost_estimate=cost(0, blocks.size * 4),
        name="preload",
    )(after, blocks)


def forward_kernel(row_ref, scale_ref, blocks_ref, *rest):
    picks, (out_ref, cells_ref) = rest[:-2], rest[-2:]
    rhs, count, edge = picks[0].shape
    lines = len(picks) * rhs
    out_ref[...] = jnp.zeros_like(out_ref)
    for place, pick_ref in enumerate(picks):
        for k in range(rhs):
            cells_ref[pl.ds(place * rhs + k, count, stride=lines), :] = pick_ref[k].astype(
                jnp.float32
            )
    chunk = 2 * chunk_of(count // 2, CHUNK // 2)

    def one_chunk(step, carry):
        values = []
        for n in range(0, chunk, 2):
            index = step * chunk + n
            at = pl.multiple_of(index * lines, 2 * lines)
            both = lax.dot_general(
                cells_ref[pl.ds(at, 2 * lines), :].astype(jnp.bfloat16),
                blocks_ref[pl.ds(index, 2)].reshape(2 * edge, edge),
                (((1,), (1,)), ((), ())),
                preferred_element_type=jnp.float32,
            )
            values += [both[:lines, :edge], both[lines:, edge:]]
        for n in range(chunk):
            index = step * chunk + n
            at = pl.multiple_of(row_ref[index] * lines, lines)
            out_ref[pl.ds(at, lines), :] += values[n] * scale_ref[index]
        return carry

    lax.fori_loop(0, count // chunk, one_chunk, 0)


def forward(row_list, scales, blocks, picks, row_blocks):
    rhs, count, edge = picks[0].shape
    lines = len(picks) * rhs
    return pl.pallas_call(
        forward_kernel,
        in_specs=[pl.BlockSpec(memory_space=pltpu.SMEM)] * 2 + in_vmem(1 + len(picks)),
        out_specs=pl.BlockSpec(memory_space=pltpu.VMEM),
        out_shape=jax.ShapeDtypeStruct((row_blocks * lines, edge), jnp.float32),
        scratch_shapes=[pltpu.VMEM((count * lines, edge), jnp.float32)],
        compiler_params=params(15),
        cost_estimate=cost(blocks.size * 2 * lines, blocks.size * 2),
        name="forward",
    )(row_list, scales, blocks, *picks)


def adjoint_kernel(rhs, row_ref, scale_ref, blocks_ref, values_ref, *rest):
    outs, terms_ref = rest[:-1], rest[-1]
    lines = len(outs) * rhs
    count, edge, _ = blocks_ref.shape
    chunk = 2 * chunk_of(count // 2, CHUNK // 2)

    def one_chunk(step, carry):
        for n in range(0, chunk, 2):
            index = step * chunk + n
            pulled = [
                values_ref[pl.ds(pl.multiple_of(row_ref[index + q] * lines, lines), lines), :]
                for q in range(2)
            ]
            both = jnp.dot(
                jnp.concatenate(pulled, axis=0).astype(jnp.bfloat16),
                jnp.concatenate([blocks_ref[index + q] for q in range(2)], axis=1),
                preferred_element_type=jnp.float32,
            )
            for q in range(2):
                to = pl.multiple_of((index + q) * lines, lines)
                part = both[q * lines : (q + 1) * lines, q * edge : (q + 1) * edge]
                terms_ref[pl.ds(to, lines), :] = part * scale_ref[index + q]
        return carry

    lax.fori_loop(0, count // chunk, one_chunk, 0)
    half = count // 2
    for place, out_ref in enumerate(outs):
        terms = [terms_ref[pl.ds(place * rhs + k, count, stride=lines), :] for k in range(rhs)]
        exponents = exponent_rows([jnp.abs(term) for term in terms])
        out_ref[rhs * half :, :] = exponents
        for k in range(rhs):
            number = to_int(terms[k], pow2(15 - exponents[k : k + 1]))
            out_ref[k * half : (k + 1) * half, :] = pack(number[:half], number[half:])


def adjoint_terms(row_list, scales, blocks, values, outs, rhs):
    count, edge, _ = blocks.shape
    lines = outs * rhs
    words = rhs * count // 2 + SUBLANES
    return pl.pallas_call(
        functools.partial(adjoint_kernel, rhs),
        in_specs=[pl.BlockSpec(memory_space=pltpu.SMEM)] * 2 + in_vmem(2),
        out_specs=in_vmem(outs),
        out_shape=[jax.ShapeDtypeStruct((words, edge), jnp.int32)] * outs,
        scratch_shapes=[pltpu.VMEM((count * lines, edge), jnp.float32)],
        compiler_params=params(15),
        cost_estimate=cost(blocks.size * 2 * lines, blocks.size * 2),
        name="adjoint",
    )(row_list, scales, blocks, values)


def gather_cells_kernel(slots, hot_ref, *rest):
    terms, (field_ref, word_ref, split_ref) = rest[:slots], rest[slots:]
    rhs, weeks, rows, lon = field_ref.shape
    count = hot_ref.shape[1] // slots
    half = count // 2
    wide = rhs * LANES
    for slot in range(slots):
        for k in range(rhs):
            scale = word_scale(terms[slot], rhs * half, k)[:1]
            word = terms[slot][k * half : (k + 1) * half, :]
            for base, number in ((0, high_of(word)), (half, low_of(word))):
                coarse = (number + 128) >> 8
                fine = number - (coarse << 8)
                at = slot * count + base
                split_ref[at : at + half, k * LANES : (k + 1) * LANES] = (
                    (coarse << 8).astype(jnp.float32) * scale
                ).astype(jnp.bfloat16)
                split_ref[at : at + half, wide + k * LANES : wide + (k + 1) * LANES] = (
                    fine.astype(jnp.float32) * scale
                ).astype(jnp.bfloat16)
    peaks = [jnp.zeros((SUBLANES, lon), jnp.float32)] * rhs
    parts = lon // LANES
    for week in range(weeks):
        at = week * parts * rows
        both = jnp.dot(
            hot_ref[at : at + parts * rows, :],
            split_ref[...],
            preferred_element_type=jnp.float32,
        )
        cells = both[:, :wide] + both[:, wide:]
        for k in range(rhs):
            for part in range(parts):
                field_ref[k, week, :, part * LANES : (part + 1) * LANES] = cells[
                    part * rows : (part + 1) * rows, k * LANES : (k + 1) * LANES
                ]
            for start in range(0, rows, SUBLANES):
                peaks[k] = jnp.maximum(
                    peaks[k], jnp.abs(field_ref[k, week, start : start + SUBLANES, :])
                )
    pack_field(field_ref, word_ref, peaks)


def gather_cells(hot_turned, terms, rhs, weeks, rows, lon):
    slots = len(terms)
    return pl.pallas_call(
        functools.partial(gather_cells_kernel, slots),
        in_specs=in_vmem(1 + slots),
        out_specs=in_vmem(2),
        out_shape=[
            jax.ShapeDtypeStruct((rhs, weeks, rows, lon), jnp.float32),
            jax.ShapeDtypeStruct((words_of(rhs, weeks, rows), lon), jnp.int32),
        ],
        scratch_shapes=[pltpu.VMEM((hot_turned.shape[1], 2 * rhs * LANES), jnp.bfloat16)],
        compiler_params=params(12),
        cost_estimate=cost(rhs * hot_turned.size * 4 * LANES, rhs * weeks * rows * lon * 10),
        name="gather_cells",
    )(hot_turned, *terms)


def pull_back_kernel(
    own_ref, before_ref, after_ref, weights_ref, count_ref, word_ref, window_ref, field_ref
):
    rhs, weeks, rows, lon = own_ref.shape
    body = before_ref.shape[0] - SUBLANES
    for k in range(rhs):
        scales = word_scale(before_ref, body, k), word_scale(after_ref, body, k)
        for week in range(weeks):
            field_ref[k, week] = lat_mix(
                weights_ref, window_ref, k, week, before_ref, own_ref, after_ref, scales
            )
    pack_field(field_ref, word_ref, lon_field(field_ref, count_ref, field_ref))


def pull_back(own, before, after, weights, counts):
    rhs, weeks, rows, lon = own.shape
    return pl.pallas_call(
        pull_back_kernel,
        in_specs=in_vmem(5),
        out_specs=pl.BlockSpec(memory_space=pltpu.VMEM),
        out_shape=jax.ShapeDtypeStruct(before.shape, jnp.int32),
        scratch_shapes=[
            pltpu.VMEM((3 * rows, lon), jnp.float32),
            pltpu.VMEM((rhs, weeks, rows, lon), jnp.float32),
        ],
        compiler_params=params(8),
        cost_estimate=cost(rhs * weeks * rows * lon * 300, rhs * weeks * rows * lon * 10),
        name="pull_back",
    )(own, before, after, weights, counts)


PAIRS = 16


def gram_kernel(with_old, count, rhs, order_ref, sums_before, residual_ref, direction_ref, *rest):
    words, rest = rest[:count], rest[count:]
    news, gram_ref, sums_ref = rest[-count - 2 : -2], rest[-2], rest[-1]
    olds = rest[: -count - 2]
    rhs_count, weeks, rows, lon = direction_ref.shape
    half = rows // 2
    body = words[0].shape[0] - SUBLANES
    first = len(olds)

    def natural(place):
        return order_ref[place // rhs] + place % rhs

    for word_ref, new_ref, slot in zip(words, news, range(first, first + count)):
        for k in range(rhs):
            index = natural(slot * rhs + k)
            scale = word_scale(word_ref, body, k)

            def one_week(week, carry):
                for start in range(0, half, SUBLANES):
                    at = pl.multiple_of((k * weeks + week) * half + start, SUBLANES)
                    word = word_ref[pl.ds(at, SUBLANES), :]
                    for base, number in ((start, high_of(word)), (half + start, low_of(word))):
                        new_ref[k, week, base : base + SUBLANES, :] = (
                            direction_ref[index, week, base : base + SUBLANES, :]
                            + number.astype(jnp.float32) * scale
                        )
                return carry

            lax.fori_loop(0, weeks, one_week, 0)

    sums_ref[...] = jnp.zeros_like(sums_ref)
    row_groups = rows // SUBLANES

    def tile(index, lefts, rights, mirror):
        def one_group(step, sums):
            week = step // row_groups
            at = pl.multiple_of((step % row_groups) * SUBLANES, SUBLANES)
            sums = list(sums)
            for lane in range(0, lon, LANES):
                spot = (week, pl.ds(at, SUBLANES), slice(lane, lane + LANES))
                left = [ref[(k, *spot)] for ref, k, _ in lefts]
                right = [ref[(k, *spot)] for ref, k, _ in rights]
                for a in range(len(lefts)):
                    for b in range(len(rights)):
                        place = a * len(rights) + b
                        sums[place] = sums[place] + left[a] * right[b]
            return tuple(sums)

        zero = jnp.zeros((SUBLANES, LANES), jnp.float32)
        sums = lax.fori_loop(
            0, weeks * row_groups, one_group, (zero,) * (len(lefts) * len(rights))
        )
        for a, (_, _, row) in enumerate(lefts):
            for b, (_, _, column) in enumerate(rights):
                for row_at, column_at in ((row, column), (column, row))[: 1 + mirror]:
                    at = ((index * rhs_count + row_at) * rhs_count + column_at) * SUBLANES
                    at = pl.multiple_of(at, SUBLANES)
                    sums_ref[pl.ds(at, SUBLANES), :] = sums[a * len(rights) + b]

    def listed(refs, slot):
        return [
            (ref, k, natural((slot + place) * rhs + k))
            for place, ref in enumerate(refs)
            for k in range(rhs)
        ]

    def tiles(index, lefts, rights, mirror=False):
        wide = min(len(rights), 4)
        tall = PAIRS // wide
        for a in range(0, len(lefts), tall):
            for b in range(0, len(rights), wide):
                if lefts is rights and b + wide <= a:
                    continue
                tile(index, lefts[a : a + tall], rights[b : b + wide], mirror)

    residuals = [(residual_ref, k, k) for k in range(rhs_count)]
    directions = [(direction_ref, k, k) for k in range(rhs_count)]
    images = listed(news, first)
    if with_old:
        tiles(0, residuals, residuals, True)
    tiles(1, directions, images)
    tiles(2, residuals, images)
    tiles(3, images, images, True)
    if olds:
        tiles(3, listed(olds, 0), images, True)

    total = sums_ref.shape[0] // SUBLANES
    lanes = sums_ref[pl.ds(0, total, stride=SUBLANES), :]
    for line in range(1, SUBLANES):
        lanes = lanes + sums_ref[pl.ds(line, total, stride=SUBLANES), :]
    gram_ref[...] = sums_before[...] + lax.dot_general(
        jnp.ones((SUBLANES, LANES), jnp.float32),
        lanes,
        (((1,), (1,)), ((), ())),
        precision=HIGHEST,
        preferred_element_type=jnp.float32,
    )


def grams(order, sums, residual, direction, words, olds, with_old):
    rhs_count, weeks, rows, lon = direction.shape
    total = 4 * rhs_count**2
    rhs = (words[0].shape[0] - SUBLANES) * 2 // (weeks * rows)
    count = len(words)
    found = pl.pallas_call(
        functools.partial(gram_kernel, with_old, count, rhs),
        in_specs=[pl.BlockSpec(memory_space=pltpu.SMEM)] + in_vmem(3 + count + len(olds)),
        out_specs=in_vmem(count + 1),
        out_shape=[jax.ShapeDtypeStruct((rhs, weeks, rows, lon), jnp.float32)] * count
        + [jax.ShapeDtypeStruct((SUBLANES, total), jnp.float32)],
        scratch_shapes=[pltpu.VMEM((total * SUBLANES, LANES), jnp.float32)],
        compiler_params=params(14),
        cost_estimate=cost(8 * rhs_count * direction.size, 16 * direction.size),
        name="grams",
    )(order, sums, residual, direction, *words, *olds)
    return list(found[:-1]), found[-1]


def small_product(left, right):
    total = jnp.zeros((SUBLANES, LANES), jnp.float32)
    for j in range(SUBLANES):
        column = jnp.broadcast_to(left[:, j : j + 1], (SUBLANES, LANES))
        total = total + column * jnp.broadcast_to(right[j : j + 1, :], (SUBLANES, LANES))
    return total


def small_transpose(value):
    rest = jnp.zeros((LANES - SUBLANES, LANES), jnp.float32)
    return jnp.concatenate([value, rest], axis=0).T[:SUBLANES]


def small_solve(matrix, right):
    line = lax.broadcasted_iota(jnp.int32, (SUBLANES, LANES), 0)
    both = matrix + pltpu.roll(right, SUBLANES, 1)
    for j in range(SUBLANES):
        column = jnp.broadcast_to(both[:, j : j + 1], (SUBLANES, LANES))
        pivot = jnp.broadcast_to(both[j : j + 1, :], (SUBLANES, LANES))
        scaled = pivot / jnp.broadcast_to(both[j : j + 1, j : j + 1], (SUBLANES, LANES))
        both = jnp.where(line == j, scaled, both - column * scaled)
    lane = lax.broadcasted_iota(jnp.int32, (SUBLANES, LANES), 1)
    return jnp.where(lane < SUBLANES, pltpu.roll(both, LANES - SUBLANES, 1), 0.0)


def solve_steps(sums_ref, coef_ref):
    total = sums_ref.shape[1]
    size = SUBLANES
    place = lax.broadcasted_iota(jnp.int32, (size, total), 1)
    line = lax.broadcasted_iota(jnp.int32, (size, total), 0)
    spot = lax.broadcasted_iota(jnp.int32, (total, LANES), 0)
    lane = lax.broadcasted_iota(jnp.int32, (total, LANES), 1)
    to_column = jnp.where(spot % size == lane, 1.0, 0.0)
    sums = sums_ref[...]

    def matrix(index):
        rows = jnp.where(place // size == index * size + line, sums, 0.0)
        return jnp.dot(rows, to_column, precision=HIGHEST, preferred_element_type=jnp.float32)

    gram_old, curvature, mixed, gram_image = [matrix(index) for index in range(4)]
    curvature = 0.5 * (curvature + small_transpose(curvature))
    step = small_solve(curvature, gram_old)
    cross = small_product(mixed, step)
    both = small_product(small_transpose(step), small_product(gram_image, step))
    gram_new = gram_old - cross - small_transpose(cross) + both
    turn = small_solve(gram_old, gram_new)
    for index, matrix in enumerate((step, turn)):
        for b in range(size):
            for a in range(size):
                at = ((index * size + b) * size + a) * SUBLANES
                coef_ref[at : at + SUBLANES, :] = jnp.broadcast_to(
                    matrix[b : b + 1, a : a + 1], (SUBLANES, LANES)
                )


def summed_slots(terms, rhs):
    parts = [
        functools.reduce(lambda left, right: left + right, terms[at : at + rhs])
        for at in range(0, len(terms), rhs)
    ]
    while len(parts) > 1:
        parts = [left + right for left, right in zip(parts[::2], parts[1::2])]
    return parts[0]


def update_kernel(
    order_ref, sums_ref, solution_ref, residual_ref, direction_ref, *rest
):
    images, (sol_out, res_out, dir_out, coef_ref) = rest[:-4], rest[-4:]
    rhs_count, _, rows, lon = direction_ref.shape
    rhs = images[0].shape[0]

    @pl.when((pl.program_id(0) == 0) & (pl.program_id(1) == 0))
    def _():
        solve_steps(sums_ref, coef_ref)

    def coef(index, b, a):
        at = ((index * rhs_count + b) * rhs_count + a) * SUBLANES
        return coef_ref[pl.ds(pl.multiple_of(at, SUBLANES), SUBLANES), :]

    natural = [order_ref[slot] + k for slot in range(len(images)) for k in range(rhs)]

    def one_group(group, carry):
        at = pl.multiple_of(group * SUBLANES, SUBLANES)
        for lane in range(0, lon, LANES):
            spot = (0, pl.ds(at, SUBLANES), slice(lane, lane + LANES))
            directions = [direction_ref[(b, *spot)] for b in range(rhs_count)]
            image = [ref[(k, *spot)] for ref in images for k in range(rhs)]
            for a in range(rhs_count):
                moved = solution_ref[(a, *spot)]
                left = residual_ref[(a, *spot)]
                for b in range(rhs_count):
                    moved = moved + coef(0, b, a) * directions[b]
                left = left - summed_slots(
                    [coef(0, natural[b], a) * image[b] for b in range(rhs_count)], rhs
                )
                sol_out[(a, *spot)] = moved
                res_out[(a, *spot)] = left
                for b in range(rhs_count):
                    left = left + coef(1, b, a) * directions[b]
                dir_out[(a, *spot)] = left
        return carry

    lax.fori_loop(0, rows // SUBLANES, one_group, 0)


def update(order, sums, solution, residual, direction, images):
    rhs_count, weeks, rows, lon = direction.shape
    half = rows // 2

    def field(rhs):
        return pl.BlockSpec((rhs, 1, half, lon), lambda w, h, _: (0, w, h, 0))

    shape = jax.ShapeDtypeStruct(direction.shape, jnp.float32)
    return pl.pallas_call(
        update_kernel,
        grid_spec=pltpu.PrefetchScalarGridSpec(
            num_scalar_prefetch=1,
            grid=(weeks, 2),
            in_specs=[whole(sums.shape)]
            + [field(rhs_count)] * 3
            + [field(image.shape[0]) for image in images],
            out_specs=[field(rhs_count)] * 3,
            scratch_shapes=[pltpu.VMEM((2 * rhs_count**2 * SUBLANES, LANES), jnp.float32)],
        ),
        out_shape=[shape] * 3,
        compiler_params=params(10),
        cost_estimate=cost(6 * rhs_count * direction.size, 28 * direction.size),
        name="update",
    )(order, sums, solution, residual, direction, *images)


def crossed(value, axis, by):
    if by == 0:
        return value
    return lax.ppermute(value, axis, [(i, i ^ by) for i in range(lax.axis_size(axis))])


def neighbours(value, axis):
    size = lax.axis_size(axis)
    before = lax.ppermute(value, axis, [(i, i + 1) for i in range(size - 1)])
    after = lax.ppermute(value, axis, [(i + 1, i) for i in range(size - 1)])
    return before, after


def summed_over(value, axis):
    size = lax.axis_size(axis)
    reach = 1
    while reach < size:
        value = value + crossed(value, axis, reach)
        reach *= 2
    return value


def summed_in_halves(value, axis):
    size = lax.axis_size(axis)
    if size < 4:
        return summed_over(value, axis)
    half = value.shape[0] // 2
    low, high = value[:half], value[half:]
    even = lax.axis_index(axis) % 2 == 0
    mine = jnp.where(even, low, high) + crossed(jnp.where(even, high, low), axis, 1)
    reach = 2
    while reach < size:
        mine = mine + crossed(mine, axis, reach)
        reach *= 2
    other = crossed(mine, axis, 1)
    return jnp.concatenate([jnp.where(even, mine, other), jnp.where(even, other, mine)], axis=0)


def lat_windows(lat_width, band, rows):
    decay = rows / 2.0
    total = lat_width.shape[0]
    offsets = jnp.abs(jnp.arange(-rows, rows + 1)).astype(jnp.float32)
    limits = lat_width.astype(jnp.float32)
    normal = jnp.sqrt(
        jnp.sum(
            jnp.where(
                offsets[None, :] <= limits[:, None], jnp.exp(-2.0 * offsets / decay)[None, :], 0.0
            ),
            axis=1,
        )
    )
    padded_limits = jnp.pad(limits, (rows, rows), constant_values=-1.0)
    padded_normal = jnp.pad(normal, (rows, rows), constant_values=1.0)
    near_limits = lax.dynamic_slice_in_dim(padded_limits, band * rows, 3 * rows)
    near_normal = lax.dynamic_slice_in_dim(padded_normal, band * rows, 3 * rows)
    distance = jnp.abs(
        jnp.arange(rows)[:, None] + rows - jnp.arange(3 * rows)[None, :]
    ).astype(jnp.float32)
    fade = jnp.exp(-distance / decay)
    own_limits, own_normal = near_limits[rows : 2 * rows, None], near_normal[rows : 2 * rows, None]
    spread = jnp.where(distance <= own_limits, fade, 0.0) / own_normal
    pulled = jnp.where(distance <= near_limits[None, :], fade, 0.0) / near_normal[None, :]
    return spread, pulled


def shards(
    footprints,
    block_rows,
    block_cols,
    block_scale,
    lat_width,
    lon_width,
    obs_weight,
    solution,
    residual,
    direction,
):
    rhs_count, weeks, rows, lon = direction.shape
    blocks = footprints[0, 0]
    count, edge, _ = blocks.shape
    row_list, col_list = block_rows[0, 0], block_cols[0, 0]
    scales = jnp.exp2(-block_scale[0, 0].astype(jnp.float32))
    row_blocks = obs_weight.shape[0] // edge
    slots = lax.axis_size("obs")
    rhs = rhs_count // slots
    slab, band = lax.axis_index("obs"), lax.axis_index("lat")
    parts = lon // edge
    cols = weeks * rows * parts

    groups = rhs // GROUP_RHS if rhs % GROUP_RHS == 0 else 1
    each = rhs // groups
    first = (slab * groups).astype(jnp.int32)
    others = slab ^ jnp.arange(slots, dtype=jnp.int32)
    order = others * rhs
    own_width = lax.dynamic_slice_in_dim(lon_width, band * rows, rows)
    counts = jnp.broadcast_to(own_width[:, None] + 1, (rows, lon))

    line, part = col_list // parts, col_list % parts
    place = ((line // rows) * parts + part) * rows + line % rows
    places = place[None]
    reach = 1
    while reach < slots:
        places = jnp.concatenate([places, crossed(places, "obs", reach)], axis=0)
        reach *= 2

    lon_own, halos = [], []
    for group in range(groups):
        own, words = spread_lon(direction, (first + group).reshape(1), each, counts)
        lon_own.append(own)
        halos.append(neighbours(words, "lat"))

    hot = (places[:, :, None] == jnp.arange(cols)[None, None, :]).astype(jnp.bfloat16)
    hot_turned = (jnp.arange(cols)[:, None] == places.reshape(1, -1)).astype(jnp.bfloat16)
    lat_spread, lat_pulled = lat_windows(lat_width, band, rows)

    cells = [[None] * groups for _ in range(slots)]
    for group in range(groups):
        picks = spread_lat(lon_own[group], *halos[group], lat_spread, hot)
        for d in range(slots):
            cells[d][group] = crossed(picks[d], "obs", d)
    cells = [cell for slot_cells in cells for cell in slot_cells]
    near_blocks = preload(blocks, cells[0])
    sums = summed_in_halves(forward(row_list, scales, near_blocks, cells, row_blocks), "lat")
    weighted = sums.reshape(row_blocks, slots * rhs, edge) * obs_weight.reshape(row_blocks, 1, edge)
    terms = adjoint_terms(
        row_list, scales, near_blocks, weighted.reshape(-1, edge), slots * groups, each
    )
    images = [[None] * groups for _ in range(slots)]
    for group in range(groups):
        sent = [crossed(terms[d * groups + group], "obs", d) for d in range(slots)]
        field, words = gather_cells(hot_turned, sent, each, weeks, rows, lon)
        words = pull_back(field, *neighbours(words, "lat"), lat_pulled, counts)
        for d in range(slots):
            images[d][group] = crossed(words, "obs", d)

    starts = (order[:, None] + jnp.arange(groups, dtype=jnp.int32) * each).reshape(-1)
    products = jnp.zeros((SUBLANES, 4 * rhs_count**2), jnp.float32)
    found = []
    for d in range(slots):
        new, products = grams(starts, products, residual, direction, images[d], found, d == 0)
        found += new
    products = summed_over(products, "lat")
    return tuple(update(starts, products, solution, residual, direction, found))


def solution(mesh):
    return jax.shard_map(
        shards,
        mesh=mesh,
        in_specs=(
            P("obs", "lat", None, None, None),
            P("obs", "lat", None),
            P("obs", "lat", None),
            P("obs", "lat", None),
            P(),
            P(),
            P("obs"),
            P(None, None, "lat", None),
            P(None, None, "lat", None),
            P(None, None, "lat", None),
        ),
        out_specs=(
            P(None, None, "lat", None),
            P(None, None, "lat", None),
            P(None, None, "lat", None),
        ),
        check_vma=False,
    )
```

```python
import functools
import math

import jax
import jax.numpy as jnp
from jax import lax
from jax.experimental import pallas as pl
from jax.experimental.pallas import tpu as pltpu
from jax.sharding import PartitionSpec as P

LANES = 128
CHUNK = 96
COPIES = 12
STREAM_MIB = 40
BACK_GROUPS = 1
SUBLANES = 8
MIB = 1024 * 1024
HIGHEST = lax.Precision.HIGHEST


def params(mib):
    return pltpu.CompilerParams(vmem_limit_bytes=mib * MIB)


def cost(flops, nbytes):
    return pl.CostEstimate(flops=int(flops), bytes_accessed=int(nbytes), transcendentals=0)


def whole(shape):
    return pl.BlockSpec(shape, lambda *_: (0,) * len(shape), pipeline_mode=pl.Buffered(1))


def in_vmem(count):
    return [pl.BlockSpec(memory_space=pltpu.VMEM)] * count


def pow2(exponent):
    size = jnp.abs(exponent)
    up = jnp.ones(exponent.shape, jnp.float32)
    down = up
    for bit in range(7):
        on = ((size >> bit) & 1) == 1
        up = up * jnp.where(on, 2.0 ** (2**bit), 1.0)
        down = down * jnp.where(on, 2.0 ** -(2**bit), 1.0)
    return jnp.where(exponent < 0, down, up)


def exponent_of(peak):
    logs = jnp.log(jnp.maximum(peak, 1e-28)) * (1.0 / math.log(2.0))
    return jnp.ceil(logs + 1e-3).astype(jnp.int32)


def to_int(values, factor):
    return jnp.clip(jnp.round(values * factor), -32767.0, 32767.0).astype(jnp.int32)


def pack(high, low):
    return (high << 16) | (low & 0xFFFF)


def high_of(word):
    return word >> 16


def low_of(word):
    return (word << 16) >> 16


def words_of(rhs, weeks, rows):
    return rhs * weeks * rows // 2 + SUBLANES


def exponent_rows(peaks):
    line = lax.broadcasted_iota(jnp.int32, (SUBLANES, peaks[0].shape[1]), 0)
    found = jnp.zeros(line.shape, jnp.int32)
    for k, peak in enumerate(peaks):
        found = jnp.where(line == k, exponent_of(jnp.max(peak, axis=0, keepdims=True)), found)
    return found


def pack_field(field_ref, word_ref, peaks):
    rhs, weeks, rows, lon = field_ref.shape
    half = rows // 2
    exponents = exponent_rows(peaks)
    word_ref[rhs * weeks * half :, :] = exponents
    for k in range(rhs):
        factor = pow2(15 - jnp.broadcast_to(exponents[k : k + 1], (SUBLANES, lon)))

        def one_week(week, carry):
            for start in range(0, half, SUBLANES):
                high = to_int(field_ref[k, week, start : start + SUBLANES, :], factor)
                low = to_int(field_ref[k, week, half + start : half + start + SUBLANES, :], factor)
                at = pl.multiple_of((k * weeks + week) * half + start, SUBLANES)
                word_ref[pl.ds(at, SUBLANES), :] = pack(high, low)
            return carry

        lax.fori_loop(0, weeks, one_week, 0)


def word_scale(word_ref, body, k):
    row = word_ref[body + k : body + k + 1, :] - 15
    return pow2(jnp.broadcast_to(row, (SUBLANES, row.shape[1])))


def lon_setup(lon):
    return lon / 32.0, (lon // 8 + 1).bit_length()


def lon_rows(rows, count, norm, lon):
    decay, bits = lon_setup(lon)
    fields = rows.shape[0] // SUBLANES
    count = jnp.concatenate([count] * fields, axis=0)
    windows = [rows, rows]
    taken = [jnp.zeros_like(rows)] * 2
    for bit in range(bits):
        reach = 2**bit
        fade = math.exp(-reach / decay)
        chosen = ((count >> bit) & 1) == 1
        for side in range(2):
            shift = reach if side == 0 else lon - reach
            moved = windows[side]
            if bit:
                moved = moved + fade * pltpu.roll(taken[side], shift, 1)
            taken[side] = jnp.where(chosen, moved, taken[side])
            if bit + 1 < bits:
                windows[side] = windows[side] + fade * pltpu.roll(windows[side], shift, 1)
    return (taken[0] + taken[1] - rows) * jnp.concatenate([norm] * fields, axis=0)


def lon_norm(count, lon):
    decay, _ = lon_setup(lon)
    ratio = math.exp(-2.0 / decay)
    ends = jnp.exp(count.astype(jnp.float32) * (-2.0 / decay))
    return 1.0 / jnp.sqrt(1.0 + (2.0 / (1.0 - ratio)) * (ratio - ends))


def lon_field(source_ref, count_ref, out_ref):
    rhs, weeks, rows, lon = out_ref.shape

    def one_group(group, peaks):
        at = pl.multiple_of(group * SUBLANES, SUBLANES)
        count = count_ref[pl.ds(at, SUBLANES), :]
        norm = lon_norm(count, lon)
        fields = [source_ref[k, w, pl.ds(at, SUBLANES), :] for k in range(rhs) for w in range(weeks)]
        result = lon_rows(jnp.concatenate(fields, axis=0), count, norm, lon)
        peaks = list(peaks)
        for k in range(rhs):
            for w in range(weeks):
                start = (k * weeks + w) * SUBLANES
                part = result[start : start + SUBLANES]
                out_ref[k, w, pl.ds(at, SUBLANES), :] = part
                peaks[k] = jnp.maximum(peaks[k], jnp.abs(part))
        return tuple(peaks)

    zero = jnp.zeros((SUBLANES, lon), jnp.float32)
    return lax.fori_loop(0, rows // SUBLANES, one_group, (zero,) * rhs)


def spread_lon_kernel(field_ref, count_ref, out_ref, word_ref):
    pack_field(out_ref, word_ref, lon_field(field_ref, count_ref, out_ref))


def spread_lon(field, counts):
    rhs, weeks, rows, lon = field.shape
    return pl.pallas_call(
        spread_lon_kernel,
        in_specs=in_vmem(2),
        out_specs=in_vmem(2),
        out_shape=[
            jax.ShapeDtypeStruct(field.shape, jnp.float32),
            jax.ShapeDtypeStruct((words_of(rhs, weeks, rows), lon), jnp.int32),
        ],
        compiler_params=params(6),
        cost_estimate=cost(field.size * 100, field.size * 10),
        name="spread_lon",
    )(field, counts)


def lat_mix(weights_ref, window_ref, k, week, before_ref, own_ref, after_ref, scales):
    rhs, weeks, rows, lon = own_ref.shape
    half = rows // 2
    for base, ref, scale in ((0, before_ref, scales[0]), (2 * rows, after_ref, scales[1])):
        for start in range(0, half, SUBLANES):
            at = (k * weeks + week) * half + start
            word = ref[at : at + SUBLANES, :]
            window_ref[base + start : base + start + SUBLANES, :] = (
                high_of(word).astype(jnp.float32) * scale
            )
            window_ref[base + half + start : base + half + start + SUBLANES, :] = (
                low_of(word).astype(jnp.float32) * scale
            )
    window_ref[rows : 2 * rows, :] = own_ref[k, week]
    return jnp.dot(
        weights_ref[...],
        window_ref[...],
        precision=HIGHEST,
        preferred_element_type=jnp.float32,
    )


def spread_lat_kernel(slots, own_ref, before_ref, after_ref, weights_ref, hot_ref, *rest):
    picks, (window_ref, cells_ref) = rest[:slots], rest[slots:]
    rhs, weeks, rows, lon = own_ref.shape
    body = before_ref.shape[0] - SUBLANES
    parts = lon // LANES
    for k in range(rhs):
        scales = word_scale(before_ref, body, k), word_scale(after_ref, body, k)
        for week in range(weeks):
            mixed = lat_mix(
                weights_ref, window_ref, k, week, before_ref, own_ref, after_ref, scales
            )
            for part in range(parts):
                at = (week * parts + part) * rows
                cells_ref[at : at + rows, k * LANES : (k + 1) * LANES] = mixed[
                    :, part * LANES : (part + 1) * LANES
                ].astype(jnp.bfloat16)
    for slot in range(slots):
        found = jnp.dot(
            hot_ref[slot], cells_ref[...], preferred_element_type=jnp.float32
        ).astype(jnp.bfloat16)
        for k in range(rhs):
            picks[slot][k] = found[:, k * LANES : (k + 1) * LANES]


def spread_lat(own, before, after, weights, hot):
    rhs, weeks, rows, lon = own.shape
    slots, blocks, cols = hot.shape
    return pl.pallas_call(
        functools.partial(spread_lat_kernel, slots),
        in_specs=in_vmem(5),
        out_specs=in_vmem(slots),
        out_shape=[jax.ShapeDtypeStruct((rhs, blocks, LANES), jnp.bfloat16)] * slots,
        scratch_shapes=[
            pltpu.VMEM((3 * rows, lon), jnp.float32),
            pltpu.VMEM((cols, rhs * LANES), jnp.bfloat16),
        ],
        compiler_params=params(10),
        cost_estimate=cost(rhs * slots * blocks * cols * LANES * 2, rhs * weeks * rows * lon * 10),
        name="spread_lat",
    )(own, before, after, weights, hot)


def chunk_of(count, most):
    return max(size for size in range(1, most + 1) if count % size == 0)


def preload_kernel(after_ref, blocks_ref, out_ref, done):
    del after_ref
    parts = done.shape[0]
    size = blocks_ref.shape[0] // parts
    copies = [
        pltpu.make_async_copy(
            blocks_ref.at[pl.ds(part * size, size)],
            out_ref.at[pl.ds(part * size, size)],
            done.at[part],
        )
        for part in range(parts)
    ]
    for copy in copies:
        copy.start()
    for copy in copies:
        copy.wait()


def preload(blocks, after):
    parts = chunk_of(blocks.shape[0], COPIES)
    return pl.pallas_call(
        preload_kernel,
        in_specs=[pl.BlockSpec(memory_space=pl.ANY)] * 2,
        out_specs=pl.BlockSpec(memory_space=pltpu.VMEM),
        out_shape=jax.ShapeDtypeStruct(blocks.shape, blocks.dtype),
        scratch_shapes=[pltpu.SemaphoreType.DMA((parts,))],
        compiler_params=params(STREAM_MIB),
        cost_estimate=cost(0, blocks.size * 4),
        name="preload",
    )(after, blocks)


def forward_kernel(row_ref, scale_ref, blocks_ref, *rest):
    picks, (out_ref, cells_ref) = rest[:-2], rest[-2:]
    rhs, count, edge = picks[0].shape
    lines = len(picks) * rhs
    out_ref[...] = jnp.zeros_like(out_ref)
    for place, pick_ref in enumerate(picks):
        for k in range(rhs):
            cells_ref[pl.ds(place * rhs + k, count, stride=lines), :] = pick_ref[k].astype(
                jnp.float32
            )
    chunk = 2 * chunk_of(count // 2, CHUNK // 2)

    def one_chunk(step, carry):
        values = []
        for n in range(0, chunk, 2):
            index = step * chunk + n
            at = pl.multiple_of(index * lines, 2 * lines)
            both = lax.dot_general(
                cells_ref[pl.ds(at, 2 * lines), :].astype(jnp.bfloat16),
                blocks_ref[pl.ds(index, 2)].reshape(2 * edge, edge),
                (((1,), (1,)), ((), ())),
                preferred_element_type=jnp.float32,
            )
            values += [both[:lines, :edge], both[lines:, edge:]]
        for n in range(chunk):
            index = step * chunk + n
            at = pl.multiple_of(row_ref[index] * lines, lines)
            out_ref[pl.ds(at, lines), :] += values[n] * scale_ref[index]
        return carry

    lax.fori_loop(0, count // chunk, one_chunk, 0)


def forward(row_list, scales, blocks, picks, row_blocks):
    rhs, count, edge = picks[0].shape
    lines = len(picks) * rhs
    return pl.pallas_call(
        forward_kernel,
        in_specs=[pl.BlockSpec(memory_space=pltpu.SMEM)] * 2 + in_vmem(1 + len(picks)),
        out_specs=pl.BlockSpec(memory_space=pltpu.VMEM),
        out_shape=jax.ShapeDtypeStruct((row_blocks * lines, edge), jnp.float32),
        scratch_shapes=[pltpu.VMEM((count * lines, edge), jnp.float32)],
        compiler_params=params(15),
        cost_estimate=cost(blocks.size * 2 * lines, blocks.size * 2),
        name="forward",
    )(row_list, scales, blocks, *picks)


def adjoint_kernel(rhs, row_ref, scale_ref, blocks_ref, values_ref, *rest):
    outs, terms_ref = rest[:-1], rest[-1]
    lines = len(outs) * rhs
    count, edge, _ = blocks_ref.shape
    chunk = 2 * chunk_of(count // 2, CHUNK // 2)

    def one_chunk(step, carry):
        for n in range(0, chunk, 2):
            index = step * chunk + n
            pulled = [
                values_ref[pl.ds(pl.multiple_of(row_ref[index + q] * lines, lines), lines), :]
                for q in range(2)
            ]
            both = jnp.dot(
                jnp.concatenate(pulled, axis=0).astype(jnp.bfloat16),
                jnp.concatenate([blocks_ref[index + q] for q in range(2)], axis=1),
                preferred_element_type=jnp.float32,
            )
            for q in range(2):
                to = pl.multiple_of((index + q) * lines, lines)
                part = both[q * lines : (q + 1) * lines, q * edge : (q + 1) * edge]
                terms_ref[pl.ds(to, lines), :] = part * scale_ref[index + q]
        return carry

    lax.fori_loop(0, count // chunk, one_chunk, 0)
    half = count // 2
    for place, out_ref in enumerate(outs):
        terms = [terms_ref[pl.ds(place * rhs + k, count, stride=lines), :] for k in range(rhs)]
        exponents = exponent_rows([jnp.abs(term) for term in terms])
        out_ref[rhs * half :, :] = exponents
        for k in range(rhs):
            number = to_int(terms[k], pow2(15 - exponents[k : k + 1]))
            out_ref[k * half : (k + 1) * half, :] = pack(number[:half], number[half:])


def adjoint_terms(row_list, scales, blocks, values, outs, rhs):
    count, edge, _ = blocks.shape
    lines = outs * rhs
    words = rhs * count // 2 + SUBLANES
    return pl.pallas_call(
        functools.partial(adjoint_kernel, rhs),
        in_specs=[pl.BlockSpec(memory_space=pltpu.SMEM)] * 2 + in_vmem(2),
        out_specs=in_vmem(outs),
        out_shape=[jax.ShapeDtypeStruct((words, edge), jnp.int32)] * outs,
        scratch_shapes=[pltpu.VMEM((count * lines, edge), jnp.float32)],
        compiler_params=params(15),
        cost_estimate=cost(blocks.size * 2 * lines, blocks.size * 2),
        name="adjoint",
    )(row_list, scales, blocks, values)


def gather_cells_kernel(slots, hot_ref, *rest):
    terms, (field_ref, word_ref, split_ref) = rest[:slots], rest[slots:]
    rhs, weeks, rows, lon = field_ref.shape
    count = hot_ref.shape[1] // slots
    half = count // 2
    wide = rhs * LANES
    for slot in range(slots):
        for k in range(rhs):
            scale = word_scale(terms[slot], rhs * half, k)[:1]
            word = terms[slot][k * half : (k + 1) * half, :]
            for base, number in ((0, high_of(word)), (half, low_of(word))):
                coarse = (number + 128) >> 8
                fine = number - (coarse << 8)
                at = slot * count + base
                split_ref[at : at + half, k * LANES : (k + 1) * LANES] = (
                    (coarse << 8).astype(jnp.float32) * scale
                ).astype(jnp.bfloat16)
                split_ref[at : at + half, wide + k * LANES : wide + (k + 1) * LANES] = (
                    fine.astype(jnp.float32) * scale
                ).astype(jnp.bfloat16)
    peaks = [jnp.zeros((SUBLANES, lon), jnp.float32)] * rhs
    parts = lon // LANES
    for week in range(weeks):
        at = week * parts * rows
        both = jnp.dot(
            hot_ref[at : at + parts * rows, :],
            split_ref[...],
            preferred_element_type=jnp.float32,
        )
        cells = both[:, :wide] + both[:, wide:]
        for k in range(rhs):
            for part in range(parts):
                field_ref[k, week, :, part * LANES : (part + 1) * LANES] = cells[
                    part * rows : (part + 1) * rows, k * LANES : (k + 1) * LANES
                ]
            for start in range(0, rows, SUBLANES):
                peaks[k] = jnp.maximum(
                    peaks[k], jnp.abs(field_ref[k, week, start : start + SUBLANES, :])
                )
    pack_field(field_ref, word_ref, peaks)


def gather_cells(hot_turned, terms, rhs, weeks, rows, lon):
    slots = len(terms)
    return pl.pallas_call(
        functools.partial(gather_cells_kernel, slots),
        in_specs=in_vmem(1 + slots),
        out_specs=in_vmem(2),
        out_shape=[
            jax.ShapeDtypeStruct((rhs, weeks, rows, lon), jnp.float32),
            jax.ShapeDtypeStruct((words_of(rhs, weeks, rows), lon), jnp.int32),
        ],
        scratch_shapes=[pltpu.VMEM((hot_turned.shape[1], 2 * rhs * LANES), jnp.bfloat16)],
        compiler_params=params(12),
        cost_estimate=cost(rhs * hot_turned.size * 4 * LANES, rhs * weeks * rows * lon * 10),
        name="gather_cells",
    )(hot_turned, *terms)


def pull_back_kernel(
    own_ref, before_ref, after_ref, weights_ref, count_ref, word_ref, window_ref, field_ref
):
    rhs, weeks, rows, lon = own_ref.shape
    body = before_ref.shape[0] - SUBLANES
    for k in range(rhs):
        scales = word_scale(before_ref, body, k), word_scale(after_ref, body, k)
        for week in range(weeks):
            field_ref[k, week] = lat_mix(
                weights_ref, window_ref, k, week, before_ref, own_ref, after_ref, scales
            )
    pack_field(field_ref, word_ref, lon_field(field_ref, count_ref, field_ref))


def pull_back(own, before, after, weights, counts):
    rhs, weeks, rows, lon = own.shape
    return pl.pallas_call(
        pull_back_kernel,
        in_specs=in_vmem(5),
        out_specs=pl.BlockSpec(memory_space=pltpu.VMEM),
        out_shape=jax.ShapeDtypeStruct(before.shape, jnp.int32),
        scratch_shapes=[
            pltpu.VMEM((3 * rows, lon), jnp.float32),
            pltpu.VMEM((rhs, weeks, rows, lon), jnp.float32),
        ],
        compiler_params=params(8),
        cost_estimate=cost(rhs * weeks * rows * lon * 300, rhs * weeks * rows * lon * 10),
        name="pull_back",
    )(own, before, after, weights, counts)


def gram_kernel(with_old, places, count, rhs, order_ref, sums_before, residual_ref, direction_ref, *rest):
    words, rest = rest[:count], rest[count:]
    news, gram_ref, sums_ref = rest[-count - 2 : -2], rest[-2], rest[-1]
    olds = rest[: -count - 2]
    rhs_count, weeks, rows, lon = direction_ref.shape
    half = rows // 2
    body = words[0].shape[0] - SUBLANES
    old_places, new_places = places[: len(olds)], places[len(olds) :]
    for word_ref, new_ref, place in zip(words, news, new_places):
        for k in range(rhs):
            index = order_ref[place] + k
            scale = word_scale(word_ref, body, k)

            def one_week(week, carry):
                for start in range(0, half, SUBLANES):
                    at = pl.multiple_of((k * weeks + week) * half + start, SUBLANES)
                    word = word_ref[pl.ds(at, SUBLANES), :]
                    for base, number in ((start, high_of(word)), (half + start, low_of(word))):
                        new_ref[k, week, base : base + SUBLANES, :] = (
                            direction_ref[index, week, base : base + SUBLANES, :]
                            + number.astype(jnp.float32) * scale
                        )
                return carry

            lax.fori_loop(0, weeks, one_week, 0)

    sums_ref[...] = jnp.zeros_like(sums_ref)
    row_groups = rows // SUBLANES

    def tile(blocks):
        def one_week(week, sums):
            sums = list(sums)
            for row in range(0, rows, SUBLANES):
                for lane in range(0, lon, LANES):
                    spot = (week, slice(row, row + SUBLANES), slice(lane, lane + LANES))
                    place = 0
                    for _, lefts, rights, _ in blocks:
                        right = [ref[(k, *spot)] for ref, k, _ in rights]
                        for ref, k, _ in lefts:
                            left = ref[(k, *spot)]
                            for b in range(len(rights)):
                                sums[place] = sums[place] + left * right[b]
                                place += 1
            return tuple(sums)

        zero = jnp.zeros((SUBLANES, LANES), jnp.float32)
        total = sum(len(lefts) * len(rights) for _, lefts, rights, _ in blocks)
        sums = list(lax.fori_loop(0, weeks, one_week, (zero,) * total))
        for index, lefts, rights, mirror in blocks:
            for _, _, row in lefts:
                for _, _, column in rights:
                    lanes = jnp.sum(sums.pop(0), axis=0, keepdims=True)
                    for row_at, column_at in ((row, column), (column, row))[: 1 + mirror]:
                        at = (index * rhs_count + row_at) * rhs_count + column_at
                        sums_ref[pl.ds(at, 1), :] = lanes

    def listed(refs, places):
        return [
            (ref, k, order_ref[place] + k) for ref, place in zip(refs, places) for k in range(rhs)
        ]

    residuals = [(residual_ref, k, k) for k in range(rhs_count)]
    directions = [(direction_ref, k, k) for k in range(rhs_count)]
    images = listed(news, new_places)
    if with_old:
        for a in range(rhs_count):
            tile([(0, residuals[a : a + 1], residuals[a:], True)])
    for b in range(0, len(images), 2):
        right = images[b : b + 2]
        left = images[: b + len(right)] + listed(olds, old_places)
        tile([(1, directions, right, False), (2, residuals, right, False), (3, left, right, True)])

    gram_ref[...] = sums_before[...] + lax.dot_general(
        jnp.ones((SUBLANES, LANES), jnp.float32),
        sums_ref[...],
        (((1,), (1,)), ((), ())),
        precision=HIGHEST,
        preferred_element_type=jnp.float32,
    )


def grams(order, places, sums, residual, direction, words, olds, with_old):
    rhs_count, weeks, rows, lon = direction.shape
    total = 4 * rhs_count**2
    rhs = (words[0].shape[0] - SUBLANES) * 2 // (weeks * rows)
    count = len(words)
    found = pl.pallas_call(
        functools.partial(gram_kernel, with_old, places, count, rhs),
        in_specs=[pl.BlockSpec(memory_space=pltpu.SMEM)] + in_vmem(3 + count + len(olds)),
        out_specs=in_vmem(count + 1),
        out_shape=[jax.ShapeDtypeStruct((rhs, weeks, rows, lon), jnp.float32)] * count
        + [jax.ShapeDtypeStruct((SUBLANES, total), jnp.float32)],
        scratch_shapes=[pltpu.VMEM((total, LANES), jnp.float32)],
        compiler_params=params(14),
        cost_estimate=cost(8 * rhs_count * direction.size, 16 * direction.size),
        name="grams",
    )(order, sums, residual, direction, *words, *olds)
    return list(found[:-1]), found[-1]


def small_product(left, right):
    total = jnp.zeros((SUBLANES, LANES), jnp.float32)
    for j in range(SUBLANES):
        column = jnp.broadcast_to(left[:, j : j + 1], (SUBLANES, LANES))
        total = total + column * jnp.broadcast_to(right[j : j + 1, :], (SUBLANES, LANES))
    return total


def small_transpose(value):
    rest = jnp.zeros((LANES - SUBLANES, LANES), jnp.float32)
    return jnp.concatenate([value, rest], axis=0).T[:SUBLANES]


def small_solves(systems):
    line = lax.broadcasted_iota(jnp.int32, (SUBLANES, LANES), 0)
    lane = lax.broadcasted_iota(jnp.int32, (SUBLANES, LANES), 1)
    states = [matrix + pltpu.roll(right, SUBLANES, 1) for matrix, right in systems]
    for j in range(SUBLANES):
        for index, both in enumerate(states):
            column = jnp.broadcast_to(both[:, j : j + 1], (SUBLANES, LANES))
            pivot = jnp.broadcast_to(both[j : j + 1, :], (SUBLANES, LANES))
            scaled = pivot / jnp.broadcast_to(both[j : j + 1, j : j + 1], (SUBLANES, LANES))
            states[index] = jnp.where(line == j, scaled, both - column * scaled)
    return [
        jnp.where(lane < SUBLANES, pltpu.roll(both, LANES - SUBLANES, 1), 0.0) for both in states
    ]


def solve_steps(sums_ref, coef_ref):
    total = sums_ref.shape[1]
    size = SUBLANES
    place = lax.broadcasted_iota(jnp.int32, (size, total), 1)
    line = lax.broadcasted_iota(jnp.int32, (size, total), 0)
    spot = lax.broadcasted_iota(jnp.int32, (total, LANES), 0)
    lane = lax.broadcasted_iota(jnp.int32, (total, LANES), 1)
    to_column = jnp.where(spot % size == lane, 1.0, 0.0)
    sums = sums_ref[...]

    def matrix(index):
        rows = jnp.where(place // size == index * size + line, sums, 0.0)
        return jnp.dot(rows, to_column, precision=HIGHEST, preferred_element_type=jnp.float32)

    gram_old, curvature, mixed, gram_image = [matrix(index) for index in range(4)]
    curvature = 0.5 * (curvature + small_transpose(curvature))
    diagonal = lax.broadcasted_iota(jnp.int32, (size, LANES), 0)
    identity = jnp.where(diagonal == lax.broadcasted_iota(jnp.int32, (size, LANES), 1), 1.0, 0.0)
    step, old_inverse = small_solves([(curvature, gram_old), (gram_old, identity)])
    cross = small_product(mixed, step)
    both = small_product(small_transpose(step), small_product(gram_image, step))
    gram_new = gram_old - cross - small_transpose(cross) + both
    turn = small_product(old_inverse, gram_new)
    for index, matrix in enumerate((step, turn)):
        for b in range(size):
            for a in range(size):
                at = ((index * size + b) * size + a) * SUBLANES
                coef_ref[at : at + SUBLANES, :] = jnp.broadcast_to(
                    matrix[b : b + 1, a : a + 1], (SUBLANES, LANES)
                )


def summed_slots(terms, rhs):
    parts = [
        functools.reduce(lambda left, right: left + right, terms[at : at + rhs])
        for at in range(0, len(terms), rhs)
    ]
    while len(parts) > 1:
        parts = [left + right for left, right in zip(parts[::2], parts[1::2])]
    return parts[0]


def update_kernel(
    order_ref, sums_ref, solution_ref, residual_ref, direction_ref, *rest
):
    images, (sol_out, res_out, dir_out, coef_ref) = rest[:-4], rest[-4:]
    rhs_count, _, rows, lon = direction_ref.shape
    rhs = images[0].shape[0]

    @pl.when((pl.program_id(0) == 0) & (pl.program_id(1) == 0))
    def _():
        solve_steps(sums_ref, coef_ref)

    def coef(index, b, a):
        at = ((index * rhs_count + b) * rhs_count + a) * SUBLANES
        return coef_ref[pl.ds(pl.multiple_of(at, SUBLANES), SUBLANES), :]

    natural = [order_ref[slot] + k for slot in range(len(images)) for k in range(rhs)]

    def one_group(group, carry):
        at = pl.multiple_of(group * SUBLANES, SUBLANES)
        for lane in range(0, lon, LANES):
            spot = (0, pl.ds(at, SUBLANES), slice(lane, lane + LANES))
            directions = [direction_ref[(b, *spot)] for b in range(rhs_count)]
            image = [ref[(k, *spot)] for ref in images for k in range(rhs)]
            for a in range(rhs_count):
                moved = solution_ref[(a, *spot)]
                left = residual_ref[(a, *spot)]
                for b in range(rhs_count):
                    moved = moved + coef(0, b, a) * directions[b]
                left = left - summed_slots(
                    [coef(0, natural[b], a) * image[b] for b in range(rhs_count)], rhs
                )
                sol_out[(a, *spot)] = moved
                res_out[(a, *spot)] = left
                for b in range(rhs_count):
                    left = left + coef(1, b, a) * directions[b]
                dir_out[(a, *spot)] = left
        return carry

    lax.fori_loop(0, rows // SUBLANES, one_group, 0)


def update(order, sums, solution, residual, direction, images):
    rhs_count, weeks, rows, lon = direction.shape
    half = rows // 2

    def field(rhs):
        return pl.BlockSpec((rhs, 1, half, lon), lambda w, h, _: (0, w, h, 0))

    shape = jax.ShapeDtypeStruct(direction.shape, jnp.float32)
    return pl.pallas_call(
        update_kernel,
        grid_spec=pltpu.PrefetchScalarGridSpec(
            num_scalar_prefetch=1,
            grid=(weeks, 2),
            in_specs=[whole(sums.shape)]
            + [field(rhs_count)] * 3
            + [field(image.shape[0]) for image in images],
            out_specs=[field(rhs_count)] * 3,
            scratch_shapes=[pltpu.VMEM((2 * rhs_count**2 * SUBLANES, LANES), jnp.float32)],
        ),
        out_shape=[shape] * 3,
        compiler_params=params(10),
        cost_estimate=cost(6 * rhs_count * direction.size, 28 * direction.size),
        name="update",
    )(order, sums, solution, residual, direction, *images)


def crossed(value, axis, by):
    if by == 0:
        return value
    return lax.ppermute(value, axis, [(i, i ^ by) for i in range(lax.axis_size(axis))])


def far_first(size):
    return [1 << bit for bit in reversed(range(size.bit_length() - 1))]


def neighbours(value, axis):
    size = lax.axis_size(axis)
    before = lax.ppermute(value, axis, [(i, i + 1) for i in range(size - 1)])
    after = lax.ppermute(value, axis, [(i + 1, i) for i in range(size - 1)])
    return before, after


def summed_over(value, axis):
    size = lax.axis_size(axis)
    reach = 1
    before = value
    while reach < size:
        before = value
        value = value + crossed(value, axis, reach)
        reach *= 2
    return value, before


def lat_windows(lat_width, band, rows):
    decay = rows / 2.0
    total = lat_width.shape[0]
    offsets = jnp.abs(jnp.arange(-rows, rows + 1)).astype(jnp.float32)
    limits = lat_width.astype(jnp.float32)
    normal = jnp.sqrt(
        jnp.sum(
            jnp.where(
                offsets[None, :] <= limits[:, None], jnp.exp(-2.0 * offsets / decay)[None, :], 0.0
            ),
            axis=1,
        )
    )
    padded_limits = jnp.pad(limits, (rows, rows), constant_values=-1.0)
    padded_normal = jnp.pad(normal, (rows, rows), constant_values=1.0)
    near_limits = lax.dynamic_slice_in_dim(padded_limits, band * rows, 3 * rows)
    near_normal = lax.dynamic_slice_in_dim(padded_normal, band * rows, 3 * rows)
    distance = jnp.abs(
        jnp.arange(rows)[:, None] + rows - jnp.arange(3 * rows)[None, :]
    ).astype(jnp.float32)
    fade = jnp.exp(-distance / decay)
    own_limits, own_normal = near_limits[rows : 2 * rows, None], near_normal[rows : 2 * rows, None]
    spread = jnp.where(distance <= own_limits, fade, 0.0) / own_normal
    pulled = jnp.where(distance <= near_limits[None, :], fade, 0.0) / near_normal[None, :]
    return spread, pulled


def shards(
    footprints,
    block_rows,
    block_cols,
    block_scale,
    lat_width,
    lon_width,
    obs_weight,
    solution,
    residual,
    direction,
):
    rhs_count, weeks, rows, lon = direction.shape
    blocks = footprints[0, 0]
    count, edge, _ = blocks.shape
    row_list, col_list = block_rows[0, 0], block_cols[0, 0]
    scales = jnp.exp2(-block_scale[0, 0].astype(jnp.float32))
    row_blocks = obs_weight.shape[0] // edge
    slots = lax.axis_size("obs")
    rhs = rhs_count // slots
    slab, band = lax.axis_index("obs"), lax.axis_index("lat")
    parts = lon // edge
    cols = weeks * rows * parts

    groups = chunk_of(rhs, BACK_GROUPS)
    each = rhs // groups
    order = (slab ^ jnp.arange(slots, dtype=jnp.int32)) * rhs
    own_width = lax.dynamic_slice_in_dim(lon_width, band * rows, rows)
    counts = jnp.broadcast_to(own_width[:, None] + 1, (rows, lon))

    line, part = col_list // parts, col_list % parts
    place = ((line // rows) * parts + part) * rows + line % rows
    places = jnp.stack([crossed(place, "obs", d) for d in range(slots)])

    lon_own, words = spread_lon(
        lax.dynamic_slice_in_dim(direction, slab * rhs, rhs, 0), counts
    )
    halo = neighbours(words, "lat")
    hot = (places[:, :, None] == jnp.arange(cols)[None, None, :]).astype(jnp.bfloat16)
    hot_turned = (jnp.arange(cols)[:, None] == places.reshape(1, -1)).astype(jnp.bfloat16)
    lat_spread, lat_pulled = lat_windows(lat_width, band, rows)

    picks = spread_lat(lon_own, *halo, lat_spread, hot)
    cells = [crossed(picks[d], "obs", d) for d in range(slots)]
    near_blocks = preload(blocks, picks[0])
    sums, partial = summed_over(forward(row_list, scales, near_blocks, cells, row_blocks), "lat")
    near_blocks = preload(blocks, partial)
    weighted = sums.reshape(row_blocks, slots * rhs, edge) * obs_weight.reshape(row_blocks, 1, edge)
    terms = adjoint_terms(
        row_list, scales, near_blocks, weighted.reshape(-1, edge), slots * groups, each
    )
    sent = [[crossed(terms[d * groups + g], "obs", d) for d in range(slots)] for g in range(groups)]
    own = []
    for group in range(groups):
        field, words = gather_cells(hot_turned, sent[group], each, weeks, rows, lon)
        own.append(pull_back(field, *neighbours(words, "lat"), lat_pulled, counts))

    starts = (order[:, None] + jnp.arange(groups, dtype=jnp.int32) * each).reshape(-1)
    products = jnp.zeros((SUBLANES, 4 * rhs_count**2), jnp.float32)
    done, places, found = {}, (), []

    def add_products(words, slot, group):
        nonlocal products, places
        places += (slot * groups + group,)
        new, products = grams(
            starts, places, products, residual, direction, [words], found, slot == group == 0
        )
        found.extend(new)
        done[slot, group] = new[0]

    arrived = [{0: words} for words in own]
    for group in range(groups):
        for reach in far_first(slots):
            arrived[group][reach] = crossed(own[group], "obs", reach)
        add_products(own[group], 0, group)
    for group in range(groups):
        near = [bits for bits in arrived[group] if bits == 1]
        for bits in near:
            add_products(arrived[group][bits], bits, group)
    for reach in far_first(slots)[1:]:
        for group in range(groups):
            for bits in [bits for bits in arrived[group] if bits > reach and not bits % (2 * reach)]:
                words, _ = lax.optimization_barrier((arrived[group][bits], done[1, group]))
                arrived[group][bits | reach] = crossed(words, "obs", reach)
    for bits in range(2, slots):
        for group in range(groups):
            add_products(arrived[group][bits], bits, group)
    products, _ = summed_over(products, "lat")
    images = [done[slot, group] for slot in range(slots) for group in range(groups)]
    return tuple(update(starts, products, solution, residual, direction, images))


def solution(mesh):
    return jax.shard_map(
        shards,
        mesh=mesh,
        in_specs=(
            P("obs", "lat", None, None, None),
            P("obs", "lat", None),
            P("obs", "lat", None),
            P("obs", "lat", None),
            P(),
            P(),
            P("obs"),
            P(None, None, "lat", None),
            P(None, None, "lat", None),
            P(None, None, "lat", None),
        ),
        out_specs=(
            P(None, None, "lat", None),
            P(None, None, "lat", None),
            P(None, None, "lat", None),
        ),
        check_vma=False,
    )
```

```python
import functools
import math

import jax
import jax.numpy as jnp
from jax import lax
from jax.experimental import pallas as pl
from jax.experimental.pallas import tpu as pltpu
from jax.sharding import PartitionSpec as P

LANES = 128
CHUNK = 96
COPIES = 12
STREAM_MIB = 40
KEPT, KEPT_OF = 1, 2
BACK_GROUPS = 2
SUBLANES = 8
MIB = 1024 * 1024
HIGHEST = lax.Precision.HIGHEST


def params(mib):
    return pltpu.CompilerParams(vmem_limit_bytes=mib * MIB)


def cost(flops, nbytes):
    return pl.CostEstimate(flops=int(flops), bytes_accessed=int(nbytes), transcendentals=0)


def whole(shape):
    return pl.BlockSpec(shape, lambda *_: (0,) * len(shape), pipeline_mode=pl.Buffered(1))


def in_vmem(count):
    return [pl.BlockSpec(memory_space=pltpu.VMEM)] * count


def pow2(exponent):
    size = jnp.abs(exponent)
    up = jnp.ones(exponent.shape, jnp.float32)
    down = up
    for bit in range(7):
        on = ((size >> bit) & 1) == 1
        up = up * jnp.where(on, 2.0 ** (2**bit), 1.0)
        down = down * jnp.where(on, 2.0 ** -(2**bit), 1.0)
    return jnp.where(exponent < 0, down, up)


def exponent_of(peak):
    logs = jnp.log(jnp.maximum(peak, 1e-28)) * (1.0 / math.log(2.0))
    return jnp.ceil(logs + 1e-3).astype(jnp.int32)


def to_int(values, factor):
    return jnp.clip(jnp.round(values * factor), -32767.0, 32767.0).astype(jnp.int32)


def pack(high, low):
    return (high << 16) | (low & 0xFFFF)


def high_of(word):
    return word >> 16


def low_of(word):
    return (word << 16) >> 16


def words_of(rhs, weeks, rows):
    return rhs * weeks * rows // 2 + SUBLANES


def exponent_rows(peaks):
    line = lax.broadcasted_iota(jnp.int32, (SUBLANES, peaks[0].shape[1]), 0)
    found = jnp.zeros(line.shape, jnp.int32)
    for k, peak in enumerate(peaks):
        found = jnp.where(line == k, exponent_of(jnp.max(peak, axis=0, keepdims=True)), found)
    return found


def pack_field(field_ref, word_ref, peaks):
    rhs, weeks, rows, lon = field_ref.shape
    half = rows // 2
    exponents = exponent_rows(peaks)
    word_ref[rhs * weeks * half :, :] = exponents
    for k in range(rhs):
        factor = pow2(15 - jnp.broadcast_to(exponents[k : k + 1], (SUBLANES, lon)))

        def one_week(week, carry):
            for start in range(0, half, SUBLANES):
                high = to_int(field_ref[k, week, start : start + SUBLANES, :], factor)
                low = to_int(field_ref[k, week, half + start : half + start + SUBLANES, :], factor)
                at = pl.multiple_of((k * weeks + week) * half + start, SUBLANES)
                word_ref[pl.ds(at, SUBLANES), :] = pack(high, low)
            return carry

        lax.fori_loop(0, weeks, one_week, 0)


def word_scale(word_ref, body, k):
    row = word_ref[body + k : body + k + 1, :] - 15
    return pow2(jnp.broadcast_to(row, (SUBLANES, row.shape[1])))


def lon_setup(lon):
    return lon / 32.0, (lon // 8 + 1).bit_length()


def lon_rows(rows, count, norm, lon):
    decay, bits = lon_setup(lon)
    fields = rows.shape[0] // SUBLANES
    count = jnp.concatenate([count] * fields, axis=0)
    windows = [rows, rows]
    taken = [jnp.zeros_like(rows)] * 2
    for bit in range(bits):
        reach = 2**bit
        fade = math.exp(-reach / decay)
        chosen = ((count >> bit) & 1) == 1
        for side in range(2):
            shift = reach if side == 0 else lon - reach
            moved = windows[side]
            if bit:
                moved = moved + fade * pltpu.roll(taken[side], shift, 1)
            taken[side] = jnp.where(chosen, moved, taken[side])
            if bit + 1 < bits:
                windows[side] = windows[side] + fade * pltpu.roll(windows[side], shift, 1)
    return (taken[0] + taken[1] - rows) * jnp.concatenate([norm] * fields, axis=0)


def lon_norm(count, lon):
    decay, _ = lon_setup(lon)
    ratio = math.exp(-2.0 / decay)
    ends = jnp.exp(count.astype(jnp.float32) * (-2.0 / decay))
    return 1.0 / jnp.sqrt(1.0 + (2.0 / (1.0 - ratio)) * (ratio - ends))


def lon_field(source_ref, count_ref, out_ref):
    rhs, weeks, rows, lon = out_ref.shape

    def one_group(group, peaks):
        at = pl.multiple_of(group * SUBLANES, SUBLANES)
        count = count_ref[pl.ds(at, SUBLANES), :]
        norm = lon_norm(count, lon)
        fields = [source_ref[k, w, pl.ds(at, SUBLANES), :] for k in range(rhs) for w in range(weeks)]
        result = lon_rows(jnp.concatenate(fields, axis=0), count, norm, lon)
        peaks = list(peaks)
        for k in range(rhs):
            for w in range(weeks):
                start = (k * weeks + w) * SUBLANES
                part = result[start : start + SUBLANES]
                out_ref[k, w, pl.ds(at, SUBLANES), :] = part
                peaks[k] = jnp.maximum(peaks[k], jnp.abs(part))
        return tuple(peaks)

    zero = jnp.zeros((SUBLANES, lon), jnp.float32)
    return lax.fori_loop(0, rows // SUBLANES, one_group, (zero,) * rhs)


def spread_lon_kernel(field_ref, count_ref, out_ref, word_ref):
    pack_field(out_ref, word_ref, lon_field(field_ref, count_ref, out_ref))


def spread_lon(field, counts):
    rhs, weeks, rows, lon = field.shape
    return pl.pallas_call(
        spread_lon_kernel,
        in_specs=in_vmem(2),
        out_specs=in_vmem(2),
        out_shape=[
            jax.ShapeDtypeStruct(field.shape, jnp.float32),
            jax.ShapeDtypeStruct((words_of(rhs, weeks, rows), lon), jnp.int32),
        ],
        compiler_params=params(6),
        cost_estimate=cost(field.size * 100, field.size * 10),
        name="spread_lon",
    )(field, counts)


def lat_mix(weights_ref, window_ref, k, week, before_ref, own_ref, after_ref, scales):
    rhs, weeks, rows, lon = own_ref.shape
    half = rows // 2
    for base, ref, scale in ((0, before_ref, scales[0]), (2 * rows, after_ref, scales[1])):
        for start in range(0, half, SUBLANES):
            at = (k * weeks + week) * half + start
            word = ref[at : at + SUBLANES, :]
            window_ref[base + start : base + start + SUBLANES, :] = (
                high_of(word).astype(jnp.float32) * scale
            )
            window_ref[base + half + start : base + half + start + SUBLANES, :] = (
                low_of(word).astype(jnp.float32) * scale
            )
    window_ref[rows : 2 * rows, :] = own_ref[k, week]
    return jnp.dot(
        weights_ref[...],
        window_ref[...],
        precision=HIGHEST,
        preferred_element_type=jnp.float32,
    )


def spread_lat_kernel(slots, own_ref, before_ref, after_ref, weights_ref, hot_ref, *rest):
    picks, (window_ref, cells_ref) = rest[:slots], rest[slots:]
    rhs, weeks, rows, lon = own_ref.shape
    body = before_ref.shape[0] - SUBLANES
    parts = lon // LANES
    for k in range(rhs):
        scales = word_scale(before_ref, body, k), word_scale(after_ref, body, k)
        for week in range(weeks):
            mixed = lat_mix(
                weights_ref, window_ref, k, week, before_ref, own_ref, after_ref, scales
            )
            for part in range(parts):
                at = (week * parts + part) * rows
                cells_ref[at : at + rows, k * LANES : (k + 1) * LANES] = mixed[
                    :, part * LANES : (part + 1) * LANES
                ].astype(jnp.bfloat16)
    for slot in range(slots):
        found = jnp.dot(
            hot_ref[slot], cells_ref[...], preferred_element_type=jnp.float32
        ).astype(jnp.bfloat16)
        for k in range(rhs):
            picks[slot][k] = found[:, k * LANES : (k + 1) * LANES]


def spread_lat(own, before, after, weights, hot):
    rhs, weeks, rows, lon = own.shape
    slots, blocks, cols = hot.shape
    return pl.pallas_call(
        functools.partial(spread_lat_kernel, slots),
        in_specs=in_vmem(5),
        out_specs=in_vmem(slots),
        out_shape=[jax.ShapeDtypeStruct((rhs, blocks, LANES), jnp.bfloat16)] * slots,
        scratch_shapes=[
            pltpu.VMEM((3 * rows, lon), jnp.float32),
            pltpu.VMEM((cols, rhs * LANES), jnp.bfloat16),
        ],
        compiler_params=params(10),
        cost_estimate=cost(rhs * slots * blocks * cols * LANES * 2, rhs * weeks * rows * lon * 10),
        name="spread_lat",
    )(own, before, after, weights, hot)


def chunk_of(count, most):
    return max(size for size in range(1, most + 1) if count % size == 0)


def preload_kernel(first, after_ref, blocks_ref, out_ref, done):
    del after_ref
    parts = done.shape[0]
    size = out_ref.shape[0] // parts
    copies = [
        pltpu.make_async_copy(
            blocks_ref.at[pl.ds(first + part * size, size)],
            out_ref.at[pl.ds(part * size, size)],
            done.at[part],
        )
        for part in range(parts)
    ]
    for copy in copies:
        copy.start()
    for copy in copies:
        copy.wait()


def preload(blocks, first, count, after):
    parts = chunk_of(count, COPIES)
    shape = (count, *blocks.shape[1:])
    return pl.pallas_call(
        functools.partial(preload_kernel, first),
        in_specs=[pl.BlockSpec(memory_space=pl.ANY)] * 2,
        out_specs=pl.BlockSpec(memory_space=pltpu.VMEM),
        out_shape=jax.ShapeDtypeStruct(shape, blocks.dtype),
        scratch_shapes=[pltpu.SemaphoreType.DMA((parts,))],
        compiler_params=params(STREAM_MIB),
        cost_estimate=cost(0, count * blocks[0].size * 4),
        name="preload",
    )(after, blocks)


def forward_kernel(pieces, row_ref, scale_ref, *rest):
    pieces, picks, (out_ref, cells_ref) = rest[:pieces], rest[pieces:-2], rest[-2:]
    rhs, count, edge = picks[0].shape
    lines = len(picks) * rhs
    out_ref[...] = jnp.zeros_like(out_ref)
    for place, pick_ref in enumerate(picks):
        for k in range(rhs):
            cells_ref[pl.ds(place * rhs + k, count, stride=lines), :] = pick_ref[k].astype(
                jnp.float32
            )

    def one_chunk(piece_ref, first, chunk, step, carry):
        values = []
        for n in range(0, chunk, 2):
            index = step * chunk + n
            at = pl.multiple_of((first + index) * lines, 2 * lines)
            both = lax.dot_general(
                cells_ref[pl.ds(at, 2 * lines), :].astype(jnp.bfloat16),
                piece_ref[pl.ds(index, 2)].reshape(2 * edge, edge),
                (((1,), (1,)), ((), ())),
                preferred_element_type=jnp.float32,
            )
            values += [both[:lines, :edge], both[lines:, edge:]]
        for n in range(chunk):
            index = first + step * chunk + n
            at = pl.multiple_of(row_ref[index] * lines, lines)
            out_ref[pl.ds(at, lines), :] += values[n] * scale_ref[index]
        return carry

    over_chunks(pieces, one_chunk)


def over_chunks(pieces, one_chunk):
    first = 0
    for piece_ref in pieces:
        count = piece_ref.shape[0]
        chunk = 2 * chunk_of(count // 2, CHUNK // 2)
        lax.fori_loop(0, count // chunk, functools.partial(one_chunk, piece_ref, first, chunk), 0)
        first += count


def forward(row_list, scales, pieces, picks, row_blocks):
    rhs, count, edge = picks[0].shape
    lines = len(picks) * rhs
    return pl.pallas_call(
        functools.partial(forward_kernel, len(pieces)),
        in_specs=[pl.BlockSpec(memory_space=pltpu.SMEM)] * 2 + in_vmem(len(pieces) + len(picks)),
        out_specs=pl.BlockSpec(memory_space=pltpu.VMEM),
        out_shape=jax.ShapeDtypeStruct((row_blocks * lines, edge), jnp.float32),
        scratch_shapes=[pltpu.VMEM((count * lines, edge), jnp.float32)],
        compiler_params=params(15),
        cost_estimate=cost(count * edge**2 * 2 * lines, count * edge**2 * 2),
        name="forward",
    )(row_list, scales, *pieces, *picks)


def adjoint_kernel(pieces, rhs, row_ref, scale_ref, *rest):
    pieces, values_ref, outs, terms_ref = rest[:pieces], rest[pieces], rest[pieces + 1 : -1], rest[-1]
    lines = len(outs) * rhs
    edge = values_ref.shape[1]
    count = terms_ref.shape[0] // lines

    def one_chunk(piece_ref, first, chunk, step, carry):
        for n in range(0, chunk, 2):
            here = step * chunk + n
            index = first + here
            pulled = [
                values_ref[pl.ds(pl.multiple_of(row_ref[index + q] * lines, lines), lines), :]
                for q in range(2)
            ]
            both = jnp.dot(
                jnp.concatenate(pulled, axis=0).astype(jnp.bfloat16),
                jnp.concatenate([piece_ref[here + q] for q in range(2)], axis=1),
                preferred_element_type=jnp.float32,
            )
            for q in range(2):
                to = pl.multiple_of((index + q) * lines, lines)
                part = both[q * lines : (q + 1) * lines, q * edge : (q + 1) * edge]
                terms_ref[pl.ds(to, lines), :] = part * scale_ref[index + q]
        return carry

    over_chunks(pieces, one_chunk)
    half = count // 2
    for place, out_ref in enumerate(outs):
        terms = [terms_ref[pl.ds(place * rhs + k, count, stride=lines), :] for k in range(rhs)]
        exponents = exponent_rows([jnp.abs(term) for term in terms])
        out_ref[rhs * half :, :] = exponents
        for k in range(rhs):
            number = to_int(terms[k], pow2(15 - exponents[k : k + 1]))
            out_ref[k * half : (k + 1) * half, :] = pack(number[:half], number[half:])


def adjoint_terms(row_list, scales, pieces, values, outs, rhs):
    count = sum(piece.shape[0] for piece in pieces)
    edge = values.shape[1]
    lines = outs * rhs
    words = rhs * count // 2 + SUBLANES
    return pl.pallas_call(
        functools.partial(adjoint_kernel, len(pieces), rhs),
        in_specs=[pl.BlockSpec(memory_space=pltpu.SMEM)] * 2 + in_vmem(len(pieces) + 1),
        out_specs=in_vmem(outs),
        out_shape=[jax.ShapeDtypeStruct((words, edge), jnp.int32)] * outs,
        scratch_shapes=[pltpu.VMEM((count * lines, edge), jnp.float32)],
        compiler_params=params(15),
        cost_estimate=cost(count * edge**2 * 2 * lines, count * edge**2 * 2),
        name="adjoint",
    )(row_list, scales, *pieces, values)


def gather_cells_kernel(slots, hot_ref, *rest):
    terms, (field_ref, word_ref, split_ref) = rest[:slots], rest[slots:]
    rhs, weeks, rows, lon = field_ref.shape
    count = hot_ref.shape[1] // slots
    half = count // 2
    wide = rhs * LANES
    for slot in range(slots):
        for k in range(rhs):
            scale = word_scale(terms[slot], rhs * half, k)[:1]
            word = terms[slot][k * half : (k + 1) * half, :]
            for base, number in ((0, high_of(word)), (half, low_of(word))):
                coarse = (number + 128) >> 8
                fine = number - (coarse << 8)
                at = slot * count + base
                split_ref[at : at + half, k * LANES : (k + 1) * LANES] = (
                    (coarse << 8).astype(jnp.float32) * scale
                ).astype(jnp.bfloat16)
                split_ref[at : at + half, wide + k * LANES : wide + (k + 1) * LANES] = (
                    fine.astype(jnp.float32) * scale
                ).astype(jnp.bfloat16)
    peaks = [jnp.zeros((SUBLANES, lon), jnp.float32)] * rhs
    parts = lon // LANES
    for week in range(weeks):
        at = week * parts * rows
        both = jnp.dot(
            hot_ref[at : at + parts * rows, :],
            split_ref[...],
            preferred_element_type=jnp.float32,
        )
        cells = both[:, :wide] + both[:, wide:]
        for k in range(rhs):
            for part in range(parts):
                field_ref[k, week, :, part * LANES : (part + 1) * LANES] = cells[
                    part * rows : (part + 1) * rows, k * LANES : (k + 1) * LANES
                ]
            for start in range(0, rows, SUBLANES):
                peaks[k] = jnp.maximum(
                    peaks[k], jnp.abs(field_ref[k, week, start : start + SUBLANES, :])
                )
    pack_field(field_ref, word_ref, peaks)


def gather_cells(hot_turned, terms, rhs, weeks, rows, lon):
    slots = len(terms)
    return pl.pallas_call(
        functools.partial(gather_cells_kernel, slots),
        in_specs=in_vmem(1 + slots),
        out_specs=in_vmem(2),
        out_shape=[
            jax.ShapeDtypeStruct((rhs, weeks, rows, lon), jnp.float32),
            jax.ShapeDtypeStruct((words_of(rhs, weeks, rows), lon), jnp.int32),
        ],
        scratch_shapes=[pltpu.VMEM((hot_turned.shape[1], 2 * rhs * LANES), jnp.bfloat16)],
        compiler_params=params(12),
        cost_estimate=cost(rhs * hot_turned.size * 4 * LANES, rhs * weeks * rows * lon * 10),
        name="gather_cells",
    )(hot_turned, *terms)


def pull_back_kernel(
    own_ref, before_ref, after_ref, weights_ref, count_ref, word_ref, window_ref, field_ref
):
    rhs, weeks, rows, lon = own_ref.shape
    body = before_ref.shape[0] - SUBLANES
    for k in range(rhs):
        scales = word_scale(before_ref, body, k), word_scale(after_ref, body, k)
        for week in range(weeks):
            field_ref[k, week] = lat_mix(
                weights_ref, window_ref, k, week, before_ref, own_ref, after_ref, scales
            )
    pack_field(field_ref, word_ref, lon_field(field_ref, count_ref, field_ref))


def pull_back(own, before, after, weights, counts):
    rhs, weeks, rows, lon = own.shape
    return pl.pallas_call(
        pull_back_kernel,
        in_specs=in_vmem(5),
        out_specs=pl.BlockSpec(memory_space=pltpu.VMEM),
        out_shape=jax.ShapeDtypeStruct(before.shape, jnp.int32),
        scratch_shapes=[
            pltpu.VMEM((3 * rows, lon), jnp.float32),
            pltpu.VMEM((rhs, weeks, rows, lon), jnp.float32),
        ],
        compiler_params=params(8),
        cost_estimate=cost(rhs * weeks * rows * lon * 300, rhs * weeks * rows * lon * 10),
        name="pull_back",
    )(own, before, after, weights, counts)


def gram_kernel(with_old, places, count, rhs, order_ref, sums_before, residual_ref, direction_ref, *rest):
    words, rest = rest[:count], rest[count:]
    news, gram_ref, sums_ref = rest[-count - 2 : -2], rest[-2], rest[-1]
    olds = rest[: -count - 2]
    rhs_count, weeks, rows, lon = direction_ref.shape
    half = rows // 2
    body = words[0].shape[0] - SUBLANES
    old_places, new_places = places[: len(olds)], places[len(olds) :]
    for word_ref, new_ref, place in zip(words, news, new_places):
        for k in range(rhs):
            index = order_ref[place] + k
            scale = word_scale(word_ref, body, k)

            def one_week(week, carry):
                for start in range(0, half, SUBLANES):
                    at = pl.multiple_of((k * weeks + week) * half + start, SUBLANES)
                    word = word_ref[pl.ds(at, SUBLANES), :]
                    for base, number in ((start, high_of(word)), (half + start, low_of(word))):
                        new_ref[k, week, base : base + SUBLANES, :] = (
                            direction_ref[index, week, base : base + SUBLANES, :]
                            + number.astype(jnp.float32) * scale
                        )
                return carry

            lax.fori_loop(0, weeks, one_week, 0)

    sums_ref[...] = jnp.zeros_like(sums_ref)
    row_groups = rows // SUBLANES

    def tile(blocks):
        def one_week(week, sums):
            sums = list(sums)
            for row in range(0, rows, SUBLANES):
                for lane in range(0, lon, LANES):
                    spot = (week, slice(row, row + SUBLANES), slice(lane, lane + LANES))
                    place = 0
                    for _, lefts, rights, _ in blocks:
                        right = [ref[(k, *spot)] for ref, k, _ in rights]
                        for ref, k, _ in lefts:
                            left = ref[(k, *spot)]
                            for b in range(len(rights)):
                                sums[place] = sums[place] + left * right[b]
                                place += 1
            return tuple(sums)

        zero = jnp.zeros((SUBLANES, LANES), jnp.float32)
        total = sum(len(lefts) * len(rights) for _, lefts, rights, _ in blocks)
        sums = list(lax.fori_loop(0, weeks, one_week, (zero,) * total))
        for index, lefts, rights, mirror in blocks:
            for _, _, row in lefts:
                for _, _, column in rights:
                    lanes = jnp.sum(sums.pop(0), axis=0, keepdims=True)
                    for row_at, column_at in ((row, column), (column, row))[: 1 + mirror]:
                        at = (index * rhs_count + row_at) * rhs_count + column_at
                        sums_ref[pl.ds(at, 1), :] = lanes

    def listed(refs, places):
        return [
            (ref, k, order_ref[place] + k) for ref, place in zip(refs, places) for k in range(rhs)
        ]

    residuals = [(residual_ref, k, k) for k in range(rhs_count)]
    directions = [(direction_ref, k, k) for k in range(rhs_count)]
    images = listed(news, new_places)
    if with_old:
        for a in range(rhs_count):
            tile([(0, residuals[a : a + 1], residuals[a:], True)])
    for b in range(0, len(images), 2):
        right = images[b : b + 2]
        left = images[: b + len(right)] + listed(olds, old_places)
        tile([(1, directions, right, False), (2, residuals, right, False), (3, left, right, True)])

    gram_ref[...] = sums_before[...] + lax.dot_general(
        jnp.ones((SUBLANES, LANES), jnp.float32),
        sums_ref[...],
        (((1,), (1,)), ((), ())),
        precision=HIGHEST,
        preferred_element_type=jnp.float32,
    )


def grams(order, places, sums, residual, direction, words, olds, with_old):
    rhs_count, weeks, rows, lon = direction.shape
    total = 4 * rhs_count**2
    rhs = (words[0].shape[0] - SUBLANES) * 2 // (weeks * rows)
    count = len(words)
    found = pl.pallas_call(
        functools.partial(gram_kernel, with_old, places, count, rhs),
        in_specs=[pl.BlockSpec(memory_space=pltpu.SMEM)] + in_vmem(3 + count + len(olds)),
        out_specs=in_vmem(count + 1),
        out_shape=[jax.ShapeDtypeStruct((rhs, weeks, rows, lon), jnp.float32)] * count
        + [jax.ShapeDtypeStruct((SUBLANES, total), jnp.float32)],
        scratch_shapes=[pltpu.VMEM((total, LANES), jnp.float32)],
        compiler_params=params(14),
        cost_estimate=cost(8 * rhs_count * direction.size, 16 * direction.size),
        name="grams",
    )(order, sums, residual, direction, *words, *olds)
    return list(found[:-1]), found[-1]


def small_product(left, right):
    total = jnp.zeros((SUBLANES, LANES), jnp.float32)
    for j in range(SUBLANES):
        column = jnp.broadcast_to(left[:, j : j + 1], (SUBLANES, LANES))
        total = total + column * jnp.broadcast_to(right[j : j + 1, :], (SUBLANES, LANES))
    return total


def small_transpose(value):
    rest = jnp.zeros((LANES - SUBLANES, LANES), jnp.float32)
    return jnp.concatenate([value, rest], axis=0).T[:SUBLANES]


def small_solves(systems):
    line = lax.broadcasted_iota(jnp.int32, (SUBLANES, LANES), 0)
    lane = lax.broadcasted_iota(jnp.int32, (SUBLANES, LANES), 1)
    states = [matrix + pltpu.roll(right, SUBLANES, 1) for matrix, right in systems]
    for j in range(SUBLANES):
        for index, both in enumerate(states):
            column = jnp.broadcast_to(both[:, j : j + 1], (SUBLANES, LANES))
            pivot = jnp.broadcast_to(both[j : j + 1, :], (SUBLANES, LANES))
            scaled = pivot / jnp.broadcast_to(both[j : j + 1, j : j + 1], (SUBLANES, LANES))
            states[index] = jnp.where(line == j, scaled, both - column * scaled)
    return [
        jnp.where(lane < SUBLANES, pltpu.roll(both, LANES - SUBLANES, 1), 0.0) for both in states
    ]


def solve_steps(sums_ref, coef_ref):
    total = sums_ref.shape[1]
    size = SUBLANES
    place = lax.broadcasted_iota(jnp.int32, (size, total), 1)
    line = lax.broadcasted_iota(jnp.int32, (size, total), 0)
    spot = lax.broadcasted_iota(jnp.int32, (total, LANES), 0)
    lane = lax.broadcasted_iota(jnp.int32, (total, LANES), 1)
    to_column = jnp.where(spot % size == lane, 1.0, 0.0)
    sums = sums_ref[...]

    def matrix(index):
        rows = jnp.where(place // size == index * size + line, sums, 0.0)
        return jnp.dot(rows, to_column, precision=HIGHEST, preferred_element_type=jnp.float32)

    gram_old, curvature, mixed, gram_image = [matrix(index) for index in range(4)]
    curvature = 0.5 * (curvature + small_transpose(curvature))
    diagonal = lax.broadcasted_iota(jnp.int32, (size, LANES), 0)
    identity = jnp.where(diagonal == lax.broadcasted_iota(jnp.int32, (size, LANES), 1), 1.0, 0.0)
    step, old_inverse = small_solves([(curvature, gram_old), (gram_old, identity)])
    cross = small_product(mixed, step)
    both = small_product(small_transpose(step), small_product(gram_image, step))
    gram_new = gram_old - cross - small_transpose(cross) + both
    turn = small_product(old_inverse, gram_new)
    for index, matrix in enumerate((step, turn)):
        for b in range(size):
            for a in range(size):
                at = ((index * size + b) * size + a) * SUBLANES
                coef_ref[at : at + SUBLANES, :] = jnp.broadcast_to(
                    matrix[b : b + 1, a : a + 1], (SUBLANES, LANES)
                )


def summed_slots(terms, rhs):
    parts = [
        functools.reduce(lambda left, right: left + right, terms[at : at + rhs])
        for at in range(0, len(terms), rhs)
    ]
    while len(parts) > 1:
        parts = [left + right for left, right in zip(parts[::2], parts[1::2])]
    return parts[0]


def update_kernel(
    order_ref, sums_ref, solution_ref, residual_ref, direction_ref, *rest
):
    images, (sol_out, res_out, dir_out, coef_ref) = rest[:-4], rest[-4:]
    rhs_count, _, rows, lon = direction_ref.shape
    rhs = images[0].shape[0]

    @pl.when((pl.program_id(0) == 0) & (pl.program_id(1) == 0))
    def _():
        solve_steps(sums_ref, coef_ref)

    def coef(index, b, a):
        at = ((index * rhs_count + b) * rhs_count + a) * SUBLANES
        return coef_ref[pl.ds(pl.multiple_of(at, SUBLANES), SUBLANES), :]

    natural = [order_ref[slot] + k for slot in range(len(images)) for k in range(rhs)]

    def one_group(group, carry):
        at = pl.multiple_of(group * SUBLANES, SUBLANES)
        for lane in range(0, lon, LANES):
            spot = (0, pl.ds(at, SUBLANES), slice(lane, lane + LANES))
            directions = [direction_ref[(b, *spot)] for b in range(rhs_count)]
            image = [ref[(k, *spot)] for ref in images for k in range(rhs)]
            for a in range(rhs_count):
                moved = solution_ref[(a, *spot)]
                left = residual_ref[(a, *spot)]
                for b in range(rhs_count):
                    moved = moved + coef(0, b, a) * directions[b]
                left = left - summed_slots(
                    [coef(0, natural[b], a) * image[b] for b in range(rhs_count)], rhs
                )
                sol_out[(a, *spot)] = moved
                res_out[(a, *spot)] = left
                for b in range(rhs_count):
                    left = left + coef(1, b, a) * directions[b]
                dir_out[(a, *spot)] = left
        return carry

    lax.fori_loop(0, rows // SUBLANES, one_group, 0)


def update(order, sums, solution, residual, direction, images):
    rhs_count, weeks, rows, lon = direction.shape
    half = rows // 2

    def field(rhs):
        return pl.BlockSpec((rhs, 1, half, lon), lambda w, h, _: (0, w, h, 0))

    shape = jax.ShapeDtypeStruct(direction.shape, jnp.float32)
    return pl.pallas_call(
        update_kernel,
        grid_spec=pltpu.PrefetchScalarGridSpec(
            num_scalar_prefetch=1,
            grid=(weeks, 2),
            in_specs=[whole(sums.shape)]
            + [field(rhs_count)] * 3
            + [field(image.shape[0]) for image in images],
            out_specs=[field(rhs_count)] * 3,
            scratch_shapes=[pltpu.VMEM((2 * rhs_count**2 * SUBLANES, LANES), jnp.float32)],
        ),
        out_shape=[shape] * 3,
        compiler_params=params(10),
        cost_estimate=cost(6 * rhs_count * direction.size, 28 * direction.size),
        name="update",
    )(order, sums, solution, residual, direction, *images)


def crossed(value, axis, by):
    if by == 0:
        return value
    return lax.ppermute(value, axis, [(i, i ^ by) for i in range(lax.axis_size(axis))])


def far_first(size):
    return [1 << bit for bit in reversed(range(size.bit_length() - 1))]


def neighbours(value, axis):
    size = lax.axis_size(axis)
    before = lax.ppermute(value, axis, [(i, i + 1) for i in range(size - 1)])
    after = lax.ppermute(value, axis, [(i + 1, i) for i in range(size - 1)])
    return before, after


def summed_over(value, axis):
    size = lax.axis_size(axis)
    reach = 1
    before = value
    while reach < size:
        before = value
        value = value + crossed(value, axis, reach)
        reach *= 2
    return value, before


def lat_windows(lat_width, band, rows):
    decay = rows / 2.0
    total = lat_width.shape[0]
    offsets = jnp.abs(jnp.arange(-rows, rows + 1)).astype(jnp.float32)
    limits = lat_width.astype(jnp.float32)
    normal = jnp.sqrt(
        jnp.sum(
            jnp.where(
                offsets[None, :] <= limits[:, None], jnp.exp(-2.0 * offsets / decay)[None, :], 0.0
            ),
            axis=1,
        )
    )
    padded_limits = jnp.pad(limits, (rows, rows), constant_values=-1.0)
    padded_normal = jnp.pad(normal, (rows, rows), constant_values=1.0)
    near_limits = lax.dynamic_slice_in_dim(padded_limits, band * rows, 3 * rows)
    near_normal = lax.dynamic_slice_in_dim(padded_normal, band * rows, 3 * rows)
    distance = jnp.abs(
        jnp.arange(rows)[:, None] + rows - jnp.arange(3 * rows)[None, :]
    ).astype(jnp.float32)
    fade = jnp.exp(-distance / decay)
    own_limits, own_normal = near_limits[rows : 2 * rows, None], near_normal[rows : 2 * rows, None]
    spread = jnp.where(distance <= own_limits, fade, 0.0) / own_normal
    pulled = jnp.where(distance <= near_limits[None, :], fade, 0.0) / near_normal[None, :]
    return spread, pulled


def shards(
    footprints,
    block_rows,
    block_cols,
    block_scale,
    lat_width,
    lon_width,
    obs_weight,
    solution,
    residual,
    direction,
):
    rhs_count, weeks, rows, lon = direction.shape
    blocks = footprints[0, 0]
    count, edge, _ = blocks.shape
    row_list = block_rows[0, 0]
    scales = jnp.exp2(-block_scale[0, 0].astype(jnp.float32))
    row_blocks = obs_weight.shape[0] // edge
    slots = lax.axis_size("obs")
    rhs = rhs_count // slots
    slab, band = lax.axis_index("obs"), lax.axis_index("lat")
    parts = lon // edge
    cols = weeks * rows * parts

    groups = chunk_of(rhs, BACK_GROUPS)
    each = rhs // groups
    order = (slab ^ jnp.arange(slots, dtype=jnp.int32)) * rhs
    own_width = lax.dynamic_slice_in_dim(lon_width, band * rows, rows)
    counts = jnp.broadcast_to(own_width[:, None] + 1, (rows, lon))

    lists = jnp.concatenate([crossed(block_cols, "obs", d) for d in range(slots)], axis=0)[:, 0]
    line, part = lists // parts, lists % parts
    places = ((line // rows) * parts + part) * rows + line % rows

    lon_own, words = spread_lon(
        lax.dynamic_slice_in_dim(direction, slab * rhs, rhs, 0), counts
    )
    halo = neighbours(words, "lat")
    hot = (places[:, :, None] == jnp.arange(cols)[None, None, :]).astype(jnp.bfloat16)
    hot_turned = (jnp.arange(cols)[:, None] == places.reshape(1, -1)).astype(jnp.bfloat16)
    lat_spread, lat_pulled = lat_windows(lat_width, band, rows)

    picks = spread_lat(lon_own, *halo, lat_spread, hot)
    cells = [crossed(picks[d], "obs", d) for d in range(slots)]
    kept = count // KEPT_OF * KEPT if count % KEPT_OF == 0 else 0
    stays = [preload(blocks, 0, kept, picks[0])] if kept else []
    near = preload(blocks, kept, count - kept, picks[0])
    sums, partial = summed_over(
        forward(row_list, scales, [*stays, near], cells, row_blocks), "lat"
    )
    near = preload(blocks, kept, count - kept, partial)
    weighted = sums.reshape(row_blocks, slots * rhs, edge) * obs_weight.reshape(row_blocks, 1, edge)
    terms = adjoint_terms(
        row_list, scales, [*stays, near], weighted.reshape(-1, edge), slots * groups, each
    )
    sent = [[crossed(terms[d * groups + g], "obs", d) for d in range(slots)] for g in range(groups)]
    own = []
    for group in range(groups):
        field, words = gather_cells(hot_turned, sent[group], each, weeks, rows, lon)
        own.append(pull_back(field, *neighbours(words, "lat"), lat_pulled, counts))

    starts = (order[:, None] + jnp.arange(groups, dtype=jnp.int32) * each).reshape(-1)
    products = jnp.zeros((SUBLANES, 4 * rhs_count**2), jnp.float32)
    done, places = {}, ()

    def add_products(slot):
        nonlocal products, places
        words = [arrived[group][slot] for group in range(groups)]
        places += tuple(slot * groups + group for group in range(groups))
        olds = [image for images in done.values() for image in images]
        done[slot], products = grams(
            starts, places, products, residual, direction, words, olds, slot == 0
        )

    arrived = [{0: words} for words in own]
    for group in range(groups):
        for reach in far_first(slots):
            arrived[group][reach] = crossed(own[group], "obs", reach)
    add_products(0)
    for reach in far_first(slots)[1:]:
        for group in range(groups):
            for bits in [bits for bits in arrived[group] if bits > reach and not bits % (2 * reach)]:
                words = arrived[group][bits]
                if group == groups - 1:
                    words, _ = lax.optimization_barrier((words, done[0][0]))
                arrived[group][bits | reach] = crossed(words, "obs", reach)
    for slot in range(1, slots):
        add_products(slot)
    products, _ = summed_over(products, "lat")
    images = [image for slot in range(slots) for image in done[slot]]
    return tuple(update(starts, products, solution, residual, direction, images))


def solution(mesh):
    return jax.shard_map(
        shards,
        mesh=mesh,
        in_specs=(
            P("obs", "lat", None, None, None),
            P("obs", "lat", None),
            P("obs", "lat", None),
            P("obs", "lat", None),
            P(),
            P(),
            P("obs"),
            P(None, None, "lat", None),
            P(None, None, "lat", None),
            P(None, None, "lat", None),
        ),
        out_specs=(
            P(None, None, "lat", None),
            P(None, None, "lat", None),
            P(None, None, "lat", None),
        ),
        check_vma=False,
    )
```

```python
import functools
import math

import jax
import jax.numpy as jnp
from jax import lax
from jax.experimental import pallas as pl
from jax.experimental.pallas import tpu as pltpu
from jax.sharding import PartitionSpec as P

LANES = 128
CHUNK = 96
COPIES = 12
STREAM_MIB = 40
KEPT, KEPT_OF = 1, 2
BACK_GROUPS = 2
SUBLANES = 8
MIB = 1024 * 1024
HIGHEST = lax.Precision.HIGHEST


def params(mib):
    return pltpu.CompilerParams(vmem_limit_bytes=mib * MIB)


def cost(flops, nbytes):
    return pl.CostEstimate(flops=int(flops), bytes_accessed=int(nbytes), transcendentals=0)


def whole(shape):
    return pl.BlockSpec(shape, lambda *_: (0,) * len(shape), pipeline_mode=pl.Buffered(1))


def in_vmem(count):
    return [pl.BlockSpec(memory_space=pltpu.VMEM)] * count


def pow2(exponent):
    size = jnp.abs(exponent)
    up = jnp.ones(exponent.shape, jnp.float32)
    down = up
    for bit in range(7):
        on = ((size >> bit) & 1) == 1
        up = up * jnp.where(on, 2.0 ** (2**bit), 1.0)
        down = down * jnp.where(on, 2.0 ** -(2**bit), 1.0)
    return jnp.where(exponent < 0, down, up)


def exponent_of(peak):
    logs = jnp.log(jnp.maximum(peak, 1e-28)) * (1.0 / math.log(2.0))
    return jnp.ceil(logs + 1e-3).astype(jnp.int32)


def to_int(values, factor):
    return jnp.clip(jnp.round(values * factor), -32767.0, 32767.0).astype(jnp.int32)


def pack(high, low):
    return (high << 16) | (low & 0xFFFF)


def high_of(word):
    return word >> 16


def low_of(word):
    return (word << 16) >> 16


def words_of(rhs, weeks, rows):
    return rhs * weeks * rows // 2 + SUBLANES


def exponent_rows(peaks):
    line = lax.broadcasted_iota(jnp.int32, (SUBLANES, peaks[0].shape[1]), 0)
    found = jnp.zeros(line.shape, jnp.int32)
    for k, peak in enumerate(peaks):
        found = jnp.where(line == k, exponent_of(jnp.max(peak, axis=0, keepdims=True)), found)
    return found


def pack_field(field_ref, word_ref, peaks):
    rhs, weeks, rows, lon = field_ref.shape
    half = rows // 2
    exponents = exponent_rows(peaks)
    word_ref[rhs * weeks * half :, :] = exponents
    for k in range(rhs):
        factor = pow2(15 - jnp.broadcast_to(exponents[k : k + 1], (SUBLANES, lon)))

        def one_week(week, carry):
            for start in range(0, half, SUBLANES):
                high = to_int(field_ref[k, week, start : start + SUBLANES, :], factor)
                low = to_int(field_ref[k, week, half + start : half + start + SUBLANES, :], factor)
                at = pl.multiple_of((k * weeks + week) * half + start, SUBLANES)
                word_ref[pl.ds(at, SUBLANES), :] = pack(high, low)
            return carry

        lax.fori_loop(0, weeks, one_week, 0)


def word_scale(word_ref, body, k):
    row = word_ref[body + k : body + k + 1, :] - 15
    return pow2(jnp.broadcast_to(row, (SUBLANES, row.shape[1])))


def lon_setup(lon):
    return lon / 32.0, (lon // 8 + 1).bit_length()


def lon_rows(rows, count, norm, lon):
    decay, bits = lon_setup(lon)
    fields = rows.shape[0] // SUBLANES
    count = jnp.concatenate([count] * fields, axis=0)
    windows = [rows, rows]
    taken = [jnp.zeros_like(rows)] * 2
    for bit in range(bits):
        reach = 2**bit
        fade = math.exp(-reach / decay)
        chosen = ((count >> bit) & 1) == 1
        for side in range(2):
            shift = reach if side == 0 else lon - reach
            moved = windows[side]
            if bit:
                moved = moved + fade * pltpu.roll(taken[side], shift, 1)
            taken[side] = jnp.where(chosen, moved, taken[side])
            if bit + 1 < bits:
                windows[side] = windows[side] + fade * pltpu.roll(windows[side], shift, 1)
    return (taken[0] + taken[1] - rows) * jnp.concatenate([norm] * fields, axis=0)


def lon_norm(count, lon):
    decay, _ = lon_setup(lon)
    ratio = math.exp(-2.0 / decay)
    ends = jnp.exp(count.astype(jnp.float32) * (-2.0 / decay))
    return 1.0 / jnp.sqrt(1.0 + (2.0 / (1.0 - ratio)) * (ratio - ends))


def lon_field(source_ref, count_ref, out_ref):
    rhs, weeks, rows, lon = out_ref.shape

    def one_group(group, peaks):
        at = pl.multiple_of(group * SUBLANES, SUBLANES)
        count = count_ref[pl.ds(at, SUBLANES), :]
        norm = lon_norm(count, lon)
        fields = [source_ref[k, w, pl.ds(at, SUBLANES), :] for k in range(rhs) for w in range(weeks)]
        result = lon_rows(jnp.concatenate(fields, axis=0), count, norm, lon)
        peaks = list(peaks)
        for k in range(rhs):
            for w in range(weeks):
                start = (k * weeks + w) * SUBLANES
                part = result[start : start + SUBLANES]
                out_ref[k, w, pl.ds(at, SUBLANES), :] = part
                peaks[k] = jnp.maximum(peaks[k], jnp.abs(part))
        return tuple(peaks)

    zero = jnp.zeros((SUBLANES, lon), jnp.float32)
    return lax.fori_loop(0, rows // SUBLANES, one_group, (zero,) * rhs)


def spread_lon_kernel(field_ref, count_ref, out_ref, word_ref):
    pack_field(out_ref, word_ref, lon_field(field_ref, count_ref, out_ref))


def spread_lon(field, counts):
    rhs, weeks, rows, lon = field.shape
    return pl.pallas_call(
        spread_lon_kernel,
        in_specs=in_vmem(2),
        out_specs=in_vmem(2),
        out_shape=[
            jax.ShapeDtypeStruct(field.shape, jnp.float32),
            jax.ShapeDtypeStruct((words_of(rhs, weeks, rows), lon), jnp.int32),
        ],
        compiler_params=params(6),
        cost_estimate=cost(field.size * 100, field.size * 10),
        name="spread_lon",
    )(field, counts)


def lat_mix(side_ref, weights_ref, window_ref, k, week, pair_ref, own_ref, cross_ref, scales):
    rhs, weeks, rows, lon = own_ref.shape
    half = rows // 2
    before = 2 * rows * (1 - side_ref[0])
    for base, ref, scale in (
        (before, pair_ref, scales[0]),
        (2 * rows - before, cross_ref, scales[1]),
    ):
        for start in range(0, half, SUBLANES):
            at = (k * weeks + week) * half + start
            word = ref[at : at + SUBLANES, :]
            for to, number in ((start, high_of(word)), (half + start, low_of(word))):
                to = pl.multiple_of(base + to, SUBLANES)
                window_ref[pl.ds(to, SUBLANES), :] = number.astype(jnp.float32) * scale
    window_ref[rows : 2 * rows, :] = own_ref[k, week]
    return jnp.dot(
        weights_ref[...],
        window_ref[...],
        precision=HIGHEST,
        preferred_element_type=jnp.float32,
    )


def spread_lat_kernel(slots, side_ref, own_ref, pair_ref, cross_ref, weights_ref, hot_ref, *rest):
    picks, (window_ref, cells_ref) = rest[:slots], rest[slots:]
    rhs, weeks, rows, lon = own_ref.shape
    body = pair_ref.shape[0] - SUBLANES
    parts = lon // LANES
    for k in range(rhs):
        scales = word_scale(pair_ref, body, k), word_scale(cross_ref, body, k)
        for week in range(weeks):
            mixed = lat_mix(
                side_ref, weights_ref, window_ref, k, week, pair_ref, own_ref, cross_ref, scales
            )
            for part in range(parts):
                at = (week * parts + part) * rows
                cells_ref[at : at + rows, k * LANES : (k + 1) * LANES] = mixed[
                    :, part * LANES : (part + 1) * LANES
                ].astype(jnp.bfloat16)
    for slot in range(slots):
        found = jnp.dot(
            hot_ref[slot], cells_ref[...], preferred_element_type=jnp.float32
        ).astype(jnp.bfloat16)
        for k in range(rhs):
            picks[slot][k] = found[:, k * LANES : (k + 1) * LANES]


def spread_lat(side, own, pair, cross, weights, hot):
    rhs, weeks, rows, lon = own.shape
    slots, blocks, cols = hot.shape
    return pl.pallas_call(
        functools.partial(spread_lat_kernel, slots),
        in_specs=[pl.BlockSpec(memory_space=pltpu.SMEM)] + in_vmem(5),
        out_specs=in_vmem(slots),
        out_shape=[jax.ShapeDtypeStruct((rhs, blocks, LANES), jnp.bfloat16)] * slots,
        scratch_shapes=[
            pltpu.VMEM((3 * rows, lon), jnp.float32),
            pltpu.VMEM((cols, rhs * LANES), jnp.bfloat16),
        ],
        compiler_params=params(10),
        cost_estimate=cost(rhs * slots * blocks * cols * LANES * 2, rhs * weeks * rows * lon * 10),
        name="spread_lat",
    )(side, own, pair, cross, weights, hot)


def chunk_of(count, most):
    return max(size for size in range(1, most + 1) if count % size == 0)


def preload_kernel(first, after_ref, blocks_ref, out_ref, done):
    del after_ref
    parts = done.shape[0]
    size = out_ref.shape[0] // parts
    copies = [
        pltpu.make_async_copy(
            blocks_ref.at[pl.ds(first + part * size, size)],
            out_ref.at[pl.ds(part * size, size)],
            done.at[part],
        )
        for part in range(parts)
    ]
    for copy in copies:
        copy.start()
    for copy in copies:
        copy.wait()


def preload(blocks, first, count, after):
    parts = chunk_of(count, COPIES)
    shape = (count, *blocks.shape[1:])
    return pl.pallas_call(
        functools.partial(preload_kernel, first),
        in_specs=[pl.BlockSpec(memory_space=pl.ANY)] * 2,
        out_specs=pl.BlockSpec(memory_space=pltpu.VMEM),
        out_shape=jax.ShapeDtypeStruct(shape, blocks.dtype),
        scratch_shapes=[pltpu.SemaphoreType.DMA((parts,))],
        compiler_params=params(STREAM_MIB),
        cost_estimate=cost(0, count * blocks[0].size * 4),
        name="preload",
    )(after, blocks)


def forward_kernel(pieces, row_ref, scale_ref, *rest):
    pieces, picks, (out_ref, cells_ref) = rest[:pieces], rest[pieces:-2], rest[-2:]
    rhs, count, edge = picks[0].shape
    lines = len(picks) * rhs
    out_ref[...] = jnp.zeros_like(out_ref)
    for place, pick_ref in enumerate(picks):
        for k in range(rhs):
            cells_ref[pl.ds(place * rhs + k, count, stride=lines), :] = pick_ref[k].astype(
                jnp.float32
            )

    def one_chunk(piece_ref, first, chunk, step, carry):
        values = []
        for n in range(0, chunk, 2):
            index = step * chunk + n
            at = pl.multiple_of((first + index) * lines, 2 * lines)
            both = lax.dot_general(
                cells_ref[pl.ds(at, 2 * lines), :].astype(jnp.bfloat16),
                piece_ref[pl.ds(index, 2)].reshape(2 * edge, edge),
                (((1,), (1,)), ((), ())),
                preferred_element_type=jnp.float32,
            )
            values += [both[:lines, :edge], both[lines:, edge:]]
        for n in range(chunk):
            index = first + step * chunk + n
            at = pl.multiple_of(row_ref[index] * lines, lines)
            out_ref[pl.ds(at, lines), :] += values[n] * scale_ref[index]
        return carry

    over_chunks(pieces, one_chunk)


def over_chunks(pieces, one_chunk):
    first = 0
    for piece_ref in pieces:
        count = piece_ref.shape[0]
        chunk = 2 * chunk_of(count // 2, CHUNK // 2)
        lax.fori_loop(0, count // chunk, functools.partial(one_chunk, piece_ref, first, chunk), 0)
        first += count


def forward(row_list, scales, pieces, picks, row_blocks):
    rhs, count, edge = picks[0].shape
    lines = len(picks) * rhs
    return pl.pallas_call(
        functools.partial(forward_kernel, len(pieces)),
        in_specs=[pl.BlockSpec(memory_space=pltpu.SMEM)] * 2 + in_vmem(len(pieces) + len(picks)),
        out_specs=pl.BlockSpec(memory_space=pltpu.VMEM),
        out_shape=jax.ShapeDtypeStruct((row_blocks * lines, edge), jnp.float32),
        scratch_shapes=[pltpu.VMEM((count * lines, edge), jnp.float32)],
        compiler_params=params(15),
        cost_estimate=cost(count * edge**2 * 2 * lines, count * edge**2 * 2),
        name="forward",
    )(row_list, scales, *pieces, *picks)


def adjoint_kernel(pieces, rhs, row_ref, scale_ref, *rest):
    pieces, values_ref, outs, terms_ref = rest[:pieces], rest[pieces], rest[pieces + 1 : -1], rest[-1]
    lines = len(outs) * rhs
    edge = values_ref.shape[1]
    count = terms_ref.shape[0] // lines

    def one_chunk(piece_ref, first, chunk, step, carry):
        for n in range(0, chunk, 2):
            here = step * chunk + n
            index = first + here
            pulled = [
                values_ref[pl.ds(pl.multiple_of(row_ref[index + q] * lines, lines), lines), :]
                for q in range(2)
            ]
            both = jnp.dot(
                jnp.concatenate(pulled, axis=0).astype(jnp.bfloat16),
                jnp.concatenate([piece_ref[here + q] for q in range(2)], axis=1),
                preferred_element_type=jnp.float32,
            )
            for q in range(2):
                to = pl.multiple_of((index + q) * lines, lines)
                part = both[q * lines : (q + 1) * lines, q * edge : (q + 1) * edge]
                terms_ref[pl.ds(to, lines), :] = part * scale_ref[index + q]
        return carry

    over_chunks(pieces, one_chunk)
    half = count // 2
    for place, out_ref in enumerate(outs):
        terms = [terms_ref[pl.ds(place * rhs + k, count, stride=lines), :] for k in range(rhs)]
        exponents = exponent_rows([jnp.abs(term) for term in terms])
        out_ref[rhs * half :, :] = exponents
        for k in range(rhs):
            number = to_int(terms[k], pow2(15 - exponents[k : k + 1]))
            out_ref[k * half : (k + 1) * half, :] = pack(number[:half], number[half:])


def adjoint_terms(row_list, scales, pieces, values, outs, rhs):
    count = sum(piece.shape[0] for piece in pieces)
    edge = values.shape[1]
    lines = outs * rhs
    words = rhs * count // 2 + SUBLANES
    return pl.pallas_call(
        functools.partial(adjoint_kernel, len(pieces), rhs),
        in_specs=[pl.BlockSpec(memory_space=pltpu.SMEM)] * 2 + in_vmem(len(pieces) + 1),
        out_specs=in_vmem(outs),
        out_shape=[jax.ShapeDtypeStruct((words, edge), jnp.int32)] * outs,
        scratch_shapes=[pltpu.VMEM((count * lines, edge), jnp.float32)],
        compiler_params=params(15),
        cost_estimate=cost(count * edge**2 * 2 * lines, count * edge**2 * 2),
        name="adjoint",
    )(row_list, scales, *pieces, values)


def gather_cells_kernel(slots, hot_ref, *rest):
    terms, (field_ref, word_ref, split_ref) = rest[:slots], rest[slots:]
    rhs, weeks, rows, lon = field_ref.shape
    count = hot_ref.shape[1] // slots
    half = count // 2
    wide = rhs * LANES
    for slot in range(slots):
        for k in range(rhs):
            scale = word_scale(terms[slot], rhs * half, k)[:1]
            word = terms[slot][k * half : (k + 1) * half, :]
            for base, number in ((0, high_of(word)), (half, low_of(word))):
                coarse = (number + 128) >> 8
                fine = number - (coarse << 8)
                at = slot * count + base
                split_ref[at : at + half, k * LANES : (k + 1) * LANES] = (
                    (coarse << 8).astype(jnp.float32) * scale
                ).astype(jnp.bfloat16)
                split_ref[at : at + half, wide + k * LANES : wide + (k + 1) * LANES] = (
                    fine.astype(jnp.float32) * scale
                ).astype(jnp.bfloat16)
    peaks = [jnp.zeros((SUBLANES, lon), jnp.float32)] * rhs
    parts = lon // LANES
    for week in range(weeks):
        at = week * parts * rows
        both = jnp.dot(
            hot_ref[at : at + parts * rows, :],
            split_ref[...],
            preferred_element_type=jnp.float32,
        )
        cells = both[:, :wide] + both[:, wide:]
        for k in range(rhs):
            for part in range(parts):
                field_ref[k, week, :, part * LANES : (part + 1) * LANES] = cells[
                    part * rows : (part + 1) * rows, k * LANES : (k + 1) * LANES
                ]
            for start in range(0, rows, SUBLANES):
                peaks[k] = jnp.maximum(
                    peaks[k], jnp.abs(field_ref[k, week, start : start + SUBLANES, :])
                )
    pack_field(field_ref, word_ref, peaks)


def gather_cells(hot_turned, terms, rhs, weeks, rows, lon):
    slots = len(terms)
    return pl.pallas_call(
        functools.partial(gather_cells_kernel, slots),
        in_specs=in_vmem(1 + slots),
        out_specs=in_vmem(2),
        out_shape=[
            jax.ShapeDtypeStruct((rhs, weeks, rows, lon), jnp.float32),
            jax.ShapeDtypeStruct((words_of(rhs, weeks, rows), lon), jnp.int32),
        ],
        scratch_shapes=[pltpu.VMEM((hot_turned.shape[1], 2 * rhs * LANES), jnp.bfloat16)],
        compiler_params=params(12),
        cost_estimate=cost(rhs * hot_turned.size * 4 * LANES, rhs * weeks * rows * lon * 10),
        name="gather_cells",
    )(hot_turned, *terms)


def pull_back_kernel(
    side_ref, own_ref, pair_ref, cross_ref, weights_ref, count_ref, word_ref, window_ref, field_ref
):
    rhs, weeks, rows, lon = own_ref.shape
    body = pair_ref.shape[0] - SUBLANES
    for k in range(rhs):
        scales = word_scale(pair_ref, body, k), word_scale(cross_ref, body, k)
        for week in range(weeks):
            field_ref[k, week] = lat_mix(
                side_ref, weights_ref, window_ref, k, week, pair_ref, own_ref, cross_ref, scales
            )
    pack_field(field_ref, word_ref, lon_field(field_ref, count_ref, field_ref))


def pull_back(side, own, pair, cross, weights, counts):
    rhs, weeks, rows, lon = own.shape
    return pl.pallas_call(
        pull_back_kernel,
        in_specs=[pl.BlockSpec(memory_space=pltpu.SMEM)] + in_vmem(5),
        out_specs=pl.BlockSpec(memory_space=pltpu.VMEM),
        out_shape=jax.ShapeDtypeStruct(pair.shape, jnp.int32),
        scratch_shapes=[
            pltpu.VMEM((3 * rows, lon), jnp.float32),
            pltpu.VMEM((rhs, weeks, rows, lon), jnp.float32),
        ],
        compiler_params=params(8),
        cost_estimate=cost(rhs * weeks * rows * lon * 300, rhs * weeks * rows * lon * 10),
        name="pull_back",
    )(side, own, pair, cross, weights, counts)


def gram_kernel(places, count, rhs, order_ref, sums_before, residual_ref, direction_ref, *rest):
    words, (image_ref, gram_ref, sums_ref) = rest[:count], rest[-3:]
    rhs_count, weeks, rows, lon = direction_ref.shape
    half = rows // 2
    body = words[0].shape[0] - SUBLANES
    old_places, new_places = places[:-count], places[-count:]
    for word_ref, place in zip(words, new_places):
        for k in range(rhs):
            index = order_ref[place] + k
            scale = word_scale(word_ref, body, k)

            def one_week(week, carry):
                for start in range(0, half, SUBLANES):
                    at = pl.multiple_of((k * weeks + week) * half + start, SUBLANES)
                    word = word_ref[pl.ds(at, SUBLANES), :]
                    for base, number in ((start, high_of(word)), (half + start, low_of(word))):
                        image_ref[index, week, base : base + SUBLANES, :] = (
                            direction_ref[index, week, base : base + SUBLANES, :]
                            + number.astype(jnp.float32) * scale
                        )
                return carry

            lax.fori_loop(0, weeks, one_week, 0)

    sums_ref[...] = jnp.zeros_like(sums_ref)
    row_groups = rows // SUBLANES

    def tile(blocks):
        def one_week(week, sums):
            sums = list(sums)
            for row in range(0, rows, SUBLANES):
                for lane in range(0, lon, LANES):
                    spot = (week, slice(row, row + SUBLANES), slice(lane, lane + LANES))
                    place = 0
                    for _, lefts, rights, _ in blocks:
                        right = [ref[(k, *spot)] for ref, k, _ in rights]
                        for ref, k, _ in lefts:
                            left = ref[(k, *spot)]
                            for b in range(len(rights)):
                                sums[place] = sums[place] + left * right[b]
                                place += 1
            return tuple(sums)

        zero = jnp.zeros((SUBLANES, LANES), jnp.float32)
        total = sum(len(lefts) * len(rights) for _, lefts, rights, _ in blocks)
        sums = list(lax.fori_loop(0, weeks, one_week, (zero,) * total))
        for index, lefts, rights, mirror in blocks:
            for _, _, row in lefts:
                for _, _, column in rights:
                    lanes = jnp.sum(sums.pop(0), axis=0, keepdims=True)
                    for row_at, column_at in ((row, column), (column, row))[: 1 + mirror]:
                        at = (index * rhs_count + row_at) * rhs_count + column_at
                        sums_ref[pl.ds(at, 1), :] = lanes

    def listed(places):
        found = [order_ref[place] + k for place in places for k in range(rhs)]
        return [(image_ref, index, index) for index in found]

    residuals = [(residual_ref, k, k) for k in range(rhs_count)]
    directions = [(direction_ref, k, k) for k in range(rhs_count)]
    images = listed(new_places)
    if not old_places:
        for a in range(rhs_count):
            tile([(0, residuals[a : a + 1], residuals[a:], True)])
    for b in range(0, len(images), 2):
        right = images[b : b + 2]
        left = images[: b + len(right)] + listed(old_places)
        tile([(1, directions, right, False), (2, residuals, right, False), (3, left, right, True)])

    gram_ref[...] = sums_before[...] + lax.dot_general(
        jnp.ones((SUBLANES, LANES), jnp.float32),
        sums_ref[...],
        (((1,), (1,)), ((), ())),
        precision=HIGHEST,
        preferred_element_type=jnp.float32,
    )


def grams(order, places, sums, residual, direction, words, images):
    rhs_count, weeks, rows, lon = direction.shape
    total = 4 * rhs_count**2
    rhs = (words[0].shape[0] - SUBLANES) * 2 // (weeks * rows)
    count = len(words)
    return pl.pallas_call(
        functools.partial(gram_kernel, places, count, rhs),
        in_specs=[pl.BlockSpec(memory_space=pltpu.SMEM)] + in_vmem(3 + count + len(images)),
        out_specs=in_vmem(2),
        out_shape=[
            jax.ShapeDtypeStruct(direction.shape, jnp.float32),
            jax.ShapeDtypeStruct((SUBLANES, total), jnp.float32),
        ],
        scratch_shapes=[pltpu.VMEM((total, LANES), jnp.float32)],
        input_output_aliases={4 + count: 0} if images else {},
        compiler_params=params(14),
        cost_estimate=cost(8 * rhs_count * direction.size, 16 * direction.size),
        name="grams",
    )(order, sums, residual, direction, *words, *images)


def small_product(left, right):
    total = jnp.zeros((SUBLANES, LANES), jnp.float32)
    for j in range(SUBLANES):
        column = jnp.broadcast_to(left[:, j : j + 1], (SUBLANES, LANES))
        total = total + column * jnp.broadcast_to(right[j : j + 1, :], (SUBLANES, LANES))
    return total


def small_transpose(value):
    rest = jnp.zeros((LANES - SUBLANES, LANES), jnp.float32)
    return jnp.concatenate([value, rest], axis=0).T[:SUBLANES]


def small_solves(systems):
    line = lax.broadcasted_iota(jnp.int32, (SUBLANES, LANES), 0)
    lane = lax.broadcasted_iota(jnp.int32, (SUBLANES, LANES), 1)
    states = [matrix + pltpu.roll(right, SUBLANES, 1) for matrix, right in systems]
    for j in range(SUBLANES):
        for index, both in enumerate(states):
            column = jnp.broadcast_to(both[:, j : j + 1], (SUBLANES, LANES))
            pivot = jnp.broadcast_to(both[j : j + 1, :], (SUBLANES, LANES))
            scaled = pivot / jnp.broadcast_to(both[j : j + 1, j : j + 1], (SUBLANES, LANES))
            states[index] = jnp.where(line == j, scaled, both - column * scaled)
    return [
        jnp.where(lane < SUBLANES, pltpu.roll(both, LANES - SUBLANES, 1), 0.0) for both in states
    ]


def solve_steps(sums_ref):
    total = sums_ref.shape[1]
    size = SUBLANES
    place = lax.broadcasted_iota(jnp.int32, (size, total), 1)
    line = lax.broadcasted_iota(jnp.int32, (size, total), 0)
    spot = lax.broadcasted_iota(jnp.int32, (total, LANES), 0)
    lane = lax.broadcasted_iota(jnp.int32, (total, LANES), 1)
    sums = sums_ref[...]

    def matrix(index, turned=False):
        row, column = place % size, spot // size % size
        if not turned:
            row, column = place // size % size, spot % size
        here = (place // size**2 == index) & (row == line)
        return jnp.dot(
            jnp.where(here, sums, 0.0),
            jnp.where(column == lane, 1.0, 0.0),
            precision=HIGHEST,
            preferred_element_type=jnp.float32,
        )

    gram_old, gram_image = matrix(0), matrix(3)
    curvature = 0.5 * (matrix(1) + matrix(1, True))
    mixed, mixed_turned = matrix(2), matrix(2, True)
    diagonal = lax.broadcasted_iota(jnp.int32, (size, LANES), 0)
    identity = jnp.where(diagonal == lax.broadcasted_iota(jnp.int32, (size, LANES), 1), 1.0, 0.0)
    step, old_inverse = small_solves([(curvature, gram_old), (gram_old, identity)])
    step_turned = small_transpose(step)
    rest = small_product(gram_image, step) - mixed_turned
    gram_new = gram_old - small_product(mixed, step) + small_product(step_turned, rest)
    return step_turned, small_product(gram_new, old_inverse)


def spread_coefficients(turned):
    size = SUBLANES
    wide = 4 * size**2
    lane = lax.broadcasted_iota(jnp.int32, (size, wide), 1)
    line = lax.broadcasted_iota(jnp.int32, (size, wide), 0)
    spread = jnp.zeros((size, wide), jnp.float32)
    for b in range(size):
        column = jnp.broadcast_to(turned[:, b : b + 1], (size, wide))
        spread = spread + jnp.where(lane // size % size == b, column, 0.0)
    high = spread.astype(jnp.bfloat16).astype(jnp.float32)
    spread = jnp.where(lane < 2 * size**2, high, spread - high)
    own = (lane % size == line) & (lane < 3 * size**2)
    rows = [
        jnp.where(own, jnp.broadcast_to(spread[a : a + 1], (size, wide)), 0.0) for a in range(size)
    ]
    return jnp.concatenate(rows, axis=0)


def split_rows(ref, row):
    value = jnp.concatenate([ref[b, 0, row : row + SUBLANES, :] for b in range(ref.shape[0])], axis=0)
    high = value.astype(jnp.bfloat16)
    low = (value - high.astype(jnp.float32)).astype(jnp.bfloat16)
    return jnp.concatenate([high, low, high], axis=0)


def update_kernel(
    sums_ref, solution_ref, residual_ref, direction_ref, image_ref, sol_out, res_out, dir_out, coef_ref
):
    rhs_count, _, rows, lon = direction_ref.shape
    size = rhs_count * SUBLANES

    @pl.when(pl.program_id(0) == 0)
    def _():
        step_turned, turn_turned = solve_steps(sums_ref)
        coefs = [spread_coefficients(step_turned), spread_coefficients(turn_turned)]
        coef_ref[...] = jnp.concatenate(coefs, axis=0).astype(jnp.bfloat16)

    for row in range(0, rows, SUBLANES):
        coefs = coef_ref[:, : 3 * size]
        moves = jnp.dot(coefs, split_rows(direction_ref, row), preferred_element_type=jnp.float32)
        drops = jnp.dot(coefs[:size], split_rows(image_ref, row), preferred_element_type=jnp.float32)
        for a in range(rhs_count):
            at = a * SUBLANES
            spot = (a, 0, slice(row, row + SUBLANES), slice(None))
            sol_out[spot] = solution_ref[spot] + moves[at : at + SUBLANES]
            left = residual_ref[spot] - drops[at : at + SUBLANES]
            res_out[spot] = left
            dir_out[spot] = left + moves[size + at : size + at + SUBLANES]


def update(sums, solution, residual, direction, image):
    rhs_count, weeks, rows, lon = direction.shape
    field = pl.BlockSpec((rhs_count, 1, rows, lon), lambda w: (0, w, 0, 0))
    shape = jax.ShapeDtypeStruct(direction.shape, jnp.float32)
    return pl.pallas_call(
        update_kernel,
        grid=(weeks,),
        in_specs=[whole(sums.shape)] + [field] * 4,
        out_specs=[field] * 3,
        scratch_shapes=[pltpu.VMEM((2 * rhs_count * SUBLANES, 4 * rhs_count * SUBLANES), jnp.bfloat16)],
        out_shape=[shape] * 3,
        compiler_params=params(16),
        cost_estimate=cost(6 * rhs_count * direction.size, 28 * direction.size),
        name="update",
    )(sums, solution, residual, direction, image)


def crossed(value, axis, by):
    if by == 0:
        return value
    return lax.ppermute(value, axis, [(i, i ^ by) for i in range(lax.axis_size(axis))])


def far_first(size):
    return [1 << bit for bit in reversed(range(size.bit_length() - 1))]


def neighbours(value, axis):
    size = lax.axis_size(axis)
    outer = [(i, i + 1) for i in range(1, size - 1, 2)]
    outer += [(after, before) for before, after in outer]
    return crossed(value, axis, 1), lax.ppermute(value, axis, outer)


def summed_over(value, axis):
    size = lax.axis_size(axis)
    reach = 1
    before = value
    while reach < size:
        before = value
        value = value + crossed(value, axis, reach)
        reach *= 2
    return value, before


def lat_windows(lat_width, band, rows):
    decay = rows / 2.0
    total = lat_width.shape[0]
    offsets = jnp.abs(jnp.arange(-rows, rows + 1)).astype(jnp.float32)
    limits = lat_width.astype(jnp.float32)
    normal = jnp.sqrt(
        jnp.sum(
            jnp.where(
                offsets[None, :] <= limits[:, None], jnp.exp(-2.0 * offsets / decay)[None, :], 0.0
            ),
            axis=1,
        )
    )
    padded_limits = jnp.pad(limits, (rows, rows), constant_values=-1.0)
    padded_normal = jnp.pad(normal, (rows, rows), constant_values=1.0)
    near_limits = lax.dynamic_slice_in_dim(padded_limits, band * rows, 3 * rows)
    near_normal = lax.dynamic_slice_in_dim(padded_normal, band * rows, 3 * rows)
    distance = jnp.abs(
        jnp.arange(rows)[:, None] + rows - jnp.arange(3 * rows)[None, :]
    ).astype(jnp.float32)
    fade = jnp.exp(-distance / decay)
    own_limits, own_normal = near_limits[rows : 2 * rows, None], near_normal[rows : 2 * rows, None]
    spread = jnp.where(distance <= own_limits, fade, 0.0) / own_normal
    pulled = jnp.where(distance <= near_limits[None, :], fade, 0.0) / near_normal[None, :]
    return spread, pulled


def shards(
    footprints,
    block_rows,
    block_cols,
    block_scale,
    lat_width,
    lon_width,
    obs_weight,
    solution,
    residual,
    direction,
):
    rhs_count, weeks, rows, lon = direction.shape
    blocks = footprints[0, 0]
    count, edge, _ = blocks.shape
    row_list = block_rows[0, 0]
    scales = jnp.exp2(-block_scale[0, 0].astype(jnp.float32))
    row_blocks = obs_weight.shape[0] // edge
    slots = lax.axis_size("obs")
    rhs = rhs_count // slots
    slab, band = lax.axis_index("obs"), lax.axis_index("lat")
    parts = lon // edge
    cols = weeks * rows * parts

    groups = chunk_of(rhs, BACK_GROUPS)
    each = rhs // groups
    order = (slab ^ jnp.arange(slots, dtype=jnp.int32)) * rhs
    own_width = lax.dynamic_slice_in_dim(lon_width, band * rows, rows)
    counts = jnp.broadcast_to(own_width[:, None] + 1, (rows, lon))

    lists = jnp.concatenate([crossed(block_cols, "obs", d) for d in range(slots)], axis=0)[:, 0]
    line, part = lists // parts, lists % parts
    places = ((line // rows) * parts + part) * rows + line % rows

    lon_own, words = spread_lon(
        lax.dynamic_slice_in_dim(direction, slab * rhs, rhs, 0), counts
    )
    halo = neighbours(words, "lat")
    hot = (places[:, :, None] == jnp.arange(cols)[None, None, :]).astype(jnp.bfloat16)
    hot_turned = (jnp.arange(cols)[:, None] == places.reshape(1, -1)).astype(jnp.bfloat16)
    lat_spread, lat_pulled = lat_windows(lat_width, band, rows)
    side = (band % 2).astype(jnp.int32).reshape(1)

    picks = spread_lat(side, lon_own, *halo, lat_spread, hot)
    cells = [crossed(picks[d], "obs", d) for d in range(slots)]
    kept = count // KEPT_OF * KEPT if count % KEPT_OF == 0 else 0
    stays = [preload(blocks, 0, kept, picks[0])] if kept else []
    near = preload(blocks, kept, count - kept, picks[0])
    sums, partial = summed_over(
        forward(row_list, scales, [*stays, near], cells, row_blocks), "lat"
    )
    near = preload(blocks, kept, count - kept, partial)
    weighted = sums.reshape(row_blocks, slots * rhs, edge) * obs_weight.reshape(row_blocks, 1, edge)
    terms = adjoint_terms(
        row_list, scales, [*stays, near], weighted.reshape(-1, edge), slots * groups, each
    )
    sent = [[crossed(terms[d * groups + g], "obs", d) for d in range(slots)] for g in range(groups)]
    own = []
    for group in range(groups):
        field, words = gather_cells(hot_turned, sent[group], each, weeks, rows, lon)
        own.append(pull_back(side, field, *neighbours(words, "lat"), lat_pulled, counts))

    starts = (order[:, None] + jnp.arange(groups, dtype=jnp.int32) * each).reshape(-1)
    products = jnp.zeros((SUBLANES, 4 * rhs_count**2), jnp.float32)
    images, places = [], ()

    def add_products(slot):
        nonlocal products, places, images
        words = [arrived[group][slot] for group in range(groups)]
        places += tuple(slot * groups + group for group in range(groups))
        *images, products = grams(starts, places, products, residual, direction, words, images)

    arrived = [{0: words} for words in own]
    for group in range(groups):
        for reach in far_first(slots):
            arrived[group][reach] = crossed(own[group], "obs", reach)
    add_products(0)
    first_products = products
    for reach in far_first(slots)[1:]:
        for group in range(groups):
            for bits in [bits for bits in arrived[group] if bits > reach and not bits % (2 * reach)]:
                words = arrived[group][bits]
                if group == groups - 1:
                    words, _ = lax.optimization_barrier((words, first_products))
                arrived[group][bits | reach] = crossed(words, "obs", reach)
    for slot in range(1, slots):
        add_products(slot)
    products, _ = summed_over(products, "lat")
    return tuple(update(products, solution, residual, direction, *images))


def solution(mesh):
    return jax.shard_map(
        shards,
        mesh=mesh,
        in_specs=(
            P("obs", "lat", None, None, None),
            P("obs", "lat", None),
            P("obs", "lat", None),
            P("obs", "lat", None),
            P(),
            P(),
            P("obs"),
            P(None, None, "lat", None),
            P(None, None, "lat", None),
            P(None, None, "lat", None),
        ),
        out_specs=(
            P(None, None, "lat", None),
            P(None, None, "lat", None),
            P(None, None, "lat", None),
        ),
        check_vma=False,
    )
```

```python
import functools
import math

import jax
import jax.numpy as jnp
from jax import lax
from jax.experimental import pallas as pl
from jax.experimental.pallas import tpu as pltpu
from jax.sharding import PartitionSpec as P

LANES = 128
CHUNK = 96
COPIES = 12
STREAM_MIB = 40
KEPT, KEPT_OF = 1, 2
BACK_GROUPS = 2
SUBLANES = 8
MIB = 1024 * 1024
HIGHEST = lax.Precision.HIGHEST


def params(mib):
    return pltpu.CompilerParams(vmem_limit_bytes=mib * MIB)


def cost(flops, nbytes):
    return pl.CostEstimate(flops=int(flops), bytes_accessed=int(nbytes), transcendentals=0)


def whole(shape):
    return pl.BlockSpec(shape, lambda *_: (0,) * len(shape), pipeline_mode=pl.Buffered(1))


def in_vmem(count):
    return [pl.BlockSpec(memory_space=pltpu.VMEM)] * count


def pow2(exponent):
    size = jnp.abs(exponent)
    up = jnp.ones(exponent.shape, jnp.float32)
    down = up
    for bit in range(7):
        on = ((size >> bit) & 1) == 1
        up = up * jnp.where(on, 2.0 ** (2**bit), 1.0)
        down = down * jnp.where(on, 2.0 ** -(2**bit), 1.0)
    return jnp.where(exponent < 0, down, up)


def exponent_of(peak):
    logs = jnp.log(jnp.maximum(peak, 1e-28)) * (1.0 / math.log(2.0))
    return jnp.ceil(logs + 1e-3).astype(jnp.int32)


def to_int(values, factor):
    return jnp.clip(jnp.round(values * factor), -32767.0, 32767.0).astype(jnp.int32)


def pack(high, low):
    return (high << 16) | (low & 0xFFFF)


def high_of(word):
    return word >> 16


def low_of(word):
    return (word << 16) >> 16


def words_shape(rhs, weeks, rows, lon):
    parts = lon // LANES
    tail = -(-rhs * parts // SUBLANES) * SUBLANES
    return parts * (rhs * weeks * rows // 2) + tail, LANES


def words_at(word_ref, body, at, parts):
    found = []
    for part in range(parts):
        start = part * body + at
        if not isinstance(start, int):
            start = pl.multiple_of(start, SUBLANES)
        found.append(word_ref[pl.ds(start, SUBLANES), :])
    return jnp.concatenate(found, axis=1)


def field_scale(word_ref, body, k, parts):
    first = parts * (body + k)
    row = jnp.concatenate(
        [word_ref[first + part : first + part + 1, :] for part in range(parts)], axis=1
    )
    return pow2(jnp.broadcast_to(row, (SUBLANES, row.shape[1])) - 15)


def exponent_rows(peaks):
    line = lax.broadcasted_iota(jnp.int32, (SUBLANES, peaks[0].shape[1]), 0)
    found = jnp.zeros(line.shape, jnp.int32)
    for k, peak in enumerate(peaks):
        found = jnp.where(line == k, exponent_of(jnp.max(peak, axis=0, keepdims=True)), found)
    return found


def pack_field(field_ref, word_ref, peaks):
    rhs, weeks, rows, lon = field_ref.shape
    half, parts = rows // 2, lon // LANES
    body = rhs * weeks * half
    tail = word_ref.shape[0] - parts * body
    line = lax.broadcasted_iota(jnp.int32, (tail, LANES), 0)
    kept = jnp.zeros((tail, LANES), jnp.int32)
    for k in range(rhs):
        exponent = exponent_of(jnp.max(peaks[k], axis=0, keepdims=True))
        for part in range(parts):
            own = exponent[:, part * LANES : (part + 1) * LANES]
            kept = jnp.where(line == k * parts + part, own, kept)
        factor = pow2(15 - jnp.broadcast_to(exponent, (SUBLANES, lon)))

        def one_week(week, carry):
            for start in range(0, half, SUBLANES):
                high = to_int(field_ref[k, week, start : start + SUBLANES, :], factor)
                low = to_int(field_ref[k, week, half + start : half + start + SUBLANES, :], factor)
                word = pack(high, low)
                for part in range(parts):
                    at = part * body + (k * weeks + week) * half + start
                    at = pl.multiple_of(at, SUBLANES)
                    word_ref[pl.ds(at, SUBLANES), :] = word[:, part * LANES : (part + 1) * LANES]
            return carry

        lax.fori_loop(0, weeks, one_week, 0)
    word_ref[parts * body :, :] = kept


def word_scale(word_ref, body, k):
    row = word_ref[body + k : body + k + 1, :] - 15
    return pow2(jnp.broadcast_to(row, (SUBLANES, row.shape[1])))


def lon_setup(lon):
    return lon / 32.0, (lon // 8 + 1).bit_length()


def lon_rows(rows, count, norm, lon):
    decay, bits = lon_setup(lon)
    fields = rows.shape[0] // SUBLANES
    count = jnp.concatenate([count] * fields, axis=0)
    windows = [rows, rows]
    taken = [jnp.zeros_like(rows)] * 2
    for bit in range(bits):
        reach = 2**bit
        fade = math.exp(-reach / decay)
        chosen = ((count >> bit) & 1) == 1
        for side in range(2):
            shift = reach if side == 0 else lon - reach
            moved = windows[side]
            if bit:
                moved = moved + fade * pltpu.roll(taken[side], shift, 1)
            taken[side] = jnp.where(chosen, moved, taken[side])
            if bit + 1 < bits:
                windows[side] = windows[side] + fade * pltpu.roll(windows[side], shift, 1)
    return (taken[0] + taken[1] - rows) * jnp.concatenate([norm] * fields, axis=0)


def lon_norm(count, lon):
    decay, _ = lon_setup(lon)
    ratio = math.exp(-2.0 / decay)
    ends = jnp.exp(count.astype(jnp.float32) * (-2.0 / decay))
    return 1.0 / jnp.sqrt(1.0 + (2.0 / (1.0 - ratio)) * (ratio - ends))


def lon_field(source_ref, count_ref, out_ref):
    rhs, weeks, rows, lon = out_ref.shape

    def one_group(group, peaks):
        at = pl.multiple_of(group * SUBLANES, SUBLANES)
        count = count_ref[pl.ds(at, SUBLANES), :]
        norm = lon_norm(count, lon)
        fields = [source_ref[k, w, pl.ds(at, SUBLANES), :] for k in range(rhs) for w in range(weeks)]
        result = lon_rows(jnp.concatenate(fields, axis=0), count, norm, lon)
        peaks = list(peaks)
        for k in range(rhs):
            for w in range(weeks):
                start = (k * weeks + w) * SUBLANES
                part = result[start : start + SUBLANES]
                out_ref[k, w, pl.ds(at, SUBLANES), :] = part
                peaks[k] = jnp.maximum(peaks[k], jnp.abs(part))
        return tuple(peaks)

    zero = jnp.zeros((SUBLANES, lon), jnp.float32)
    return lax.fori_loop(0, rows // SUBLANES, one_group, (zero,) * rhs)


def spread_lon_kernel(field_ref, count_ref, out_ref, word_ref):
    pack_field(out_ref, word_ref, lon_field(field_ref, count_ref, out_ref))


def spread_lon(field, counts):
    rhs, weeks, rows, lon = field.shape
    return pl.pallas_call(
        spread_lon_kernel,
        in_specs=in_vmem(2),
        out_specs=in_vmem(2),
        out_shape=[
            jax.ShapeDtypeStruct(field.shape, jnp.float32),
            jax.ShapeDtypeStruct(words_shape(rhs, weeks, rows, lon), jnp.int32),
        ],
        compiler_params=params(6),
        cost_estimate=cost(field.size * 100, field.size * 10),
        name="spread_lon",
    )(field, counts)


def lat_mix(side_ref, weights_ref, window_ref, k, week, pair_ref, own_ref, cross_ref, scales):
    rhs, weeks, rows, lon = own_ref.shape
    half = rows // 2
    body, parts = rhs * weeks * half, lon // LANES
    before = 2 * rows * (1 - side_ref[0])
    for base, ref, scale in (
        (before, pair_ref, scales[0]),
        (2 * rows - before, cross_ref, scales[1]),
    ):
        for start in range(0, half, SUBLANES):
            at = (k * weeks + week) * half + start
            word = words_at(ref, body, at, parts)
            for to, number in ((start, high_of(word)), (half + start, low_of(word))):
                to = pl.multiple_of(base + to, SUBLANES)
                window_ref[pl.ds(to, SUBLANES), :] = number.astype(jnp.float32) * scale
    window_ref[rows : 2 * rows, :] = own_ref[k, week]
    return jnp.dot(
        weights_ref[...],
        window_ref[...],
        precision=HIGHEST,
        preferred_element_type=jnp.float32,
    )


def spread_lat_kernel(slots, side_ref, own_ref, pair_ref, cross_ref, weights_ref, hot_ref, *rest):
    picks, (window_ref, cells_ref) = rest[:slots], rest[slots:]
    rhs, weeks, rows, lon = own_ref.shape
    parts = lon // LANES
    body = rhs * weeks * rows // 2
    for k in range(rhs):
        scales = [field_scale(ref, body, k, parts) for ref in (pair_ref, cross_ref)]
        for week in range(weeks):
            mixed = lat_mix(
                side_ref, weights_ref, window_ref, k, week, pair_ref, own_ref, cross_ref, scales
            )
            for part in range(parts):
                at = (week * parts + part) * rows
                cells_ref[at : at + rows, k * LANES : (k + 1) * LANES] = mixed[
                    :, part * LANES : (part + 1) * LANES
                ].astype(jnp.bfloat16)
    for slot in range(slots):
        found = jnp.dot(
            hot_ref[slot], cells_ref[...], preferred_element_type=jnp.float32
        ).astype(jnp.bfloat16)
        for k in range(rhs):
            picks[slot][k] = found[:, k * LANES : (k + 1) * LANES]


def spread_lat(side, own, pair, cross, weights, hot):
    rhs, weeks, rows, lon = own.shape
    slots, blocks, cols = hot.shape
    return pl.pallas_call(
        functools.partial(spread_lat_kernel, slots),
        in_specs=[pl.BlockSpec(memory_space=pltpu.SMEM)] + in_vmem(5),
        out_specs=in_vmem(slots),
        out_shape=[jax.ShapeDtypeStruct((rhs, blocks, LANES), jnp.bfloat16)] * slots,
        scratch_shapes=[
            pltpu.VMEM((3 * rows, lon), jnp.float32),
            pltpu.VMEM((cols, rhs * LANES), jnp.bfloat16),
        ],
        compiler_params=params(10),
        cost_estimate=cost(rhs * slots * blocks * cols * LANES * 2, rhs * weeks * rows * lon * 10),
        name="spread_lat",
    )(side, own, pair, cross, weights, hot)


def chunk_of(count, most):
    return max(size for size in range(1, most + 1) if count % size == 0)


def preload_kernel(first, after_ref, blocks_ref, out_ref, done):
    del after_ref
    parts = done.shape[0]
    size = out_ref.shape[0] // parts
    copies = [
        pltpu.make_async_copy(
            blocks_ref.at[pl.ds(first + part * size, size)],
            out_ref.at[pl.ds(part * size, size)],
            done.at[part],
        )
        for part in range(parts)
    ]
    for copy in copies:
        copy.start()
    for copy in copies:
        copy.wait()


def preload(blocks, first, count, after):
    parts = chunk_of(count, COPIES)
    shape = (count, *blocks.shape[1:])
    return pl.pallas_call(
        functools.partial(preload_kernel, first),
        in_specs=[pl.BlockSpec(memory_space=pl.ANY)] * 2,
        out_specs=pl.BlockSpec(memory_space=pltpu.VMEM),
        out_shape=jax.ShapeDtypeStruct(shape, blocks.dtype),
        scratch_shapes=[pltpu.SemaphoreType.DMA((parts,))],
        compiler_params=params(STREAM_MIB),
        cost_estimate=cost(0, count * blocks[0].size * 4),
        name="preload",
    )(after, blocks)


def forward_kernel(pieces, row_ref, scale_ref, *rest):
    pieces, picks, (out_ref, cells_ref) = rest[:pieces], rest[pieces:-2], rest[-2:]
    rhs, count, edge = picks[0].shape
    lines = len(picks) * rhs
    out_ref[...] = jnp.zeros_like(out_ref)
    for place, pick_ref in enumerate(picks):
        for k in range(rhs):
            cells_ref[pl.ds(place * rhs + k, count, stride=lines), :] = pick_ref[k].astype(
                jnp.float32
            )

    def one_chunk(piece_ref, first, chunk, step, carry):
        values = []
        for n in range(0, chunk, 2):
            index = step * chunk + n
            at = pl.multiple_of((first + index) * lines, 2 * lines)
            both = lax.dot_general(
                cells_ref[pl.ds(at, 2 * lines), :].astype(jnp.bfloat16),
                piece_ref[pl.ds(index, 2)].reshape(2 * edge, edge),
                (((1,), (1,)), ((), ())),
                preferred_element_type=jnp.float32,
            )
            values += [both[:lines, :edge], both[lines:, edge:]]
        for n in range(chunk):
            index = first + step * chunk + n
            at = pl.multiple_of(row_ref[index] * lines, lines)
            out_ref[pl.ds(at, lines), :] += values[n] * scale_ref[index]
        return carry

    over_chunks(pieces, one_chunk)


def over_chunks(pieces, one_chunk):
    first = 0
    for piece_ref in pieces:
        count = piece_ref.shape[0]
        chunk = 2 * chunk_of(count // 2, CHUNK // 2)
        lax.fori_loop(0, count // chunk, functools.partial(one_chunk, piece_ref, first, chunk), 0)
        first += count


def forward(row_list, scales, pieces, picks, row_blocks):
    rhs, count, edge = picks[0].shape
    lines = len(picks) * rhs
    return pl.pallas_call(
        functools.partial(forward_kernel, len(pieces)),
        in_specs=[pl.BlockSpec(memory_space=pltpu.SMEM)] * 2 + in_vmem(len(pieces) + len(picks)),
        out_specs=pl.BlockSpec(memory_space=pltpu.VMEM),
        out_shape=jax.ShapeDtypeStruct((row_blocks * lines, edge), jnp.float32),
        scratch_shapes=[pltpu.VMEM((count * lines, edge), jnp.float32)],
        compiler_params=params(15),
        cost_estimate=cost(count * edge**2 * 2 * lines, count * edge**2 * 2),
        name="forward",
    )(row_list, scales, *pieces, *picks)


def adjoint_kernel(pieces, rhs, row_ref, scale_ref, *rest):
    pieces, values_ref, outs, terms_ref = rest[:pieces], rest[pieces], rest[pieces + 1 : -1], rest[-1]
    lines = len(outs) * rhs
    edge = values_ref.shape[1]
    count = terms_ref.shape[0] // lines

    def one_chunk(piece_ref, first, chunk, step, carry):
        for n in range(0, chunk, 2):
            here = step * chunk + n
            index = first + here
            pulled = [
                values_ref[pl.ds(pl.multiple_of(row_ref[index + q] * lines, lines), lines), :]
                for q in range(2)
            ]
            both = jnp.dot(
                jnp.concatenate(pulled, axis=0).astype(jnp.bfloat16),
                jnp.concatenate([piece_ref[here + q] for q in range(2)], axis=1),
                preferred_element_type=jnp.float32,
            )
            for q in range(2):
                to = pl.multiple_of((index + q) * lines, lines)
                part = both[q * lines : (q + 1) * lines, q * edge : (q + 1) * edge]
                terms_ref[pl.ds(to, lines), :] = part * scale_ref[index + q]
        return carry

    over_chunks(pieces, one_chunk)
    half = count // 2
    for place, out_ref in enumerate(outs):
        terms = [terms_ref[pl.ds(place * rhs + k, count, stride=lines), :] for k in range(rhs)]
        exponents = exponent_rows([jnp.abs(term) for term in terms])
        out_ref[rhs * half :, :] = exponents
        for k in range(rhs):
            number = to_int(terms[k], pow2(15 - exponents[k : k + 1]))
            out_ref[k * half : (k + 1) * half, :] = pack(number[:half], number[half:])


def adjoint_terms(row_list, scales, pieces, values, outs, rhs):
    count = sum(piece.shape[0] for piece in pieces)
    edge = values.shape[1]
    lines = outs * rhs
    words = rhs * count // 2 + SUBLANES
    return pl.pallas_call(
        functools.partial(adjoint_kernel, len(pieces), rhs),
        in_specs=[pl.BlockSpec(memory_space=pltpu.SMEM)] * 2 + in_vmem(len(pieces) + 1),
        out_specs=in_vmem(outs),
        out_shape=[jax.ShapeDtypeStruct((words, edge), jnp.int32)] * outs,
        scratch_shapes=[pltpu.VMEM((count * lines, edge), jnp.float32)],
        compiler_params=params(15),
        cost_estimate=cost(count * edge**2 * 2 * lines, count * edge**2 * 2),
        name="adjoint",
    )(row_list, scales, *pieces, values)


def gather_cells_kernel(slots, hot_ref, *rest):
    terms, (field_ref, word_ref, split_ref) = rest[:slots], rest[slots:]
    rhs, weeks, rows, lon = field_ref.shape
    count = hot_ref.shape[1] // slots
    half = count // 2
    wide = rhs * LANES
    for slot in range(slots):
        for k in range(rhs):
            scale = word_scale(terms[slot], rhs * half, k)[:1]
            word = terms[slot][k * half : (k + 1) * half, :]
            for base, number in ((0, high_of(word)), (half, low_of(word))):
                coarse = (number + 128) >> 8
                fine = number - (coarse << 8)
                at = slot * count + base
                split_ref[at : at + half, k * LANES : (k + 1) * LANES] = (
                    (coarse << 8).astype(jnp.float32) * scale
                ).astype(jnp.bfloat16)
                split_ref[at : at + half, wide + k * LANES : wide + (k + 1) * LANES] = (
                    fine.astype(jnp.float32) * scale
                ).astype(jnp.bfloat16)
    peaks = [jnp.zeros((SUBLANES, lon), jnp.float32)] * rhs
    parts = lon // LANES
    for week in range(weeks):
        at = week * parts * rows
        both = jnp.dot(
            hot_ref[at : at + parts * rows, :],
            split_ref[...],
            preferred_element_type=jnp.float32,
        )
        cells = both[:, :wide] + both[:, wide:]
        for k in range(rhs):
            for part in range(parts):
                field_ref[k, week, :, part * LANES : (part + 1) * LANES] = cells[
                    part * rows : (part + 1) * rows, k * LANES : (k + 1) * LANES
                ]
            for start in range(0, rows, SUBLANES):
                peaks[k] = jnp.maximum(
                    peaks[k], jnp.abs(field_ref[k, week, start : start + SUBLANES, :])
                )
    pack_field(field_ref, word_ref, peaks)


def gather_cells(hot_turned, terms, rhs, weeks, rows, lon):
    slots = len(terms)
    return pl.pallas_call(
        functools.partial(gather_cells_kernel, slots),
        in_specs=in_vmem(1 + slots),
        out_specs=in_vmem(2),
        out_shape=[
            jax.ShapeDtypeStruct((rhs, weeks, rows, lon), jnp.float32),
            jax.ShapeDtypeStruct(words_shape(rhs, weeks, rows, lon), jnp.int32),
        ],
        scratch_shapes=[pltpu.VMEM((hot_turned.shape[1], 2 * rhs * LANES), jnp.bfloat16)],
        compiler_params=params(12),
        cost_estimate=cost(rhs * hot_turned.size * 4 * LANES, rhs * weeks * rows * lon * 10),
        name="gather_cells",
    )(hot_turned, *terms)


def pull_back_kernel(
    side_ref, own_ref, pair_ref, cross_ref, weights_ref, count_ref, word_ref, window_ref, field_ref
):
    rhs, weeks, rows, lon = own_ref.shape
    parts = lon // LANES
    body = rhs * weeks * rows // 2
    for k in range(rhs):
        scales = [field_scale(ref, body, k, parts) for ref in (pair_ref, cross_ref)]
        for week in range(weeks):
            field_ref[k, week] = lat_mix(
                side_ref, weights_ref, window_ref, k, week, pair_ref, own_ref, cross_ref, scales
            )
    pack_field(field_ref, word_ref, lon_field(field_ref, count_ref, field_ref))


def pull_back(side, own, pair, cross, weights, counts):
    rhs, weeks, rows, lon = own.shape
    return pl.pallas_call(
        pull_back_kernel,
        in_specs=[pl.BlockSpec(memory_space=pltpu.SMEM)] + in_vmem(5),
        out_specs=pl.BlockSpec(memory_space=pltpu.VMEM),
        out_shape=jax.ShapeDtypeStruct(pair.shape, jnp.int32),
        scratch_shapes=[
            pltpu.VMEM((3 * rows, lon), jnp.float32),
            pltpu.VMEM((rhs, weeks, rows, lon), jnp.float32),
        ],
        compiler_params=params(8),
        cost_estimate=cost(rhs * weeks * rows * lon * 300, rhs * weeks * rows * lon * 10),
        name="pull_back",
    )(side, own, pair, cross, weights, counts)


def gram_kernel(places, count, rhs, order_ref, sums_before, residual_ref, direction_ref, *rest):
    words, (image_ref, gram_ref, sums_ref) = rest[:count], rest[-3:]
    rhs_count, weeks, rows, lon = direction_ref.shape
    half = rows // 2
    body, parts = rhs * weeks * half, lon // LANES
    old_places, new_places = places[:-count], places[-count:]
    for word_ref, place in zip(words, new_places):
        for k in range(rhs):
            index = order_ref[place] + k
            scale = field_scale(word_ref, body, k, parts)

            def one_week(week, carry):
                for start in range(0, half, SUBLANES):
                    word = words_at(word_ref, body, (k * weeks + week) * half + start, parts)
                    for base, number in ((start, high_of(word)), (half + start, low_of(word))):
                        image_ref[index, week, base : base + SUBLANES, :] = (
                            direction_ref[index, week, base : base + SUBLANES, :]
                            + number.astype(jnp.float32) * scale
                        )
                return carry

            lax.fori_loop(0, weeks, one_week, 0)

    sums_ref[...] = jnp.zeros_like(sums_ref)
    row_groups = rows // SUBLANES

    def tile(blocks):
        def one_week(week, sums):
            sums = list(sums)
            for row in range(0, rows, SUBLANES):
                for lane in range(0, lon, LANES):
                    spot = (week, slice(row, row + SUBLANES), slice(lane, lane + LANES))
                    place = 0
                    for _, lefts, rights, _ in blocks:
                        right = [ref[(k, *spot)] for ref, k, _ in rights]
                        for ref, k, _ in lefts:
                            left = ref[(k, *spot)]
                            for b in range(len(rights)):
                                sums[place] = sums[place] + left * right[b]
                                place += 1
            return tuple(sums)

        zero = jnp.zeros((SUBLANES, LANES), jnp.float32)
        total = sum(len(lefts) * len(rights) for _, lefts, rights, _ in blocks)
        sums = list(lax.fori_loop(0, weeks, one_week, (zero,) * total))
        for index, lefts, rights, mirror in blocks:
            for _, _, row in lefts:
                for _, _, column in rights:
                    lanes = jnp.sum(sums.pop(0), axis=0, keepdims=True)
                    for row_at, column_at in ((row, column), (column, row))[: 1 + mirror]:
                        at = (index * rhs_count + row_at) * rhs_count + column_at
                        sums_ref[pl.ds(at, 1), :] = lanes

    def listed(places):
        found = [order_ref[place] + k for place in places for k in range(rhs)]
        return [(image_ref, index, index) for index in found]

    residuals = [(residual_ref, k, k) for k in range(rhs_count)]
    directions = [(direction_ref, k, k) for k in range(rhs_count)]
    images = listed(new_places)
    if not old_places:
        for a in range(rhs_count):
            tile([(0, residuals[a : a + 1], residuals[a:], True)])
    for b in range(0, len(images), 2):
        right = images[b : b + 2]
        left = images[: b + len(right)] + listed(old_places)
        tile([(1, directions, right, False), (2, residuals, right, False), (3, left, right, True)])

    gram_ref[...] = sums_before[...] + lax.dot_general(
        jnp.ones((SUBLANES, LANES), jnp.float32),
        sums_ref[...],
        (((1,), (1,)), ((), ())),
        precision=HIGHEST,
        preferred_element_type=jnp.float32,
    )


def grams(order, places, sums, residual, direction, words, rhs, images):
    rhs_count, weeks, rows, lon = direction.shape
    total = 4 * rhs_count**2
    count = len(words)
    return pl.pallas_call(
        functools.partial(gram_kernel, places, count, rhs),
        in_specs=[pl.BlockSpec(memory_space=pltpu.SMEM)] + in_vmem(3 + count + len(images)),
        out_specs=in_vmem(2),
        out_shape=[
            jax.ShapeDtypeStruct(direction.shape, jnp.float32),
            jax.ShapeDtypeStruct((SUBLANES, total), jnp.float32),
        ],
        scratch_shapes=[pltpu.VMEM((total, LANES), jnp.float32)],
        input_output_aliases={4 + count: 0} if images else {},
        compiler_params=params(14),
        cost_estimate=cost(8 * rhs_count * direction.size, 16 * direction.size),
        name="grams",
    )(order, sums, residual, direction, *words, *images)


def small_product(left, right):
    total = jnp.zeros((SUBLANES, LANES), jnp.float32)
    for j in range(SUBLANES):
        column = jnp.broadcast_to(left[:, j : j + 1], (SUBLANES, LANES))
        total = total + column * jnp.broadcast_to(right[j : j + 1, :], (SUBLANES, LANES))
    return total


def small_transpose(value):
    rest = jnp.zeros((LANES - SUBLANES, LANES), jnp.float32)
    return jnp.concatenate([value, rest], axis=0).T[:SUBLANES]


def small_solves(systems):
    line = lax.broadcasted_iota(jnp.int32, (SUBLANES, LANES), 0)
    lane = lax.broadcasted_iota(jnp.int32, (SUBLANES, LANES), 1)
    states = [matrix + pltpu.roll(right, SUBLANES, 1) for matrix, right in systems]
    for j in range(SUBLANES):
        for index, both in enumerate(states):
            column = jnp.broadcast_to(both[:, j : j + 1], (SUBLANES, LANES))
            pivot = jnp.broadcast_to(both[j : j + 1, :], (SUBLANES, LANES))
            scaled = pivot / jnp.broadcast_to(both[j : j + 1, j : j + 1], (SUBLANES, LANES))
            states[index] = jnp.where(line == j, scaled, both - column * scaled)
    return [
        jnp.where(lane < SUBLANES, pltpu.roll(both, LANES - SUBLANES, 1), 0.0) for both in states
    ]


def solve_steps(sums_ref):
    total = sums_ref.shape[1]
    size = SUBLANES
    place = lax.broadcasted_iota(jnp.int32, (size, total), 1)
    line = lax.broadcasted_iota(jnp.int32, (size, total), 0)
    spot = lax.broadcasted_iota(jnp.int32, (total, LANES), 0)
    lane = lax.broadcasted_iota(jnp.int32, (total, LANES), 1)
    sums = sums_ref[...]

    def matrix(index, turned=False):
        row, column = place % size, spot // size % size
        if not turned:
            row, column = place // size % size, spot % size
        here = (place // size**2 == index) & (row == line)
        return jnp.dot(
            jnp.where(here, sums, 0.0),
            jnp.where(column == lane, 1.0, 0.0),
            precision=HIGHEST,
            preferred_element_type=jnp.float32,
        )

    gram_old, gram_image = matrix(0), matrix(3)
    curvature = 0.5 * (matrix(1) + matrix(1, True))
    mixed, mixed_turned = matrix(2), matrix(2, True)
    diagonal = lax.broadcasted_iota(jnp.int32, (size, LANES), 0)
    identity = jnp.where(diagonal == lax.broadcasted_iota(jnp.int32, (size, LANES), 1), 1.0, 0.0)
    step, old_inverse = small_solves([(curvature, gram_old), (gram_old, identity)])
    step_turned = small_transpose(step)
    rest = small_product(gram_image, step) - mixed_turned
    gram_new = gram_old - small_product(mixed, step) + small_product(step_turned, rest)
    return step_turned, small_product(gram_new, old_inverse)


def spread_coefficients(turned):
    size = SUBLANES
    wide = 4 * size**2
    lane = lax.broadcasted_iota(jnp.int32, (size, wide), 1)
    line = lax.broadcasted_iota(jnp.int32, (size, wide), 0)
    spread = jnp.zeros((size, wide), jnp.float32)
    for b in range(size):
        column = jnp.broadcast_to(turned[:, b : b + 1], (size, wide))
        spread = spread + jnp.where(lane // size % size == b, column, 0.0)
    high = spread.astype(jnp.bfloat16).astype(jnp.float32)
    spread = jnp.where(lane < 2 * size**2, high, spread - high)
    own = (lane % size == line) & (lane < 3 * size**2)
    rows = [
        jnp.where(own, jnp.broadcast_to(spread[a : a + 1], (size, wide)), 0.0) for a in range(size)
    ]
    return jnp.concatenate(rows, axis=0)


def split_rows(ref, row):
    value = jnp.concatenate([ref[b, 0, row : row + SUBLANES, :] for b in range(ref.shape[0])], axis=0)
    high = value.astype(jnp.bfloat16)
    low = (value - high.astype(jnp.float32)).astype(jnp.bfloat16)
    return jnp.concatenate([high, low, high], axis=0)


def update_kernel(
    sums_ref, solution_ref, residual_ref, direction_ref, image_ref, sol_out, res_out, dir_out, coef_ref
):
    rhs_count, _, rows, lon = direction_ref.shape
    size = rhs_count * SUBLANES

    @pl.when(pl.program_id(0) == 0)
    def _():
        step_turned, turn_turned = solve_steps(sums_ref)
        coefs = [spread_coefficients(step_turned), spread_coefficients(turn_turned)]
        coef_ref[...] = jnp.concatenate(coefs, axis=0).astype(jnp.bfloat16)

    for row in range(0, rows, SUBLANES):
        coefs = coef_ref[:, : 3 * size]
        moves = jnp.dot(coefs, split_rows(direction_ref, row), preferred_element_type=jnp.float32)
        drops = jnp.dot(coefs[:size], split_rows(image_ref, row), preferred_element_type=jnp.float32)
        for a in range(rhs_count):
            at = a * SUBLANES
            spot = (a, 0, slice(row, row + SUBLANES), slice(None))
            sol_out[spot] = solution_ref[spot] + moves[at : at + SUBLANES]
            left = residual_ref[spot] - drops[at : at + SUBLANES]
            res_out[spot] = left
            dir_out[spot] = left + moves[size + at : size + at + SUBLANES]


def update(sums, solution, residual, direction, image):
    rhs_count, weeks, rows, lon = direction.shape
    field = pl.BlockSpec((rhs_count, 1, rows, lon), lambda w: (0, w, 0, 0))
    shape = jax.ShapeDtypeStruct(direction.shape, jnp.float32)
    return pl.pallas_call(
        update_kernel,
        grid=(weeks,),
        in_specs=[whole(sums.shape)] + [field] * 4,
        out_specs=[field] * 3,
        scratch_shapes=[pltpu.VMEM((2 * rhs_count * SUBLANES, 4 * rhs_count * SUBLANES), jnp.bfloat16)],
        out_shape=[shape] * 3,
        compiler_params=params(16),
        cost_estimate=cost(6 * rhs_count * direction.size, 28 * direction.size),
        name="update",
    )(sums, solution, residual, direction, image)


def crossed(value, axis, by):
    if by == 0:
        return value
    return lax.ppermute(value, axis, [(i, i ^ by) for i in range(lax.axis_size(axis))])


def far_first(size):
    return [1 << bit for bit in reversed(range(size.bit_length() - 1))]


def neighbours(value, axis):
    size = lax.axis_size(axis)
    outer = [(i, i + 1) for i in range(1, size - 1, 2)]
    outer += [(after, before) for before, after in outer]
    return crossed(value, axis, 1), lax.ppermute(value, axis, outer)


def summed_over(value, axis):
    size = lax.axis_size(axis)
    reach = 1
    before = value
    while reach < size:
        before = value
        value = value + crossed(value, axis, reach)
        reach *= 2
    return value, before


def lat_windows(lat_width, band, rows):
    decay = rows / 2.0
    total = lat_width.shape[0]
    offsets = jnp.abs(jnp.arange(-rows, rows + 1)).astype(jnp.float32)
    limits = lat_width.astype(jnp.float32)
    normal = jnp.sqrt(
        jnp.sum(
            jnp.where(
                offsets[None, :] <= limits[:, None], jnp.exp(-2.0 * offsets / decay)[None, :], 0.0
            ),
            axis=1,
        )
    )
    padded_limits = jnp.pad(limits, (rows, rows), constant_values=-1.0)
    padded_normal = jnp.pad(normal, (rows, rows), constant_values=1.0)
    near_limits = lax.dynamic_slice_in_dim(padded_limits, band * rows, 3 * rows)
    near_normal = lax.dynamic_slice_in_dim(padded_normal, band * rows, 3 * rows)
    distance = jnp.abs(
        jnp.arange(rows)[:, None] + rows - jnp.arange(3 * rows)[None, :]
    ).astype(jnp.float32)
    fade = jnp.exp(-distance / decay)
    own_limits, own_normal = near_limits[rows : 2 * rows, None], near_normal[rows : 2 * rows, None]
    spread = jnp.where(distance <= own_limits, fade, 0.0) / own_normal
    pulled = jnp.where(distance <= near_limits[None, :], fade, 0.0) / near_normal[None, :]
    return spread, pulled


def shards(
    footprints,
    block_rows,
    block_cols,
    block_scale,
    lat_width,
    lon_width,
    obs_weight,
    solution,
    residual,
    direction,
):
    rhs_count, weeks, rows, lon = direction.shape
    blocks = footprints[0, 0]
    count, edge, _ = blocks.shape
    row_list = block_rows[0, 0]
    scales = jnp.exp2(-block_scale[0, 0].astype(jnp.float32))
    row_blocks = obs_weight.shape[0] // edge
    slots = lax.axis_size("obs")
    rhs = rhs_count // slots
    slab, band = lax.axis_index("obs"), lax.axis_index("lat")
    parts = lon // edge
    cols = weeks * rows * parts

    groups = chunk_of(rhs, BACK_GROUPS)
    each = rhs // groups
    order = (slab ^ jnp.arange(slots, dtype=jnp.int32)) * rhs
    own_width = lax.dynamic_slice_in_dim(lon_width, band * rows, rows)
    counts = jnp.broadcast_to(own_width[:, None] + 1, (rows, lon))

    lists = jnp.concatenate([crossed(block_cols, "obs", d) for d in range(slots)], axis=0)[:, 0]
    line, part = lists // parts, lists % parts
    places = ((line // rows) * parts + part) * rows + line % rows

    lon_own, words = spread_lon(
        lax.dynamic_slice_in_dim(direction, slab * rhs, rhs, 0), counts
    )
    halo = neighbours(words, "lat")
    hot = (places[:, :, None] == jnp.arange(cols)[None, None, :]).astype(jnp.bfloat16)
    hot_turned = (jnp.arange(cols)[:, None] == places.reshape(1, -1)).astype(jnp.bfloat16)
    lat_spread, lat_pulled = lat_windows(lat_width, band, rows)
    side = (band % 2).astype(jnp.int32).reshape(1)

    picks = spread_lat(side, lon_own, *halo, lat_spread, hot)
    cells = [crossed(picks[d], "obs", d) for d in range(slots)]
    kept = count // KEPT_OF * KEPT if count % KEPT_OF == 0 else 0
    stays = [preload(blocks, 0, kept, picks[0])] if kept else []
    near = preload(blocks, kept, count - kept, picks[0])
    sums, partial = summed_over(
        forward(row_list, scales, [*stays, near], cells, row_blocks), "lat"
    )
    near = preload(blocks, kept, count - kept, partial)
    weighted = sums.reshape(row_blocks, slots * rhs, edge) * obs_weight.reshape(row_blocks, 1, edge)
    terms = adjoint_terms(
        row_list, scales, [*stays, near], weighted.reshape(-1, edge), slots * groups, each
    )
    sent = [[crossed(terms[d * groups + g], "obs", d) for d in range(slots)] for g in range(groups)]
    own = []
    for group in range(groups):
        field, words = gather_cells(hot_turned, sent[group], each, weeks, rows, lon)
        own.append(pull_back(side, field, *neighbours(words, "lat"), lat_pulled, counts))

    starts = (order[:, None] + jnp.arange(groups, dtype=jnp.int32) * each).reshape(-1)
    products = jnp.zeros((SUBLANES, 4 * rhs_count**2), jnp.float32)
    images, places = [], ()

    def add_products(slot):
        nonlocal products, places, images
        words = [arrived[group][slot] for group in range(groups)]
        places += tuple(slot * groups + group for group in range(groups))
        *images, products = grams(
            starts, places, products, residual, direction, words, each, images
        )

    arrived = [{0: words} for words in own]
    for group in range(groups):
        for reach in far_first(slots):
            arrived[group][reach] = crossed(own[group], "obs", reach)
    add_products(0)
    first_products = products
    for reach in far_first(slots)[1:]:
        for group in range(groups):
            for bits in [bits for bits in arrived[group] if bits > reach and not bits % (2 * reach)]:
                words = arrived[group][bits]
                if group == groups - 1:
                    words, _ = lax.optimization_barrier((words, first_products))
                arrived[group][bits | reach] = crossed(words, "obs", reach)
    for slot in range(1, slots):
        add_products(slot)
    products, _ = summed_over(products, "lat")
    return tuple(update(products, solution, residual, direction, *images))


def solution(mesh):
    return jax.shard_map(
        shards,
        mesh=mesh,
        in_specs=(
            P("obs", "lat", None, None, None),
            P("obs", "lat", None),
            P("obs", "lat", None),
            P("obs", "lat", None),
            P(),
            P(),
            P("obs"),
            P(None, None, "lat", None),
            P(None, None, "lat", None),
            P(None, None, "lat", None),
        ),
        out_specs=(
            P(None, None, "lat", None),
            P(None, None, "lat", None),
            P(None, None, "lat", None),
        ),
        check_vma=False,
    )
```

```python
import functools
import math

import jax
import jax.numpy as jnp
from jax import lax
from jax.experimental import pallas as pl
from jax.experimental.pallas import tpu as pltpu
from jax.sharding import PartitionSpec as P

LANES = 128
CHUNK = 96
COPIES = 12
STREAM_MIB = 40
KEPT, KEPT_OF = 1, 2
BACK_GROUPS = 2
SUBLANES = 8
MIB = 1024 * 1024
HIGHEST = lax.Precision.HIGHEST


def params(mib):
    return pltpu.CompilerParams(vmem_limit_bytes=mib * MIB)


def cost(flops, nbytes):
    return pl.CostEstimate(flops=int(flops), bytes_accessed=int(nbytes), transcendentals=0)


def whole(shape):
    return pl.BlockSpec(shape, lambda *_: (0,) * len(shape), pipeline_mode=pl.Buffered(1))


def in_vmem(count):
    return [pl.BlockSpec(memory_space=pltpu.VMEM)] * count


def pow2(exponent):
    size = jnp.abs(exponent)
    up = jnp.ones(exponent.shape, jnp.float32)
    down = up
    for bit in range(7):
        on = ((size >> bit) & 1) == 1
        up = up * jnp.where(on, 2.0 ** (2**bit), 1.0)
        down = down * jnp.where(on, 2.0 ** -(2**bit), 1.0)
    return jnp.where(exponent < 0, down, up)


def exponent_of(peak):
    logs = jnp.log(jnp.maximum(peak, 1e-28)) * (1.0 / math.log(2.0))
    return jnp.ceil(logs + 1e-3).astype(jnp.int32)


def to_int(values, factor):
    return jnp.clip(jnp.round(values * factor), -32767.0, 32767.0).astype(jnp.int32)


def pack(high, low):
    return (high << 16) | (low & 0xFFFF)


def high_of(word):
    return word >> 16


def low_of(word):
    return (word << 16) >> 16


def words_shape(rhs, weeks, rows, lon):
    parts = lon // LANES
    tail = -(-rhs * parts // SUBLANES) * SUBLANES
    return parts * (rhs * weeks * rows // 2) + tail, LANES


def words_at(word_ref, body, at, parts):
    found = []
    for part in range(parts):
        start = part * body + at
        if not isinstance(start, int):
            start = pl.multiple_of(start, SUBLANES)
        found.append(word_ref[pl.ds(start, SUBLANES), :])
    return jnp.concatenate(found, axis=1)


def field_scale(word_ref, body, k, parts):
    first = parts * (body + k)
    row = jnp.concatenate(
        [word_ref[first + part : first + part + 1, :] for part in range(parts)], axis=1
    )
    return pow2(jnp.broadcast_to(row, (SUBLANES, row.shape[1])) - 15)


def exponent_rows(peaks):
    line = lax.broadcasted_iota(jnp.int32, (SUBLANES, peaks[0].shape[1]), 0)
    found = jnp.zeros(line.shape, jnp.int32)
    for k, peak in enumerate(peaks):
        found = jnp.where(line == k, exponent_of(jnp.max(peak, axis=0, keepdims=True)), found)
    return found


def pack_field(field_ref, word_ref, peaks):
    rhs, weeks, rows, lon = field_ref.shape
    half, parts = rows // 2, lon // LANES
    body = rhs * weeks * half
    tail = word_ref.shape[0] - parts * body
    line = lax.broadcasted_iota(jnp.int32, (tail, LANES), 0)
    kept = jnp.zeros((tail, LANES), jnp.int32)
    for k in range(rhs):
        exponent = exponent_of(jnp.max(peaks[k], axis=0, keepdims=True))
        for part in range(parts):
            own = exponent[:, part * LANES : (part + 1) * LANES]
            kept = jnp.where(line == k * parts + part, own, kept)
        factor = pow2(15 - jnp.broadcast_to(exponent, (SUBLANES, lon)))

        def one_week(week, carry):
            for start in range(0, half, SUBLANES):
                high = to_int(field_ref[k, week, start : start + SUBLANES, :], factor)
                low = to_int(field_ref[k, week, half + start : half + start + SUBLANES, :], factor)
                word = pack(high, low)
                for part in range(parts):
                    at = part * body + (k * weeks + week) * half + start
                    at = pl.multiple_of(at, SUBLANES)
                    word_ref[pl.ds(at, SUBLANES), :] = word[:, part * LANES : (part + 1) * LANES]
            return carry

        lax.fori_loop(0, weeks, one_week, 0)
    word_ref[parts * body :, :] = kept


def word_scale(word_ref, body, k):
    row = word_ref[body + k : body + k + 1, :] - 15
    return pow2(jnp.broadcast_to(row, (SUBLANES, row.shape[1])))


def lon_setup(lon):
    return lon / 32.0, (lon // 8 + 1).bit_length()


def lon_rows(rows, count, norm, lon):
    decay, bits = lon_setup(lon)
    fields = rows.shape[0] // SUBLANES
    count = jnp.concatenate([count] * fields, axis=0)
    windows = [rows, rows]
    taken = [jnp.zeros_like(rows)] * 2
    for bit in range(bits):
        reach = 2**bit
        fade = math.exp(-reach / decay)
        chosen = ((count >> bit) & 1) == 1
        for side in range(2):
            shift = reach if side == 0 else lon - reach
            moved = windows[side]
            if bit:
                moved = moved + fade * pltpu.roll(taken[side], shift, 1)
            taken[side] = jnp.where(chosen, moved, taken[side])
            if bit + 1 < bits:
                windows[side] = windows[side] + fade * pltpu.roll(windows[side], shift, 1)
    return (taken[0] + taken[1] - rows) * jnp.concatenate([norm] * fields, axis=0)


def lon_norm(count, lon):
    decay, _ = lon_setup(lon)
    ratio = math.exp(-2.0 / decay)
    ends = jnp.exp(count.astype(jnp.float32) * (-2.0 / decay))
    return 1.0 / jnp.sqrt(1.0 + (2.0 / (1.0 - ratio)) * (ratio - ends))


def lon_field(source_ref, count_ref, out_ref):
    rhs, weeks, rows, lon = out_ref.shape

    def one_group(group, peaks):
        at = pl.multiple_of(group * SUBLANES, SUBLANES)
        count = count_ref[pl.ds(at, SUBLANES), :]
        norm = lon_norm(count, lon)
        fields = [source_ref[k, w, pl.ds(at, SUBLANES), :] for k in range(rhs) for w in range(weeks)]
        result = lon_rows(jnp.concatenate(fields, axis=0), count, norm, lon)
        peaks = list(peaks)
        for k in range(rhs):
            for w in range(weeks):
                start = (k * weeks + w) * SUBLANES
                part = result[start : start + SUBLANES]
                out_ref[k, w, pl.ds(at, SUBLANES), :] = part
                peaks[k] = jnp.maximum(peaks[k], jnp.abs(part))
        return tuple(peaks)

    zero = jnp.zeros((SUBLANES, lon), jnp.float32)
    return lax.fori_loop(0, rows // SUBLANES, one_group, (zero,) * rhs)


def spread_lon_kernel(field_ref, count_ref, out_ref, word_ref):
    pack_field(out_ref, word_ref, lon_field(field_ref, count_ref, out_ref))


def spread_lon(field, counts):
    rhs, weeks, rows, lon = field.shape
    return pl.pallas_call(
        spread_lon_kernel,
        in_specs=in_vmem(2),
        out_specs=in_vmem(2),
        out_shape=[
            jax.ShapeDtypeStruct(field.shape, jnp.float32),
            jax.ShapeDtypeStruct(words_shape(rhs, weeks, rows, lon), jnp.int32),
        ],
        compiler_params=params(6),
        cost_estimate=cost(field.size * 100, field.size * 10),
        name="spread_lon",
    )(field, counts)


def lat_mix(side_ref, weights_ref, window_ref, k, week, pair_ref, own_ref, cross_ref, scales):
    rhs, weeks, rows, lon = own_ref.shape
    half = rows // 2
    body, parts = rhs * weeks * half, lon // LANES
    before = 2 * rows * (1 - side_ref[0])
    for base, ref, scale in (
        (before, pair_ref, scales[0]),
        (2 * rows - before, cross_ref, scales[1]),
    ):
        for start in range(0, half, SUBLANES):
            at = (k * weeks + week) * half + start
            word = words_at(ref, body, at, parts)
            for to, number in ((start, high_of(word)), (half + start, low_of(word))):
                to = pl.multiple_of(base + to, SUBLANES)
                window_ref[pl.ds(to, SUBLANES), :] = number.astype(jnp.float32) * scale
    window_ref[rows : 2 * rows, :] = own_ref[k, week]
    return jnp.dot(
        weights_ref[...],
        window_ref[...],
        precision=HIGHEST,
        preferred_element_type=jnp.float32,
    )


def spread_lat_kernel(slots, side_ref, own_ref, pair_ref, cross_ref, weights_ref, hot_ref, *rest):
    picks, (window_ref, cells_ref) = rest[:slots], rest[slots:]
    rhs, weeks, rows, lon = own_ref.shape
    parts = lon // LANES
    body = rhs * weeks * rows // 2
    for k in range(rhs):
        scales = [field_scale(ref, body, k, parts) for ref in (pair_ref, cross_ref)]
        for week in range(weeks):
            mixed = lat_mix(
                side_ref, weights_ref, window_ref, k, week, pair_ref, own_ref, cross_ref, scales
            )
            for part in range(parts):
                at = (week * parts + part) * rows
                cells_ref[at : at + rows, k * LANES : (k + 1) * LANES] = mixed[
                    :, part * LANES : (part + 1) * LANES
                ].astype(jnp.bfloat16)
    for slot in range(slots):
        found = jnp.dot(
            hot_ref[slot], cells_ref[...], preferred_element_type=jnp.float32
        ).astype(jnp.bfloat16)
        for k in range(rhs):
            picks[slot][k] = found[:, k * LANES : (k + 1) * LANES]


def spread_lat(side, own, pair, cross, weights, hot):
    rhs, weeks, rows, lon = own.shape
    slots, blocks, cols = hot.shape
    return pl.pallas_call(
        functools.partial(spread_lat_kernel, slots),
        in_specs=[pl.BlockSpec(memory_space=pltpu.SMEM)] + in_vmem(5),
        out_specs=in_vmem(slots),
        out_shape=[jax.ShapeDtypeStruct((rhs, blocks, LANES), jnp.bfloat16)] * slots,
        scratch_shapes=[
            pltpu.VMEM((3 * rows, lon), jnp.float32),
            pltpu.VMEM((cols, rhs * LANES), jnp.bfloat16),
        ],
        compiler_params=params(10),
        cost_estimate=cost(rhs * slots * blocks * cols * LANES * 2, rhs * weeks * rows * lon * 10),
        name="spread_lat",
    )(side, own, pair, cross, weights, hot)


def chunk_of(count, most):
    return max(size for size in range(1, most + 1) if count % size == 0)


def preload_kernel(first, after_ref, blocks_ref, out_ref, done):
    del after_ref
    parts = done.shape[0]
    size = out_ref.shape[0] // parts
    copies = [
        pltpu.make_async_copy(
            blocks_ref.at[pl.ds(first + part * size, size)],
            out_ref.at[pl.ds(part * size, size)],
            done.at[part],
        )
        for part in range(parts)
    ]
    for copy in copies:
        copy.start()
    for copy in copies:
        copy.wait()


def preload(blocks, first, count, after):
    parts = chunk_of(count, COPIES)
    shape = (count, *blocks.shape[1:])
    return pl.pallas_call(
        functools.partial(preload_kernel, first),
        in_specs=[pl.BlockSpec(memory_space=pl.ANY)] * 2,
        out_specs=pl.BlockSpec(memory_space=pltpu.VMEM),
        out_shape=jax.ShapeDtypeStruct(shape, blocks.dtype),
        scratch_shapes=[pltpu.SemaphoreType.DMA((parts,))],
        compiler_params=params(STREAM_MIB),
        cost_estimate=cost(0, count * blocks[0].size * 4),
        name="preload",
    )(after, blocks)


def forward_kernel(pieces, row_ref, scale_ref, *rest):
    pieces, picks, (out_ref, cells_ref) = rest[:pieces], rest[pieces:-2], rest[-2:]
    rhs, count, edge = picks[0].shape
    lines = len(picks) * rhs
    out_ref[...] = jnp.zeros_like(out_ref)
    for place, pick_ref in enumerate(picks):
        for k in range(rhs):
            cells_ref[pl.ds(place * rhs + k, count, stride=lines), :] = pick_ref[k].astype(
                jnp.float32
            )

    def one_chunk(piece_ref, first, chunk, step, carry):
        values = []
        for n in range(0, chunk, 2):
            index = step * chunk + n
            at = pl.multiple_of((first + index) * lines, 2 * lines)
            both = lax.dot_general(
                cells_ref[pl.ds(at, 2 * lines), :].astype(jnp.bfloat16),
                piece_ref[pl.ds(index, 2)].reshape(2 * edge, edge),
                (((1,), (1,)), ((), ())),
                preferred_element_type=jnp.float32,
            )
            values += [both[:lines, :edge], both[lines:, edge:]]
        for n in range(chunk):
            index = first + step * chunk + n
            at = pl.multiple_of(row_ref[index] * lines, lines)
            out_ref[pl.ds(at, lines), :] += values[n] * scale_ref[index]
        return carry

    over_chunks(pieces, one_chunk)


def over_chunks(pieces, one_chunk):
    first = 0
    for piece_ref in pieces:
        count = piece_ref.shape[0]
        chunk = 2 * chunk_of(count // 2, CHUNK // 2)
        lax.fori_loop(0, count // chunk, functools.partial(one_chunk, piece_ref, first, chunk), 0)
        first += count


def forward(row_list, scales, pieces, picks, row_blocks):
    rhs, count, edge = picks[0].shape
    lines = len(picks) * rhs
    return pl.pallas_call(
        functools.partial(forward_kernel, len(pieces)),
        in_specs=[pl.BlockSpec(memory_space=pltpu.SMEM)] * 2 + in_vmem(len(pieces) + len(picks)),
        out_specs=pl.BlockSpec(memory_space=pltpu.VMEM),
        out_shape=jax.ShapeDtypeStruct((row_blocks * lines, edge), jnp.float32),
        scratch_shapes=[pltpu.VMEM((count * lines, edge), jnp.float32)],
        compiler_params=params(15),
        cost_estimate=cost(count * edge**2 * 2 * lines, count * edge**2 * 2),
        name="forward",
    )(row_list, scales, *pieces, *picks)


def adjoint_kernel(pieces, rhs, row_ref, scale_ref, *rest):
    pieces, values_ref, outs, terms_ref = rest[:pieces], rest[pieces], rest[pieces + 1 : -1], rest[-1]
    lines = len(outs) * rhs
    edge = values_ref.shape[1]
    count = terms_ref.shape[0] // lines

    def one_chunk(piece_ref, first, chunk, step, carry):
        for n in range(0, chunk, 2):
            here = step * chunk + n
            index = first + here
            pulled = [
                values_ref[pl.ds(pl.multiple_of(row_ref[index + q] * lines, lines), lines), :]
                for q in range(2)
            ]
            both = jnp.dot(
                jnp.concatenate(pulled, axis=0).astype(jnp.bfloat16),
                jnp.concatenate([piece_ref[here + q] for q in range(2)], axis=1),
                preferred_element_type=jnp.float32,
            )
            for q in range(2):
                to = pl.multiple_of((index + q) * lines, lines)
                part = both[q * lines : (q + 1) * lines, q * edge : (q + 1) * edge]
                terms_ref[pl.ds(to, lines), :] = part * scale_ref[index + q]
        return carry

    over_chunks(pieces, one_chunk)
    half = count // 2
    for place, out_ref in enumerate(outs):
        terms = [terms_ref[pl.ds(place * rhs + k, count, stride=lines), :] for k in range(rhs)]
        exponents = exponent_rows([jnp.abs(term) for term in terms])
        out_ref[rhs * half :, :] = exponents
        for k in range(rhs):
            number = to_int(terms[k], pow2(15 - exponents[k : k + 1]))
            out_ref[k * half : (k + 1) * half, :] = pack(number[:half], number[half:])


def adjoint_terms(row_list, scales, pieces, values, outs, rhs):
    count = sum(piece.shape[0] for piece in pieces)
    edge = values.shape[1]
    lines = outs * rhs
    words = rhs * count // 2 + SUBLANES
    return pl.pallas_call(
        functools.partial(adjoint_kernel, len(pieces), rhs),
        in_specs=[pl.BlockSpec(memory_space=pltpu.SMEM)] * 2 + in_vmem(len(pieces) + 1),
        out_specs=in_vmem(outs),
        out_shape=[jax.ShapeDtypeStruct((words, edge), jnp.int32)] * outs,
        scratch_shapes=[pltpu.VMEM((count * lines, edge), jnp.float32)],
        compiler_params=params(15),
        cost_estimate=cost(count * edge**2 * 2 * lines, count * edge**2 * 2),
        name="adjoint",
    )(row_list, scales, *pieces, values)


def gather_cells_kernel(slots, hot_ref, *rest):
    terms, (field_ref, word_ref, split_ref) = rest[:slots], rest[slots:]
    rhs, weeks, rows, lon = field_ref.shape
    count = hot_ref.shape[1] // slots
    half = count // 2
    wide = rhs * LANES
    for slot in range(slots):
        for k in range(rhs):
            scale = word_scale(terms[slot], rhs * half, k)[:1]
            word = terms[slot][k * half : (k + 1) * half, :]
            for base, number in ((0, high_of(word)), (half, low_of(word))):
                coarse = (number + 128) >> 8
                fine = number - (coarse << 8)
                at = slot * count + base
                split_ref[at : at + half, k * LANES : (k + 1) * LANES] = (
                    (coarse << 8).astype(jnp.float32) * scale
                ).astype(jnp.bfloat16)
                split_ref[at : at + half, wide + k * LANES : wide + (k + 1) * LANES] = (
                    fine.astype(jnp.float32) * scale
                ).astype(jnp.bfloat16)
    peaks = [jnp.zeros((SUBLANES, lon), jnp.float32)] * rhs
    parts = lon // LANES
    for week in range(weeks):
        at = week * parts * rows
        both = jnp.dot(
            hot_ref[at : at + parts * rows, :],
            split_ref[...],
            preferred_element_type=jnp.float32,
        )
        cells = both[:, :wide] + both[:, wide:]
        for k in range(rhs):
            for part in range(parts):
                field_ref[k, week, :, part * LANES : (part + 1) * LANES] = cells[
                    part * rows : (part + 1) * rows, k * LANES : (k + 1) * LANES
                ]
            for start in range(0, rows, SUBLANES):
                peaks[k] = jnp.maximum(
                    peaks[k], jnp.abs(field_ref[k, week, start : start + SUBLANES, :])
                )
    pack_field(field_ref, word_ref, peaks)


def gather_cells(hot_turned, terms, rhs, weeks, rows, lon):
    slots = len(terms)
    return pl.pallas_call(
        functools.partial(gather_cells_kernel, slots),
        in_specs=in_vmem(1 + slots),
        out_specs=in_vmem(2),
        out_shape=[
            jax.ShapeDtypeStruct((rhs, weeks, rows, lon), jnp.float32),
            jax.ShapeDtypeStruct(words_shape(rhs, weeks, rows, lon), jnp.int32),
        ],
        scratch_shapes=[pltpu.VMEM((hot_turned.shape[1], 2 * rhs * LANES), jnp.bfloat16)],
        compiler_params=params(12),
        cost_estimate=cost(rhs * hot_turned.size * 4 * LANES, rhs * weeks * rows * lon * 10),
        name="gather_cells",
    )(hot_turned, *terms)


def pull_back_kernel(
    side_ref, own_ref, pair_ref, cross_ref, weights_ref, count_ref, word_ref, window_ref, field_ref
):
    rhs, weeks, rows, lon = own_ref.shape
    parts = lon // LANES
    body = rhs * weeks * rows // 2
    for k in range(rhs):
        scales = [field_scale(ref, body, k, parts) for ref in (pair_ref, cross_ref)]
        for week in range(weeks):
            field_ref[k, week] = lat_mix(
                side_ref, weights_ref, window_ref, k, week, pair_ref, own_ref, cross_ref, scales
            )
    pack_field(field_ref, word_ref, lon_field(field_ref, count_ref, field_ref))


def pull_back(side, own, pair, cross, weights, counts):
    rhs, weeks, rows, lon = own.shape
    return pl.pallas_call(
        pull_back_kernel,
        in_specs=[pl.BlockSpec(memory_space=pltpu.SMEM)] + in_vmem(5),
        out_specs=pl.BlockSpec(memory_space=pltpu.VMEM),
        out_shape=jax.ShapeDtypeStruct(pair.shape, jnp.int32),
        scratch_shapes=[
            pltpu.VMEM((3 * rows, lon), jnp.float32),
            pltpu.VMEM((rhs, weeks, rows, lon), jnp.float32),
        ],
        compiler_params=params(8),
        cost_estimate=cost(rhs * weeks * rows * lon * 300, rhs * weeks * rows * lon * 10),
        name="pull_back",
    )(side, own, pair, cross, weights, counts)


def gram_kernel(places, count, rhs, order_ref, sums_before, residual_ref, direction_ref, *rest):
    words, (image_ref, gram_ref, sums_ref) = rest[:count], rest[-3:]
    rhs_count, weeks, rows, lon = direction_ref.shape
    half = rows // 2
    body, parts = rhs * weeks * half, lon // LANES
    old_places, new_places = places[:-count], places[-count:]
    for word_ref, place in zip(words, new_places):
        for k in range(rhs):
            index = order_ref[place] + k
            scale = field_scale(word_ref, body, k, parts)

            def one_week(week, carry):
                for start in range(0, half, SUBLANES):
                    word = words_at(word_ref, body, (k * weeks + week) * half + start, parts)
                    for base, number in ((start, high_of(word)), (half + start, low_of(word))):
                        image_ref[index, week, base : base + SUBLANES, :] = (
                            direction_ref[index, week, base : base + SUBLANES, :]
                            + number.astype(jnp.float32) * scale
                        )
                return carry

            lax.fori_loop(0, weeks, one_week, 0)

    sums_ref[...] = jnp.zeros_like(sums_ref)
    row_groups = rows // SUBLANES

    def tile(blocks):
        def one_week(week, sums):
            sums = list(sums)
            for row in range(0, rows, SUBLANES):
                for lane in range(0, lon, LANES):
                    spot = (week, slice(row, row + SUBLANES), slice(lane, lane + LANES))
                    place = 0
                    for _, lefts, rights, _ in blocks:
                        right = [ref[(k, *spot)] for ref, k, _ in rights]
                        for ref, k, _ in lefts:
                            left = ref[(k, *spot)]
                            for b in range(len(rights)):
                                sums[place] = sums[place] + left * right[b]
                                place += 1
            return tuple(sums)

        zero = jnp.zeros((SUBLANES, LANES), jnp.float32)
        total = sum(len(lefts) * len(rights) for _, lefts, rights, _ in blocks)
        sums = list(lax.fori_loop(0, weeks, one_week, (zero,) * total))
        for index, lefts, rights, mirror in blocks:
            for _, _, row in lefts:
                for _, _, column in rights:
                    lanes = jnp.sum(sums.pop(0), axis=0, keepdims=True)
                    for row_at, column_at in ((row, column), (column, row))[: 1 + mirror]:
                        at = (index * rhs_count + row_at) * rhs_count + column_at
                        sums_ref[pl.ds(at, 1), :] = lanes

    def listed(places):
        found = [order_ref[place] + k for place in places for k in range(rhs)]
        return [(image_ref, index, index) for index in found]

    residuals = [(residual_ref, k, k) for k in range(rhs_count)]
    directions = [(direction_ref, k, k) for k in range(rhs_count)]
    images = listed(new_places)
    if not old_places:
        for a in range(rhs_count):
            tile([(0, residuals[a : a + 1], residuals[a:], True)])
    for b in range(0, len(images), 2):
        right = images[b : b + 2]
        left = images[: b + len(right)] + listed(old_places)
        tile([(1, directions, right, False), (2, residuals, right, False), (3, left, right, True)])

    gram_ref[...] = sums_before[...] + lax.dot_general(
        jnp.ones((SUBLANES, LANES), jnp.float32),
        sums_ref[...],
        (((1,), (1,)), ((), ())),
        precision=HIGHEST,
        preferred_element_type=jnp.float32,
    )


def grams(order, places, sums, residual, direction, words, rhs, images):
    rhs_count, weeks, rows, lon = direction.shape
    total = 4 * rhs_count**2
    count = len(words)
    return pl.pallas_call(
        functools.partial(gram_kernel, places, count, rhs),
        in_specs=[pl.BlockSpec(memory_space=pltpu.SMEM)] + in_vmem(3 + count + len(images)),
        out_specs=in_vmem(2),
        out_shape=[
            jax.ShapeDtypeStruct(direction.shape, jnp.float32),
            jax.ShapeDtypeStruct((SUBLANES, total), jnp.float32),
        ],
        scratch_shapes=[pltpu.VMEM((total, LANES), jnp.float32)],
        input_output_aliases={4 + count: 0} if images else {},
        compiler_params=params(14),
        cost_estimate=cost(8 * rhs_count * direction.size, 16 * direction.size),
        name="grams",
    )(order, sums, residual, direction, *words, *images)


def small_product(left, right):
    total = jnp.zeros((SUBLANES, LANES), jnp.float32)
    for j in range(SUBLANES):
        column = jnp.broadcast_to(left[:, j : j + 1], (SUBLANES, LANES))
        total = total + column * jnp.broadcast_to(right[j : j + 1, :], (SUBLANES, LANES))
    return total


def small_transpose(value):
    rest = jnp.zeros((LANES - SUBLANES, LANES), jnp.float32)
    return jnp.concatenate([value, rest], axis=0).T[:SUBLANES]


def small_solves(systems):
    line = lax.broadcasted_iota(jnp.int32, (SUBLANES, LANES), 0)
    lane = lax.broadcasted_iota(jnp.int32, (SUBLANES, LANES), 1)
    states = [matrix + pltpu.roll(right, SUBLANES, 1) for matrix, right in systems]
    for j in range(SUBLANES):
        for index, both in enumerate(states):
            column = jnp.broadcast_to(both[:, j : j + 1], (SUBLANES, LANES))
            pivot = jnp.broadcast_to(both[j : j + 1, :], (SUBLANES, LANES))
            scaled = pivot / jnp.broadcast_to(both[j : j + 1, j : j + 1], (SUBLANES, LANES))
            states[index] = jnp.where(line == j, scaled, both - column * scaled)
    return [
        jnp.where(lane < SUBLANES, pltpu.roll(both, LANES - SUBLANES, 1), 0.0) for both in states
    ]


def solve_steps(sums_ref):
    total = sums_ref.shape[1]
    size = SUBLANES
    place = lax.broadcasted_iota(jnp.int32, (size, total), 1)
    line = lax.broadcasted_iota(jnp.int32, (size, total), 0)
    spot = lax.broadcasted_iota(jnp.int32, (total, LANES), 0)
    lane = lax.broadcasted_iota(jnp.int32, (total, LANES), 1)
    sums = sums_ref[...]

    def matrix(index, turned=False):
        row, column = place % size, spot // size % size
        if not turned:
            row, column = place // size % size, spot % size
        here = (place // size**2 == index) & (row == line)
        return jnp.dot(
            jnp.where(here, sums, 0.0),
            jnp.where(column == lane, 1.0, 0.0),
            precision=HIGHEST,
            preferred_element_type=jnp.float32,
        )

    gram_old, gram_image = matrix(0), matrix(3)
    curvature = 0.5 * (matrix(1) + matrix(1, True))
    mixed, mixed_turned = matrix(2), matrix(2, True)
    diagonal = lax.broadcasted_iota(jnp.int32, (size, LANES), 0)
    identity = jnp.where(diagonal == lax.broadcasted_iota(jnp.int32, (size, LANES), 1), 1.0, 0.0)
    step, old_inverse = small_solves([(curvature, gram_old), (gram_old, identity)])
    step_turned = small_transpose(step)
    rest = small_product(gram_image, step) - mixed_turned
    gram_new = gram_old - small_product(mixed, step) + small_product(step_turned, rest)
    return step_turned, small_product(gram_new, old_inverse)


def spread_coefficients(turned):
    size = SUBLANES
    wide = 4 * size**2
    lane = lax.broadcasted_iota(jnp.int32, (size, wide), 1)
    line = lax.broadcasted_iota(jnp.int32, (size, wide), 0)
    spread = jnp.zeros((size, wide), jnp.float32)
    for b in range(size):
        column = jnp.broadcast_to(turned[:, b : b + 1], (size, wide))
        spread = spread + jnp.where(lane // size % size == b, column, 0.0)
    high = spread.astype(jnp.bfloat16).astype(jnp.float32)
    spread = jnp.where(lane < 2 * size**2, high, spread - high)
    own = (lane % size == line) & (lane < 3 * size**2)
    rows = [
        jnp.where(own, jnp.broadcast_to(spread[a : a + 1], (size, wide)), 0.0) for a in range(size)
    ]
    return jnp.concatenate(rows, axis=0)


def split_rows(ref, row):
    value = jnp.concatenate([ref[b, 0, row : row + SUBLANES, :] for b in range(ref.shape[0])], axis=0)
    high = value.astype(jnp.bfloat16)
    low = (value - high.astype(jnp.float32)).astype(jnp.bfloat16)
    return jnp.concatenate([high, low, high], axis=0)


def update_kernel(
    sums_ref, solution_ref, residual_ref, direction_ref, image_ref, sol_out, res_out, dir_out, coef_ref
):
    rhs_count, _, rows, lon = direction_ref.shape
    size = rhs_count * SUBLANES

    @pl.when(pl.program_id(0) == 0)
    def _():
        step_turned, turn_turned = solve_steps(sums_ref)
        coefs = [spread_coefficients(step_turned), spread_coefficients(turn_turned)]
        coef_ref[...] = jnp.concatenate(coefs, axis=0).astype(jnp.bfloat16)

    for row in range(0, rows, SUBLANES):
        coefs = coef_ref[:, : 3 * size]
        moves = jnp.dot(coefs, split_rows(direction_ref, row), preferred_element_type=jnp.float32)
        drops = jnp.dot(coefs[:size], split_rows(image_ref, row), preferred_element_type=jnp.float32)
        for a in range(rhs_count):
            at = a * SUBLANES
            spot = (a, 0, slice(row, row + SUBLANES), slice(None))
            sol_out[spot] = solution_ref[spot] + moves[at : at + SUBLANES]
            left = residual_ref[spot] - drops[at : at + SUBLANES]
            res_out[spot] = left
            dir_out[spot] = left + moves[size + at : size + at + SUBLANES]


def update(sums, solution, residual, direction, image):
    rhs_count, weeks, rows, lon = direction.shape
    field = pl.BlockSpec((rhs_count, 1, rows, lon), lambda w: (0, w, 0, 0))
    shape = jax.ShapeDtypeStruct(direction.shape, jnp.float32)
    return pl.pallas_call(
        update_kernel,
        grid=(weeks,),
        in_specs=[whole(sums.shape)] + [field] * 4,
        out_specs=[field] * 3,
        scratch_shapes=[pltpu.VMEM((2 * rhs_count * SUBLANES, 4 * rhs_count * SUBLANES), jnp.bfloat16)],
        out_shape=[shape] * 3,
        compiler_params=params(16),
        cost_estimate=cost(6 * rhs_count * direction.size, 28 * direction.size),
        name="update",
    )(sums, solution, residual, direction, image)


def crossed(value, axis, by):
    if by == 0:
        return value
    return lax.ppermute(value, axis, [(i, i ^ by) for i in range(lax.axis_size(axis))])


def far_first(size):
    return [1 << bit for bit in reversed(range(size.bit_length() - 1))]


def neighbours(value, axis):
    size = lax.axis_size(axis)
    outer = [(i, i + 1) for i in range(1, size - 1, 2)]
    outer += [(after, before) for before, after in outer]
    return crossed(value, axis, 1), lax.ppermute(value, axis, outer)


def summed_over(value, axis):
    bits = far_first(lax.axis_size(axis))[::-1]
    before = value
    for step in [bits[:1]] + [bits[at : at + 2] for at in range(1, len(bits), 2)]:
        before = value
        for reach in step[:1]:
            value = value + crossed(before, axis, reach)
        for reach in step[1:]:
            far = crossed(before, axis, reach) + crossed(before, axis, reach | step[0])
            value = value + far
    return value, before


def lat_windows(lat_width, band, rows):
    decay = rows / 2.0
    total = lat_width.shape[0]
    offsets = jnp.abs(jnp.arange(-rows, rows + 1)).astype(jnp.float32)
    limits = lat_width.astype(jnp.float32)
    normal = jnp.sqrt(
        jnp.sum(
            jnp.where(
                offsets[None, :] <= limits[:, None], jnp.exp(-2.0 * offsets / decay)[None, :], 0.0
            ),
            axis=1,
        )
    )
    padded_limits = jnp.pad(limits, (rows, rows), constant_values=-1.0)
    padded_normal = jnp.pad(normal, (rows, rows), constant_values=1.0)
    near_limits = lax.dynamic_slice_in_dim(padded_limits, band * rows, 3 * rows)
    near_normal = lax.dynamic_slice_in_dim(padded_normal, band * rows, 3 * rows)
    distance = jnp.abs(
        jnp.arange(rows)[:, None] + rows - jnp.arange(3 * rows)[None, :]
    ).astype(jnp.float32)
    fade = jnp.exp(-distance / decay)
    own_limits, own_normal = near_limits[rows : 2 * rows, None], near_normal[rows : 2 * rows, None]
    spread = jnp.where(distance <= own_limits, fade, 0.0) / own_normal
    pulled = jnp.where(distance <= near_limits[None, :], fade, 0.0) / near_normal[None, :]
    return spread, pulled


def shards(
    footprints,
    block_rows,
    block_cols,
    block_scale,
    lat_width,
    lon_width,
    obs_weight,
    solution,
    residual,
    direction,
):
    rhs_count, weeks, rows, lon = direction.shape
    blocks = footprints[0, 0]
    count, edge, _ = blocks.shape
    row_list = block_rows[0, 0]
    scales = jnp.exp2(-block_scale[0, 0].astype(jnp.float32))
    row_blocks = obs_weight.shape[0] // edge
    slots = lax.axis_size("obs")
    rhs = rhs_count // slots
    slab, band = lax.axis_index("obs"), lax.axis_index("lat")
    parts = lon // edge
    cols = weeks * rows * parts

    groups = chunk_of(rhs, BACK_GROUPS)
    each = rhs // groups
    order = (slab ^ jnp.arange(slots, dtype=jnp.int32)) * rhs
    own_width = lax.dynamic_slice_in_dim(lon_width, band * rows, rows)
    counts = jnp.broadcast_to(own_width[:, None] + 1, (rows, lon))

    lists = jnp.concatenate([crossed(block_cols, "obs", d) for d in range(slots)], axis=0)[:, 0]
    line, part = lists // parts, lists % parts
    places = ((line // rows) * parts + part) * rows + line % rows

    lon_own, words = spread_lon(
        lax.dynamic_slice_in_dim(direction, slab * rhs, rhs, 0), counts
    )
    halo = neighbours(words, "lat")
    hot = (places[:, :, None] == jnp.arange(cols)[None, None, :]).astype(jnp.bfloat16)
    hot_turned = (jnp.arange(cols)[:, None] == places.reshape(1, -1)).astype(jnp.bfloat16)
    lat_spread, lat_pulled = lat_windows(lat_width, band, rows)
    side = (band % 2).astype(jnp.int32).reshape(1)

    picks = spread_lat(side, lon_own, *halo, lat_spread, hot)
    cells = [crossed(picks[d], "obs", d) for d in range(slots)]
    kept = count // KEPT_OF * KEPT if count % KEPT_OF == 0 else 0
    stays = [preload(blocks, 0, kept, picks[0])] if kept else []
    near = preload(blocks, kept, count - kept, picks[0])
    sums, partial = summed_over(
        forward(row_list, scales, [*stays, near], cells, row_blocks), "lat"
    )
    near = preload(blocks, kept, count - kept, partial)
    weighted = sums.reshape(row_blocks, slots * rhs, edge) * obs_weight.reshape(row_blocks, 1, edge)
    terms = adjoint_terms(
        row_list, scales, [*stays, near], weighted.reshape(-1, edge), slots * groups, each
    )
    sent = [[crossed(terms[d * groups + g], "obs", d) for d in range(slots)] for g in range(groups)]
    own = []
    for group in range(groups):
        field, words = gather_cells(hot_turned, sent[group], each, weeks, rows, lon)
        own.append(pull_back(side, field, *neighbours(words, "lat"), lat_pulled, counts))

    starts = (order[:, None] + jnp.arange(groups, dtype=jnp.int32) * each).reshape(-1)
    products = jnp.zeros((SUBLANES, 4 * rhs_count**2), jnp.float32)
    images, places = [], ()

    def add_products(slot):
        nonlocal products, places, images
        words = [arrived[group][slot] for group in range(groups)]
        places += tuple(slot * groups + group for group in range(groups))
        *images, products = grams(
            starts, places, products, residual, direction, words, each, images
        )

    arrived = [{0: words} for words in own]
    for group in range(groups):
        for reach in far_first(slots):
            arrived[group][reach] = crossed(own[group], "obs", reach)
    add_products(0)
    first_products = products
    for reach in far_first(slots)[1:]:
        for group in range(groups):
            for bits in [bits for bits in arrived[group] if bits > reach and not bits % (2 * reach)]:
                words = arrived[group][bits]
                if group == groups - 1:
                    words, _ = lax.optimization_barrier((words, first_products))
                arrived[group][bits | reach] = crossed(words, "obs", reach)
    for slot in range(1, slots):
        add_products(slot)
    products, _ = summed_over(products, "lat")
    return tuple(update(products, solution, residual, direction, *images))


def solution(mesh):
    return jax.shard_map(
        shards,
        mesh=mesh,
        in_specs=(
            P("obs", "lat", None, None, None),
            P("obs", "lat", None),
            P("obs", "lat", None),
            P("obs", "lat", None),
            P(),
            P(),
            P("obs"),
            P(None, None, "lat", None),
            P(None, None, "lat", None),
            P(None, None, "lat", None),
        ),
        out_specs=(
            P(None, None, "lat", None),
            P(None, None, "lat", None),
            P(None, None, "lat", None),
        ),
        check_vma=False,
    )
```

```python
import functools
import math

import jax
import jax.numpy as jnp
from jax import lax
from jax.experimental import pallas as pl
from jax.experimental.pallas import tpu as pltpu
from jax.sharding import PartitionSpec as P

LANES = 128
CHUNK = 96
COPIES = 12
STREAM_MIB = 40
KEPT, KEPT_OF = 1, 2
BACK_GROUPS = 2
SUBLANES = 8
MIB = 1024 * 1024
HIGHEST = lax.Precision.HIGHEST


def params(mib):
    return pltpu.CompilerParams(vmem_limit_bytes=mib * MIB)


def cost(flops, nbytes):
    return pl.CostEstimate(flops=int(flops), bytes_accessed=int(nbytes), transcendentals=0)


def whole(shape):
    return pl.BlockSpec(shape, lambda *_: (0,) * len(shape), pipeline_mode=pl.Buffered(1))


def in_vmem(count):
    return [pl.BlockSpec(memory_space=pltpu.VMEM)] * count


def pow2(exponent):
    size = jnp.abs(exponent)
    up = jnp.ones(exponent.shape, jnp.float32)
    down = up
    for bit in range(7):
        on = ((size >> bit) & 1) == 1
        up = up * jnp.where(on, 2.0 ** (2**bit), 1.0)
        down = down * jnp.where(on, 2.0 ** -(2**bit), 1.0)
    return jnp.where(exponent < 0, down, up)


def exponent_of(peak):
    logs = jnp.log(jnp.maximum(peak, 1e-28)) * (1.0 / math.log(2.0))
    return jnp.ceil(logs + 1e-3).astype(jnp.int32)


def to_int(values, factor):
    return jnp.clip(jnp.round(values * factor), -32767.0, 32767.0).astype(jnp.int32)


def pack(high, low):
    return (high << 16) | (low & 0xFFFF)


def high_of(word):
    return word >> 16


def low_of(word):
    return (word << 16) >> 16


def words_shape(rhs, weeks, rows, lon):
    parts = lon // LANES
    tail = -(-rhs * parts // SUBLANES) * SUBLANES
    return parts * (rhs * weeks * rows // 2) + tail, LANES


def words_at(word_ref, body, at, parts):
    found = []
    for part in range(parts):
        start = part * body + at
        if not isinstance(start, int):
            start = pl.multiple_of(start, SUBLANES)
        found.append(word_ref[pl.ds(start, SUBLANES), :])
    return jnp.concatenate(found, axis=1)


def field_scale(word_ref, body, k, parts):
    first = parts * (body + k)
    row = jnp.concatenate(
        [word_ref[first + part : first + part + 1, :] for part in range(parts)], axis=1
    )
    return pow2(jnp.broadcast_to(row, (SUBLANES, row.shape[1])) - 15)


def exponent_rows(peaks):
    line = lax.broadcasted_iota(jnp.int32, (SUBLANES, peaks[0].shape[1]), 0)
    found = jnp.zeros(line.shape, jnp.int32)
    for k, peak in enumerate(peaks):
        found = jnp.where(line == k, exponent_of(jnp.max(peak, axis=0, keepdims=True)), found)
    return found


def pack_field(field_ref, word_ref, peaks):
    rhs, weeks, rows, lon = field_ref.shape
    half, parts = rows // 2, lon // LANES
    body = rhs * weeks * half
    tail = word_ref.shape[0] - parts * body
    line = lax.broadcasted_iota(jnp.int32, (tail, LANES), 0)
    kept = jnp.zeros((tail, LANES), jnp.int32)
    for k in range(rhs):
        exponent = exponent_of(jnp.max(peaks[k], axis=0, keepdims=True))
        for part in range(parts):
            own = exponent[:, part * LANES : (part + 1) * LANES]
            kept = jnp.where(line == k * parts + part, own, kept)
        factor = pow2(15 - jnp.broadcast_to(exponent, (SUBLANES, lon)))

        def one_week(week, carry):
            for start in range(0, half, SUBLANES):
                high = to_int(field_ref[k, week, start : start + SUBLANES, :], factor)
                low = to_int(field_ref[k, week, half + start : half + start + SUBLANES, :], factor)
                word = pack(high, low)
                for part in range(parts):
                    at = part * body + (k * weeks + week) * half + start
                    at = pl.multiple_of(at, SUBLANES)
                    word_ref[pl.ds(at, SUBLANES), :] = word[:, part * LANES : (part + 1) * LANES]
            return carry

        lax.fori_loop(0, weeks, one_week, 0)
    word_ref[parts * body :, :] = kept


def word_scale(word_ref, body, k):
    row = word_ref[body + k : body + k + 1, :] - 15
    return pow2(jnp.broadcast_to(row, (SUBLANES, row.shape[1])))


def lon_setup(lon):
    return lon / 32.0, (lon // 8 + 1).bit_length()


def lon_rows(rows, count, norm, lon):
    decay, bits = lon_setup(lon)
    fields = rows.shape[0] // SUBLANES
    count = jnp.concatenate([count] * fields, axis=0)
    windows = [rows, rows]
    taken = [jnp.zeros_like(rows)] * 2
    for bit in range(bits):
        reach = 2**bit
        fade = math.exp(-reach / decay)
        chosen = ((count >> bit) & 1) == 1
        for side in range(2):
            shift = reach if side == 0 else lon - reach
            moved = windows[side]
            if bit:
                moved = moved + fade * pltpu.roll(taken[side], shift, 1)
            taken[side] = jnp.where(chosen, moved, taken[side])
            if bit + 1 < bits:
                windows[side] = windows[side] + fade * pltpu.roll(windows[side], shift, 1)
    return (taken[0] + taken[1] - rows) * jnp.concatenate([norm] * fields, axis=0)


def lon_norm(count, lon):
    decay, _ = lon_setup(lon)
    ratio = math.exp(-2.0 / decay)
    ends = jnp.exp(count.astype(jnp.float32) * (-2.0 / decay))
    return 1.0 / jnp.sqrt(1.0 + (2.0 / (1.0 - ratio)) * (ratio - ends))


def lon_field(source_ref, count_ref, out_ref):
    rhs, weeks, rows, lon = out_ref.shape

    def one_group(group, peaks):
        at = pl.multiple_of(group * SUBLANES, SUBLANES)
        count = count_ref[pl.ds(at, SUBLANES), :]
        norm = lon_norm(count, lon)
        fields = [source_ref[k, w, pl.ds(at, SUBLANES), :] for k in range(rhs) for w in range(weeks)]
        result = lon_rows(jnp.concatenate(fields, axis=0), count, norm, lon)
        peaks = list(peaks)
        for k in range(rhs):
            for w in range(weeks):
                start = (k * weeks + w) * SUBLANES
                part = result[start : start + SUBLANES]
                out_ref[k, w, pl.ds(at, SUBLANES), :] = part
                peaks[k] = jnp.maximum(peaks[k], jnp.abs(part))
        return tuple(peaks)

    zero = jnp.zeros((SUBLANES, lon), jnp.float32)
    return lax.fori_loop(0, rows // SUBLANES, one_group, (zero,) * rhs)


def spread_lon_kernel(field_ref, count_ref, out_ref, word_ref):
    pack_field(out_ref, word_ref, lon_field(field_ref, count_ref, out_ref))


def spread_lon(field, counts):
    rhs, weeks, rows, lon = field.shape
    return pl.pallas_call(
        spread_lon_kernel,
        in_specs=in_vmem(2),
        out_specs=in_vmem(2),
        out_shape=[
            jax.ShapeDtypeStruct(field.shape, jnp.float32),
            jax.ShapeDtypeStruct(words_shape(rhs, weeks, rows, lon), jnp.int32),
        ],
        compiler_params=params(6),
        cost_estimate=cost(field.size * 100, field.size * 10),
        name="spread_lon",
    )(field, counts)


def lat_mix(side_ref, weights_ref, window_ref, k, week, pair_ref, own_ref, cross_ref, scales):
    rhs, weeks, rows, lon = own_ref.shape
    half = rows // 2
    body, parts = rhs * weeks * half, lon // LANES
    before = 2 * rows * (1 - side_ref[0])
    for base, ref, scale in (
        (before, pair_ref, scales[0]),
        (2 * rows - before, cross_ref, scales[1]),
    ):
        for start in range(0, half, SUBLANES):
            at = (k * weeks + week) * half + start
            word = words_at(ref, body, at, parts)
            for to, number in ((start, high_of(word)), (half + start, low_of(word))):
                to = pl.multiple_of(base + to, SUBLANES)
                window_ref[pl.ds(to, SUBLANES), :] = number.astype(jnp.float32) * scale
    window_ref[rows : 2 * rows, :] = own_ref[k, week]
    return jnp.dot(
        weights_ref[...],
        window_ref[...],
        precision=HIGHEST,
        preferred_element_type=jnp.float32,
    )


def spread_lat_kernel(slots, side_ref, own_ref, pair_ref, cross_ref, weights_ref, hot_ref, *rest):
    picks, (window_ref, cells_ref) = rest[:slots], rest[slots:]
    rhs, weeks, rows, lon = own_ref.shape
    parts = lon // LANES
    body = rhs * weeks * rows // 2
    for k in range(rhs):
        scales = [field_scale(ref, body, k, parts) for ref in (pair_ref, cross_ref)]
        for week in range(weeks):
            mixed = lat_mix(
                side_ref, weights_ref, window_ref, k, week, pair_ref, own_ref, cross_ref, scales
            )
            for part in range(parts):
                at = (week * parts + part) * rows
                cells_ref[at : at + rows, k * LANES : (k + 1) * LANES] = mixed[
                    :, part * LANES : (part + 1) * LANES
                ].astype(jnp.bfloat16)
    for slot in range(slots):
        found = jnp.dot(
            hot_ref[slot], cells_ref[...], preferred_element_type=jnp.float32
        ).astype(jnp.bfloat16)
        for k in range(rhs):
            picks[slot][k] = found[:, k * LANES : (k + 1) * LANES]


def spread_lat(side, own, pair, cross, weights, hot):
    rhs, weeks, rows, lon = own.shape
    slots, blocks, cols = hot.shape
    return pl.pallas_call(
        functools.partial(spread_lat_kernel, slots),
        in_specs=[pl.BlockSpec(memory_space=pltpu.SMEM)] + in_vmem(5),
        out_specs=in_vmem(slots),
        out_shape=[jax.ShapeDtypeStruct((rhs, blocks, LANES), jnp.bfloat16)] * slots,
        scratch_shapes=[
            pltpu.VMEM((3 * rows, lon), jnp.float32),
            pltpu.VMEM((cols, rhs * LANES), jnp.bfloat16),
        ],
        compiler_params=params(10),
        cost_estimate=cost(rhs * slots * blocks * cols * LANES * 2, rhs * weeks * rows * lon * 10),
        name="spread_lat",
    )(side, own, pair, cross, weights, hot)


def chunk_of(count, most):
    return max(size for size in range(1, most + 1) if count % size == 0)


def preload_kernel(first, after_ref, blocks_ref, out_ref, done):
    del after_ref
    parts = done.shape[0]
    size = out_ref.shape[0] // parts
    copies = [
        pltpu.make_async_copy(
            blocks_ref.at[pl.ds(first + part * size, size)],
            out_ref.at[pl.ds(part * size, size)],
            done.at[part],
        )
        for part in range(parts)
    ]
    for copy in copies:
        copy.start()
    for copy in copies:
        copy.wait()


def preload(blocks, first, count, after):
    parts = chunk_of(count, COPIES)
    shape = (count, *blocks.shape[1:])
    return pl.pallas_call(
        functools.partial(preload_kernel, first),
        in_specs=[pl.BlockSpec(memory_space=pl.ANY)] * 2,
        out_specs=pl.BlockSpec(memory_space=pltpu.VMEM),
        out_shape=jax.ShapeDtypeStruct(shape, blocks.dtype),
        scratch_shapes=[pltpu.SemaphoreType.DMA((parts,))],
        compiler_params=params(STREAM_MIB),
        cost_estimate=cost(0, count * blocks[0].size * 4),
        name="preload",
    )(after, blocks)


def forward_kernel(pieces, row_ref, scale_ref, *rest):
    pieces, picks, (out_ref, cells_ref) = rest[:pieces], rest[pieces:-2], rest[-2:]
    rhs, count, edge = picks[0].shape
    lines = len(picks) * rhs
    out_ref[...] = jnp.zeros_like(out_ref)
    for place, pick_ref in enumerate(picks):
        for k in range(rhs):
            cells_ref[pl.ds(place * rhs + k, count, stride=lines), :] = pick_ref[k].astype(
                jnp.float32
            )

    def one_chunk(piece_ref, first, chunk, step, carry):
        values = []
        for n in range(0, chunk, 2):
            index = step * chunk + n
            at = pl.multiple_of((first + index) * lines, 2 * lines)
            both = lax.dot_general(
                cells_ref[pl.ds(at, 2 * lines), :].astype(jnp.bfloat16),
                piece_ref[pl.ds(index, 2)].reshape(2 * edge, edge),
                (((1,), (1,)), ((), ())),
                preferred_element_type=jnp.float32,
            )
            values += [both[:lines, :edge], both[lines:, edge:]]
        for n in range(chunk):
            index = first + step * chunk + n
            at = pl.multiple_of(row_ref[index] * lines, lines)
            out_ref[pl.ds(at, lines), :] += values[n] * scale_ref[index]
        return carry

    over_chunks(pieces, one_chunk)


def over_chunks(pieces, one_chunk):
    first = 0
    for piece_ref in pieces:
        count = piece_ref.shape[0]
        chunk = 2 * chunk_of(count // 2, CHUNK // 2)
        lax.fori_loop(0, count // chunk, functools.partial(one_chunk, piece_ref, first, chunk), 0)
        first += count


def forward(row_list, scales, pieces, picks, row_blocks):
    rhs, count, edge = picks[0].shape
    lines = len(picks) * rhs
    return pl.pallas_call(
        functools.partial(forward_kernel, len(pieces)),
        in_specs=[pl.BlockSpec(memory_space=pltpu.SMEM)] * 2 + in_vmem(len(pieces) + len(picks)),
        out_specs=pl.BlockSpec(memory_space=pltpu.VMEM),
        out_shape=jax.ShapeDtypeStruct((row_blocks * lines, edge), jnp.float32),
        scratch_shapes=[pltpu.VMEM((count * lines, edge), jnp.float32)],
        compiler_params=params(15),
        cost_estimate=cost(count * edge**2 * 2 * lines, count * edge**2 * 2),
        name="forward",
    )(row_list, scales, *pieces, *picks)


def adjoint_kernel(pieces, rhs, row_ref, scale_ref, *rest):
    pieces, values_ref, outs, terms_ref = rest[:pieces], rest[pieces], rest[pieces + 1 : -1], rest[-1]
    lines = len(outs) * rhs
    edge = values_ref.shape[1]
    count = terms_ref.shape[0] // lines

    def one_chunk(piece_ref, first, chunk, step, carry):
        for n in range(0, chunk, 2):
            here = step * chunk + n
            index = first + here
            pulled = [
                values_ref[pl.ds(pl.multiple_of(row_ref[index + q] * lines, lines), lines), :]
                for q in range(2)
            ]
            both = jnp.dot(
                jnp.concatenate(pulled, axis=0).astype(jnp.bfloat16),
                jnp.concatenate([piece_ref[here + q] for q in range(2)], axis=1),
                preferred_element_type=jnp.float32,
            )
            for q in range(2):
                to = pl.multiple_of((index + q) * lines, lines)
                part = both[q * lines : (q + 1) * lines, q * edge : (q + 1) * edge]
                terms_ref[pl.ds(to, lines), :] = part * scale_ref[index + q]
        return carry

    over_chunks(pieces, one_chunk)
    half = count // 2
    for place, out_ref in enumerate(outs):
        terms = [terms_ref[pl.ds(place * rhs + k, count, stride=lines), :] for k in range(rhs)]
        exponents = exponent_rows([jnp.abs(term) for term in terms])
        out_ref[rhs * half :, :] = exponents
        for k in range(rhs):
            number = to_int(terms[k], pow2(15 - exponents[k : k + 1]))
            out_ref[k * half : (k + 1) * half, :] = pack(number[:half], number[half:])


def adjoint_terms(row_list, scales, pieces, values, outs, rhs):
    count = sum(piece.shape[0] for piece in pieces)
    edge = values.shape[1]
    lines = outs * rhs
    words = rhs * count // 2 + SUBLANES
    return pl.pallas_call(
        functools.partial(adjoint_kernel, len(pieces), rhs),
        in_specs=[pl.BlockSpec(memory_space=pltpu.SMEM)] * 2 + in_vmem(len(pieces) + 1),
        out_specs=in_vmem(outs),
        out_shape=[jax.ShapeDtypeStruct((words, edge), jnp.int32)] * outs,
        scratch_shapes=[pltpu.VMEM((count * lines, edge), jnp.float32)],
        compiler_params=params(15),
        cost_estimate=cost(count * edge**2 * 2 * lines, count * edge**2 * 2),
        name="adjoint",
    )(row_list, scales, *pieces, values)


def gather_cells_kernel(slots, hot_ref, *rest):
    terms, (field_ref, word_ref, split_ref) = rest[:slots], rest[slots:]
    rhs, weeks, rows, lon = field_ref.shape
    count = hot_ref.shape[1] // slots
    half = count // 2
    wide = rhs * LANES
    for slot in range(slots):
        for k in range(rhs):
            scale = word_scale(terms[slot], rhs * half, k)[:1]
            word = terms[slot][k * half : (k + 1) * half, :]
            for base, number in ((0, high_of(word)), (half, low_of(word))):
                coarse = (number + 128) >> 8
                fine = number - (coarse << 8)
                at = slot * count + base
                split_ref[at : at + half, k * LANES : (k + 1) * LANES] = (
                    (coarse << 8).astype(jnp.float32) * scale
                ).astype(jnp.bfloat16)
                split_ref[at : at + half, wide + k * LANES : wide + (k + 1) * LANES] = (
                    fine.astype(jnp.float32) * scale
                ).astype(jnp.bfloat16)
    peaks = [jnp.zeros((SUBLANES, lon), jnp.float32)] * rhs
    parts = lon // LANES
    for week in range(weeks):
        at = week * parts * rows
        both = jnp.dot(
            hot_ref[at : at + parts * rows, :],
            split_ref[...],
            preferred_element_type=jnp.float32,
        )
        cells = both[:, :wide] + both[:, wide:]
        for k in range(rhs):
            for part in range(parts):
                field_ref[k, week, :, part * LANES : (part + 1) * LANES] = cells[
                    part * rows : (part + 1) * rows, k * LANES : (k + 1) * LANES
                ]
            for start in range(0, rows, SUBLANES):
                peaks[k] = jnp.maximum(
                    peaks[k], jnp.abs(field_ref[k, week, start : start + SUBLANES, :])
                )
    pack_field(field_ref, word_ref, peaks)


def gather_cells(hot_turned, terms, rhs, weeks, rows, lon):
    slots = len(terms)
    return pl.pallas_call(
        functools.partial(gather_cells_kernel, slots),
        in_specs=in_vmem(1 + slots),
        out_specs=in_vmem(2),
        out_shape=[
            jax.ShapeDtypeStruct((rhs, weeks, rows, lon), jnp.float32),
            jax.ShapeDtypeStruct(words_shape(rhs, weeks, rows, lon), jnp.int32),
        ],
        scratch_shapes=[pltpu.VMEM((hot_turned.shape[1], 2 * rhs * LANES), jnp.bfloat16)],
        compiler_params=params(12),
        cost_estimate=cost(rhs * hot_turned.size * 4 * LANES, rhs * weeks * rows * lon * 10),
        name="gather_cells",
    )(hot_turned, *terms)


def pull_back_kernel(
    side_ref, own_ref, pair_ref, cross_ref, weights_ref, count_ref, word_ref, window_ref, field_ref
):
    rhs, weeks, rows, lon = own_ref.shape
    parts = lon // LANES
    body = rhs * weeks * rows // 2
    for k in range(rhs):
        scales = [field_scale(ref, body, k, parts) for ref in (pair_ref, cross_ref)]
        for week in range(weeks):
            field_ref[k, week] = lat_mix(
                side_ref, weights_ref, window_ref, k, week, pair_ref, own_ref, cross_ref, scales
            )
    pack_field(field_ref, word_ref, lon_field(field_ref, count_ref, field_ref))


def pull_back(side, own, pair, cross, weights, counts):
    rhs, weeks, rows, lon = own.shape
    return pl.pallas_call(
        pull_back_kernel,
        in_specs=[pl.BlockSpec(memory_space=pltpu.SMEM)] + in_vmem(5),
        out_specs=pl.BlockSpec(memory_space=pltpu.VMEM),
        out_shape=jax.ShapeDtypeStruct(pair.shape, jnp.int32),
        scratch_shapes=[
            pltpu.VMEM((3 * rows, lon), jnp.float32),
            pltpu.VMEM((rhs, weeks, rows, lon), jnp.float32),
        ],
        compiler_params=params(8),
        cost_estimate=cost(rhs * weeks * rows * lon * 300, rhs * weeks * rows * lon * 10),
        name="pull_back",
    )(side, own, pair, cross, weights, counts)


def gram_kernel(places, count, rhs, order_ref, sums_before, residual_ref, direction_ref, *rest):
    words, (image_ref, gram_ref, sums_ref) = rest[:count], rest[-3:]
    rhs_count, weeks, rows, lon = direction_ref.shape
    half = rows // 2
    body, parts = rhs * weeks * half, lon // LANES
    old_places, new_places = places[:-count], places[-count:]
    for word_ref, place in zip(words, new_places):
        for k in range(rhs):
            index = order_ref[place] + k
            scale = field_scale(word_ref, body, k, parts)

            def one_week(week, carry):
                for start in range(0, half, SUBLANES):
                    word = words_at(word_ref, body, (k * weeks + week) * half + start, parts)
                    for base, number in ((start, high_of(word)), (half + start, low_of(word))):
                        image_ref[index, week, base : base + SUBLANES, :] = (
                            direction_ref[index, week, base : base + SUBLANES, :]
                            + number.astype(jnp.float32) * scale
                        )
                return carry

            lax.fori_loop(0, weeks, one_week, 0)

    sums_ref[...] = jnp.zeros_like(sums_ref)
    row_groups = rows // SUBLANES

    def tile(blocks):
        def one_week(week, sums):
            sums = list(sums)
            for row in range(0, rows, SUBLANES):
                for lane in range(0, lon, LANES):
                    spot = (week, slice(row, row + SUBLANES), slice(lane, lane + LANES))
                    place = 0
                    for _, lefts, rights, _ in blocks:
                        right = [ref[(k, *spot)] for ref, k, _ in rights]
                        for ref, k, _ in lefts:
                            left = ref[(k, *spot)]
                            for b in range(len(rights)):
                                sums[place] = sums[place] + left * right[b]
                                place += 1
            return tuple(sums)

        zero = jnp.zeros((SUBLANES, LANES), jnp.float32)
        total = sum(len(lefts) * len(rights) for _, lefts, rights, _ in blocks)
        sums = list(lax.fori_loop(0, weeks, one_week, (zero,) * total))
        for index, lefts, rights, mirror in blocks:
            for _, _, row in lefts:
                for _, _, column in rights:
                    lanes = jnp.sum(sums.pop(0), axis=0, keepdims=True)
                    for row_at, column_at in ((row, column), (column, row))[: 1 + mirror]:
                        at = (index * rhs_count + row_at) * rhs_count + column_at
                        sums_ref[pl.ds(at, 1), :] = lanes

    def listed(places):
        found = [order_ref[place] + k for place in places for k in range(rhs)]
        return [(image_ref, index, index) for index in found]

    residuals = [(residual_ref, k, k) for k in range(rhs_count)]
    directions = [(direction_ref, k, k) for k in range(rhs_count)]
    images = listed(new_places)
    if not old_places:
        for a in range(rhs_count):
            tile([(0, residuals[a : a + 1], residuals[a:], True)])
    for b in range(0, len(images), 2):
        right = images[b : b + 2]
        left = images[: b + len(right)] + listed(old_places)
        tile([(1, directions, right, False), (2, residuals, right, False), (3, left, right, True)])

    gram_ref[...] = sums_before[...] + lax.dot_general(
        jnp.ones((SUBLANES, LANES), jnp.float32),
        sums_ref[...],
        (((1,), (1,)), ((), ())),
        precision=HIGHEST,
        preferred_element_type=jnp.float32,
    )


def grams(order, places, sums, residual, direction, words, rhs, images):
    rhs_count, weeks, rows, lon = direction.shape
    total = 4 * rhs_count**2
    count = len(words)
    return pl.pallas_call(
        functools.partial(gram_kernel, places, count, rhs),
        in_specs=[pl.BlockSpec(memory_space=pltpu.SMEM)] + in_vmem(3 + count + len(images)),
        out_specs=in_vmem(2),
        out_shape=[
            jax.ShapeDtypeStruct(direction.shape, jnp.float32),
            jax.ShapeDtypeStruct((SUBLANES, total), jnp.float32),
        ],
        scratch_shapes=[pltpu.VMEM((total, LANES), jnp.float32)],
        input_output_aliases={4 + count: 0} if images else {},
        compiler_params=params(14),
        cost_estimate=cost(8 * rhs_count * direction.size, 16 * direction.size),
        name="grams",
    )(order, sums, residual, direction, *words, *images)


def small_product(left, right):
    total = jnp.zeros((SUBLANES, LANES), jnp.float32)
    for j in range(SUBLANES):
        column = jnp.broadcast_to(left[:, j : j + 1], (SUBLANES, LANES))
        total = total + column * jnp.broadcast_to(right[j : j + 1, :], (SUBLANES, LANES))
    return total


def small_transpose(value):
    rest = jnp.zeros((LANES - SUBLANES, LANES), jnp.float32)
    return jnp.concatenate([value, rest], axis=0).T[:SUBLANES]


def small_solves(systems):
    line = lax.broadcasted_iota(jnp.int32, (SUBLANES, LANES), 0)
    lane = lax.broadcasted_iota(jnp.int32, (SUBLANES, LANES), 1)
    states = [matrix + pltpu.roll(right, SUBLANES, 1) for matrix, right in systems]
    for j in range(SUBLANES):
        for index, both in enumerate(states):
            column = jnp.broadcast_to(both[:, j : j + 1], (SUBLANES, LANES))
            pivot = jnp.broadcast_to(both[j : j + 1, :], (SUBLANES, LANES))
            scaled = pivot / jnp.broadcast_to(both[j : j + 1, j : j + 1], (SUBLANES, LANES))
            states[index] = jnp.where(line == j, scaled, both - column * scaled)
    return [
        jnp.where(lane < SUBLANES, pltpu.roll(both, LANES - SUBLANES, 1), 0.0) for both in states
    ]


def solve_steps(sums_ref):
    total = sums_ref.shape[1]
    size = SUBLANES
    place = lax.broadcasted_iota(jnp.int32, (size, total), 1)
    line = lax.broadcasted_iota(jnp.int32, (size, total), 0)
    spot = lax.broadcasted_iota(jnp.int32, (total, LANES), 0)
    lane = lax.broadcasted_iota(jnp.int32, (total, LANES), 1)
    sums = sums_ref[...]

    def matrix(index, turned=False):
        row, column = place % size, spot // size % size
        if not turned:
            row, column = place // size % size, spot % size
        here = (place // size**2 == index) & (row == line)
        return jnp.dot(
            jnp.where(here, sums, 0.0),
            jnp.where(column == lane, 1.0, 0.0),
            precision=HIGHEST,
            preferred_element_type=jnp.float32,
        )

    gram_old, gram_image = matrix(0), matrix(3)
    curvature = 0.5 * (matrix(1) + matrix(1, True))
    mixed, mixed_turned = matrix(2), matrix(2, True)
    diagonal = lax.broadcasted_iota(jnp.int32, (size, LANES), 0)
    identity = jnp.where(diagonal == lax.broadcasted_iota(jnp.int32, (size, LANES), 1), 1.0, 0.0)
    step, old_inverse = small_solves([(curvature, gram_old), (gram_old, identity)])
    step_turned = small_transpose(step)
    rest = small_product(gram_image, step) - mixed_turned
    gram_new = gram_old - small_product(mixed, step) + small_product(step_turned, rest)
    return step_turned, small_product(gram_new, old_inverse)


def spread_coefficients(turned):
    size = SUBLANES
    wide = 4 * size**2
    lane = lax.broadcasted_iota(jnp.int32, (size, wide), 1)
    line = lax.broadcasted_iota(jnp.int32, (size, wide), 0)
    spread = jnp.zeros((size, wide), jnp.float32)
    for b in range(size):
        column = jnp.broadcast_to(turned[:, b : b + 1], (size, wide))
        spread = spread + jnp.where(lane // size % size == b, column, 0.0)
    high = spread.astype(jnp.bfloat16).astype(jnp.float32)
    spread = jnp.where(lane < 2 * size**2, high, spread - high)
    own = (lane % size == line) & (lane < 3 * size**2)
    rows = [
        jnp.where(own, jnp.broadcast_to(spread[a : a + 1], (size, wide)), 0.0) for a in range(size)
    ]
    return jnp.concatenate(rows, axis=0)


def split_rows(ref, row):
    value = jnp.concatenate([ref[b, 0, row : row + SUBLANES, :] for b in range(ref.shape[0])], axis=0)
    high = value.astype(jnp.bfloat16)
    low = (value - high.astype(jnp.float32)).astype(jnp.bfloat16)
    return jnp.concatenate([high, low, high], axis=0)


def update_kernel(
    sums_ref, solution_ref, residual_ref, direction_ref, image_ref, sol_out, res_out, dir_out, coef_ref
):
    rhs_count, _, rows, lon = direction_ref.shape
    size = rhs_count * SUBLANES

    @pl.when(pl.program_id(0) == 0)
    def _():
        step_turned, turn_turned = solve_steps(sums_ref)
        coefs = [spread_coefficients(step_turned), spread_coefficients(turn_turned)]
        coef_ref[...] = jnp.concatenate(coefs, axis=0).astype(jnp.bfloat16)

    for row in range(0, rows, SUBLANES):
        coefs = coef_ref[:, : 3 * size]
        moves = jnp.dot(coefs, split_rows(direction_ref, row), preferred_element_type=jnp.float32)
        drops = jnp.dot(coefs[:size], split_rows(image_ref, row), preferred_element_type=jnp.float32)
        for a in range(rhs_count):
            at = a * SUBLANES
            spot = (a, 0, slice(row, row + SUBLANES), slice(None))
            sol_out[spot] = solution_ref[spot] + moves[at : at + SUBLANES]
            left = residual_ref[spot] - drops[at : at + SUBLANES]
            res_out[spot] = left
            dir_out[spot] = left + moves[size + at : size + at + SUBLANES]


def update(sums, solution, residual, direction, image):
    rhs_count, weeks, rows, lon = direction.shape
    field = pl.BlockSpec((rhs_count, 1, rows, lon), lambda w: (0, w, 0, 0))
    shape = jax.ShapeDtypeStruct(direction.shape, jnp.float32)
    return pl.pallas_call(
        update_kernel,
        grid=(weeks,),
        in_specs=[whole(sums.shape)] + [field] * 4,
        out_specs=[field] * 3,
        scratch_shapes=[pltpu.VMEM((2 * rhs_count * SUBLANES, 4 * rhs_count * SUBLANES), jnp.bfloat16)],
        out_shape=[shape] * 3,
        compiler_params=params(16),
        cost_estimate=cost(6 * rhs_count * direction.size, 28 * direction.size),
        name="update",
    )(sums, solution, residual, direction, image)


def crossed(value, axis, by):
    if by == 0:
        return value
    return lax.ppermute(value, axis, [(i, i ^ by) for i in range(lax.axis_size(axis))])


def far_first(size):
    return [1 << bit for bit in reversed(range(size.bit_length() - 1))]


def neighbours(value, axis):
    size = lax.axis_size(axis)
    outer = [(i, i + 1) for i in range(1, size - 1, 2)]
    outer += [(after, before) for before, after in outer]
    return crossed(value, axis, 1), lax.ppermute(value, axis, outer)


def summed_over(value, axis):
    bits = far_first(lax.axis_size(axis))[::-1]
    before = value
    for step in [bits[:1]] + [bits[at : at + 2] for at in range(1, len(bits), 2)]:
        before = value
        for reach in step[:1]:
            value = value + crossed(before, axis, reach)
        for reach in step[1:]:
            far = crossed(before, axis, reach) + crossed(before, axis, reach | step[0])
            value = value + far
    return value, before


def lat_windows(lat_width, band, rows):
    decay = rows / 2.0
    total = lat_width.shape[0]
    offsets = jnp.abs(jnp.arange(-rows, rows + 1)).astype(jnp.float32)
    limits = lat_width.astype(jnp.float32)
    normal = jnp.sqrt(
        jnp.sum(
            jnp.where(
                offsets[None, :] <= limits[:, None], jnp.exp(-2.0 * offsets / decay)[None, :], 0.0
            ),
            axis=1,
        )
    )
    padded_limits = jnp.pad(limits, (rows, rows), constant_values=-1.0)
    padded_normal = jnp.pad(normal, (rows, rows), constant_values=1.0)
    near_limits = lax.dynamic_slice_in_dim(padded_limits, band * rows, 3 * rows)
    near_normal = lax.dynamic_slice_in_dim(padded_normal, band * rows, 3 * rows)
    distance = jnp.abs(
        jnp.arange(rows)[:, None] + rows - jnp.arange(3 * rows)[None, :]
    ).astype(jnp.float32)
    fade = jnp.exp(-distance / decay)
    own_limits, own_normal = near_limits[rows : 2 * rows, None], near_normal[rows : 2 * rows, None]
    spread = jnp.where(distance <= own_limits, fade, 0.0) / own_normal
    pulled = jnp.where(distance <= near_limits[None, :], fade, 0.0) / near_normal[None, :]
    return spread, pulled


def shards(
    footprints,
    block_rows,
    block_cols,
    block_scale,
    lat_width,
    lon_width,
    obs_weight,
    solution,
    residual,
    direction,
):
    rhs_count, weeks, rows, lon = direction.shape
    blocks = footprints[0, 0]
    count, edge, _ = blocks.shape
    row_list = block_rows[0, 0]
    scales = jnp.exp2(-block_scale[0, 0].astype(jnp.float32))
    row_blocks = obs_weight.shape[0] // edge
    slots = lax.axis_size("obs")
    rhs = rhs_count // slots
    slab, band = lax.axis_index("obs"), lax.axis_index("lat")
    parts = lon // edge
    cols = weeks * rows * parts

    groups = chunk_of(rhs, BACK_GROUPS)
    each = rhs // groups
    order = (slab ^ jnp.arange(slots, dtype=jnp.int32)) * rhs
    own_width = lax.dynamic_slice_in_dim(lon_width, band * rows, rows)
    counts = jnp.broadcast_to(own_width[:, None] + 1, (rows, lon))

    lists = block_cols
    for reach in reversed(far_first(slots)):
        lists = jnp.concatenate([lists, crossed(lists, "obs", reach)], axis=0)
    lists = lists[:, 0]
    line, part = lists // parts, lists % parts
    places = ((line // rows) * parts + part) * rows + line % rows

    lon_own, words = spread_lon(
        lax.dynamic_slice_in_dim(direction, slab * rhs, rhs, 0), counts
    )
    halo = neighbours(words, "lat")
    hot = (places[:, :, None] == jnp.arange(cols)[None, None, :]).astype(jnp.bfloat16)
    hot_turned = (jnp.arange(cols)[:, None] == places.reshape(1, -1)).astype(jnp.bfloat16)
    lat_spread, lat_pulled = lat_windows(lat_width, band, rows)
    side = (band % 2).astype(jnp.int32).reshape(1)

    picks = spread_lat(side, lon_own, *halo, lat_spread, hot)
    cells = [crossed(picks[d], "obs", d) for d in range(slots)]
    kept = count // KEPT_OF * KEPT if count % KEPT_OF == 0 else 0
    stays = [preload(blocks, 0, kept, picks[0])] if kept else []
    near = preload(blocks, kept, count - kept, picks[0])
    sums, partial = summed_over(
        forward(row_list, scales, [*stays, near], cells, row_blocks), "lat"
    )
    near = preload(blocks, kept, count - kept, partial)
    weighted = sums.reshape(row_blocks, slots * rhs, edge) * obs_weight.reshape(row_blocks, 1, edge)
    terms = adjoint_terms(
        row_list, scales, [*stays, near], weighted.reshape(-1, edge), slots * groups, each
    )
    sent = [[crossed(terms[d * groups + g], "obs", d) for d in range(slots)] for g in range(groups)]
    own = []
    for group in range(groups):
        field, words = gather_cells(hot_turned, sent[group], each, weeks, rows, lon)
        own.append(pull_back(side, field, *neighbours(words, "lat"), lat_pulled, counts))

    starts = (order[:, None] + jnp.arange(groups, dtype=jnp.int32) * each).reshape(-1)
    products = jnp.zeros((SUBLANES, 4 * rhs_count**2), jnp.float32)
    images, places = [], ()

    def add_products(slot):
        nonlocal products, places, images
        words = [arrived[group][slot] for group in range(groups)]
        places += tuple(slot * groups + group for group in range(groups))
        *images, products = grams(
            starts, places, products, residual, direction, words, each, images
        )

    arrived = [{0: words} for words in own]
    for group in range(groups):
        for reach in far_first(slots):
            arrived[group][reach] = crossed(own[group], "obs", reach)
    add_products(0)
    first_products = products
    for reach in far_first(slots)[1:]:
        for group in range(groups):
            for bits in [bits for bits in arrived[group] if bits > reach and not bits % (2 * reach)]:
                words = arrived[group][bits]
                if group == groups - 1:
                    words, _ = lax.optimization_barrier((words, first_products))
                arrived[group][bits | reach] = crossed(words, "obs", reach)
    for slot in range(1, slots):
        add_products(slot)
    products, _ = summed_over(products, "lat")
    return tuple(update(products, solution, residual, direction, *images))


def solution(mesh):
    return jax.shard_map(
        shards,
        mesh=mesh,
        in_specs=(
            P("obs", "lat", None, None, None),
            P("obs", "lat", None),
            P("obs", "lat", None),
            P("obs", "lat", None),
            P(),
            P(),
            P("obs"),
            P(None, None, "lat", None),
            P(None, None, "lat", None),
            P(None, None, "lat", None),
        ),
        out_specs=(
            P(None, None, "lat", None),
            P(None, None, "lat", None),
            P(None, None, "lat", None),
        ),
        check_vma=False,
    )
```

```python
import functools
import math

import jax
import jax.numpy as jnp
from jax import lax
from jax.experimental import pallas as pl
from jax.experimental.pallas import tpu as pltpu
from jax.sharding import PartitionSpec as P

LANES = 128
CHUNK = 192
COPIES = 12
STREAM_MIB = 40
KEPT, KEPT_OF = 0, 2
BACK_GROUPS = 2
SUBLANES = 8
MIB = 1024 * 1024
HIGHEST = lax.Precision.HIGHEST


def params(mib):
    return pltpu.CompilerParams(vmem_limit_bytes=mib * MIB)


def cost(flops, nbytes):
    return pl.CostEstimate(flops=int(flops), bytes_accessed=int(nbytes), transcendentals=0)


def whole(shape):
    return pl.BlockSpec(shape, lambda *_: (0,) * len(shape), pipeline_mode=pl.Buffered(1))


def in_vmem(count):
    return [pl.BlockSpec(memory_space=pltpu.VMEM)] * count


def pow2(exponent):
    size = jnp.abs(exponent)
    up = jnp.ones(exponent.shape, jnp.float32)
    down = up
    for bit in range(7):
        on = ((size >> bit) & 1) == 1
        up = up * jnp.where(on, 2.0 ** (2**bit), 1.0)
        down = down * jnp.where(on, 2.0 ** -(2**bit), 1.0)
    return jnp.where(exponent < 0, down, up)


def exponent_of(peak):
    logs = jnp.log(jnp.maximum(peak, 1e-28)) * (1.0 / math.log(2.0))
    return jnp.ceil(logs + 1e-3).astype(jnp.int32)


def to_int(values, factor):
    return jnp.clip(jnp.round(values * factor), -32767.0, 32767.0).astype(jnp.int32)


def pack(high, low):
    return (high << 16) | (low & 0xFFFF)


def high_of(word):
    return word >> 16


def low_of(word):
    return (word << 16) >> 16


def words_shape(rhs, weeks, rows, lon):
    parts = lon // LANES
    tail = -(-rhs * parts // SUBLANES) * SUBLANES
    return parts * (rhs * weeks * rows // 2) + tail, LANES


def words_at(word_ref, body, at, parts):
    found = []
    for part in range(parts):
        start = part * body + at
        if not isinstance(start, int):
            start = pl.multiple_of(start, SUBLANES)
        found.append(word_ref[pl.ds(start, SUBLANES), :])
    return jnp.concatenate(found, axis=1)


def field_scale(word_ref, body, k, parts):
    first = parts * (body + k)
    row = jnp.concatenate(
        [word_ref[first + part : first + part + 1, :] for part in range(parts)], axis=1
    )
    return pow2(jnp.broadcast_to(row, (SUBLANES, row.shape[1])) - 15)


def exponent_rows(peaks):
    line = lax.broadcasted_iota(jnp.int32, (SUBLANES, peaks[0].shape[1]), 0)
    found = jnp.zeros(line.shape, jnp.int32)
    for k, peak in enumerate(peaks):
        found = jnp.where(line == k, exponent_of(jnp.max(peak, axis=0, keepdims=True)), found)
    return found


def pack_field(field_ref, word_ref, peaks):
    rhs, weeks, rows, lon = field_ref.shape
    half, parts = rows // 2, lon // LANES
    body = rhs * weeks * half
    tail = word_ref.shape[0] - parts * body
    line = lax.broadcasted_iota(jnp.int32, (tail, LANES), 0)
    kept = jnp.zeros((tail, LANES), jnp.int32)
    for k in range(rhs):
        exponent = exponent_of(jnp.max(peaks[k], axis=0, keepdims=True))
        for part in range(parts):
            own = exponent[:, part * LANES : (part + 1) * LANES]
            kept = jnp.where(line == k * parts + part, own, kept)
        factor = pow2(15 - jnp.broadcast_to(exponent, (SUBLANES, lon)))

        def one_week(week, carry):
            for start in range(0, half, SUBLANES):
                high = to_int(field_ref[k, week, start : start + SUBLANES, :], factor)
                low = to_int(field_ref[k, week, half + start : half + start + SUBLANES, :], factor)
                word = pack(high, low)
                for part in range(parts):
                    at = part * body + (k * weeks + week) * half + start
                    at = pl.multiple_of(at, SUBLANES)
                    word_ref[pl.ds(at, SUBLANES), :] = word[:, part * LANES : (part + 1) * LANES]
            return carry

        lax.fori_loop(0, weeks, one_week, 0)
    word_ref[parts * body :, :] = kept


def word_scale(word_ref, body, k):
    row = word_ref[body + k : body + k + 1, :] - 15
    return pow2(jnp.broadcast_to(row, (SUBLANES, row.shape[1])))


def lon_setup(lon):
    return lon / 32.0, (lon // 8 + 1).bit_length()


def lon_rows(rows, count, norm, lon):
    decay, bits = lon_setup(lon)
    fields = rows.shape[0] // SUBLANES
    count = jnp.concatenate([count] * fields, axis=0)
    windows = [rows, rows]
    taken = [jnp.zeros_like(rows)] * 2
    for bit in range(bits):
        reach = 2**bit
        fade = math.exp(-reach / decay)
        chosen = ((count >> bit) & 1) == 1
        for side in range(2):
            shift = reach if side == 0 else lon - reach
            moved = windows[side]
            if bit:
                moved = moved + fade * pltpu.roll(taken[side], shift, 1)
            taken[side] = jnp.where(chosen, moved, taken[side])
            if bit + 1 < bits:
                windows[side] = windows[side] + fade * pltpu.roll(windows[side], shift, 1)
    return (taken[0] + taken[1] - rows) * jnp.concatenate([norm] * fields, axis=0)


def lon_norm(count, lon):
    decay, _ = lon_setup(lon)
    ratio = math.exp(-2.0 / decay)
    ends = jnp.exp(count.astype(jnp.float32) * (-2.0 / decay))
    return 1.0 / jnp.sqrt(1.0 + (2.0 / (1.0 - ratio)) * (ratio - ends))


def lon_field(source_ref, count_ref, out_ref):
    rhs, weeks, rows, lon = out_ref.shape

    def one_group(group, peaks):
        at = pl.multiple_of(group * SUBLANES, SUBLANES)
        count = count_ref[pl.ds(at, SUBLANES), :]
        norm = lon_norm(count, lon)
        fields = [source_ref[k, w, pl.ds(at, SUBLANES), :] for k in range(rhs) for w in range(weeks)]
        result = lon_rows(jnp.concatenate(fields, axis=0), count, norm, lon)
        peaks = list(peaks)
        for k in range(rhs):
            for w in range(weeks):
                start = (k * weeks + w) * SUBLANES
                part = result[start : start + SUBLANES]
                out_ref[k, w, pl.ds(at, SUBLANES), :] = part
                peaks[k] = jnp.maximum(peaks[k], jnp.abs(part))
        return tuple(peaks)

    zero = jnp.zeros((SUBLANES, lon), jnp.float32)
    return lax.fori_loop(0, rows // SUBLANES, one_group, (zero,) * rhs)


def spread_lon_kernel(field_ref, count_ref, out_ref, word_ref):
    pack_field(out_ref, word_ref, lon_field(field_ref, count_ref, out_ref))


def spread_lon(field, counts):
    rhs, weeks, rows, lon = field.shape
    return pl.pallas_call(
        spread_lon_kernel,
        in_specs=in_vmem(2),
        out_specs=in_vmem(2),
        out_shape=[
            jax.ShapeDtypeStruct(field.shape, jnp.float32),
            jax.ShapeDtypeStruct(words_shape(rhs, weeks, rows, lon), jnp.int32),
        ],
        compiler_params=params(6),
        cost_estimate=cost(field.size * 100, field.size * 10),
        name="spread_lon",
    )(field, counts)


def lat_mix(side_ref, weights_ref, window_ref, k, week, pair_ref, own_ref, cross_ref, scales):
    rhs, weeks, rows, lon = own_ref.shape
    half = rows // 2
    body, parts = rhs * weeks * half, lon // LANES
    before = 2 * rows * (1 - side_ref[0])
    for base, ref, scale in (
        (before, pair_ref, scales[0]),
        (2 * rows - before, cross_ref, scales[1]),
    ):
        for start in range(0, half, SUBLANES):
            at = (k * weeks + week) * half + start
            word = words_at(ref, body, at, parts)
            for to, number in ((start, high_of(word)), (half + start, low_of(word))):
                to = pl.multiple_of(base + to, SUBLANES)
                window_ref[pl.ds(to, SUBLANES), :] = number.astype(jnp.float32) * scale
    window_ref[rows : 2 * rows, :] = own_ref[k, week]
    return jnp.dot(
        weights_ref[...],
        window_ref[...],
        precision=HIGHEST,
        preferred_element_type=jnp.float32,
    )


def spread_lat_kernel(slots, side_ref, own_ref, pair_ref, cross_ref, weights_ref, hot_ref, *rest):
    picks, (window_ref, cells_ref) = rest[:slots], rest[slots:]
    rhs, weeks, rows, lon = own_ref.shape
    parts = lon // LANES
    body = rhs * weeks * rows // 2
    for k in range(rhs):
        scales = [field_scale(ref, body, k, parts) for ref in (pair_ref, cross_ref)]
        for week in range(weeks):
            mixed = lat_mix(
                side_ref, weights_ref, window_ref, k, week, pair_ref, own_ref, cross_ref, scales
            )
            for part in range(parts):
                at = (week * parts + part) * rows
                cells_ref[at : at + rows, k * LANES : (k + 1) * LANES] = mixed[
                    :, part * LANES : (part + 1) * LANES
                ].astype(jnp.bfloat16)
    for slot in range(slots):
        found = jnp.dot(
            hot_ref[slot], cells_ref[...], preferred_element_type=jnp.float32
        ).astype(jnp.bfloat16)
        for k in range(rhs):
            picks[slot][k] = found[:, k * LANES : (k + 1) * LANES]


def spread_lat(side, own, pair, cross, weights, hot):
    rhs, weeks, rows, lon = own.shape
    slots, blocks, cols = hot.shape
    return pl.pallas_call(
        functools.partial(spread_lat_kernel, slots),
        in_specs=[pl.BlockSpec(memory_space=pltpu.SMEM)] + in_vmem(5),
        out_specs=in_vmem(slots),
        out_shape=[jax.ShapeDtypeStruct((rhs, blocks, LANES), jnp.bfloat16)] * slots,
        scratch_shapes=[
            pltpu.VMEM((3 * rows, lon), jnp.float32),
            pltpu.VMEM((cols, rhs * LANES), jnp.bfloat16),
        ],
        compiler_params=params(10),
        cost_estimate=cost(rhs * slots * blocks * cols * LANES * 2, rhs * weeks * rows * lon * 10),
        name="spread_lat",
    )(side, own, pair, cross, weights, hot)


def chunk_of(count, most):
    return max(size for size in range(1, most + 1) if count % size == 0)


def preload_kernel(first, after_ref, blocks_ref, out_ref, done):
    del after_ref
    parts = done.shape[0]
    size = out_ref.shape[0] // parts
    copies = [
        pltpu.make_async_copy(
            blocks_ref.at[pl.ds(first + part * size, size)],
            out_ref.at[pl.ds(part * size, size)],
            done.at[part],
        )
        for part in range(parts)
    ]
    for copy in copies:
        copy.start()
    for copy in copies:
        copy.wait()


def preload(blocks, first, count, after):
    parts = chunk_of(count, COPIES)
    shape = (count, *blocks.shape[1:])
    return pl.pallas_call(
        functools.partial(preload_kernel, first),
        in_specs=[pl.BlockSpec(memory_space=pl.ANY)] * 2,
        out_specs=pl.BlockSpec(memory_space=pltpu.VMEM),
        out_shape=jax.ShapeDtypeStruct(shape, blocks.dtype),
        scratch_shapes=[pltpu.SemaphoreType.DMA((parts,))],
        compiler_params=params(STREAM_MIB),
        cost_estimate=cost(0, count * blocks[0].size * 4),
        name="preload",
    )(after, blocks)


def forward_kernel(pieces, row_ref, scale_ref, *rest):
    pieces, picks, (out_ref, cells_ref) = rest[:pieces], rest[pieces:-2], rest[-2:]
    rhs, count, edge = picks[0].shape
    lines = len(picks) * rhs
    out_ref[...] = jnp.zeros_like(out_ref)
    for place, pick_ref in enumerate(picks):
        for k in range(rhs):
            cells_ref[pl.ds(place * rhs + k, count, stride=lines), :] = pick_ref[k].astype(
                jnp.float32
            )

    def one_chunk(piece_ref, first, chunk, step, carry):
        values = []
        for n in range(0, chunk, 2):
            index = step * chunk + n
            at = pl.multiple_of((first + index) * lines, 2 * lines)
            both = lax.dot_general(
                cells_ref[pl.ds(at, 2 * lines), :].astype(jnp.bfloat16),
                piece_ref[pl.ds(index, 2)].reshape(2 * edge, edge),
                (((1,), (1,)), ((), ())),
                preferred_element_type=jnp.float32,
            )
            values += [both[:lines, :edge], both[lines:, edge:]]
        for n in range(chunk):
            index = first + step * chunk + n
            at = pl.multiple_of(row_ref[index] * lines, lines)
            out_ref[pl.ds(at, lines), :] += values[n] * scale_ref[index]
        return carry

    over_chunks(pieces, one_chunk)


def over_chunks(pieces, one_chunk):
    first = 0
    for piece_ref in pieces:
        count = piece_ref.shape[0]
        chunk = 2 * chunk_of(count // 2, CHUNK // 2)
        lax.fori_loop(0, count // chunk, functools.partial(one_chunk, piece_ref, first, chunk), 0)
        first += count


def forward(row_list, scales, pieces, picks, row_blocks):
    rhs, count, edge = picks[0].shape
    lines = len(picks) * rhs
    return pl.pallas_call(
        functools.partial(forward_kernel, len(pieces)),
        in_specs=[pl.BlockSpec(memory_space=pltpu.SMEM)] * 2 + in_vmem(len(pieces) + len(picks)),
        out_specs=pl.BlockSpec(memory_space=pltpu.VMEM),
        out_shape=jax.ShapeDtypeStruct((row_blocks * lines, edge), jnp.float32),
        scratch_shapes=[pltpu.VMEM((count * lines, edge), jnp.float32)],
        compiler_params=params(15),
        cost_estimate=cost(count * edge**2 * 2 * lines, count * edge**2 * 2),
        name="forward",
    )(row_list, scales, *pieces, *picks)


def adjoint_kernel(pieces, rhs, row_ref, scale_ref, *rest):
    pieces, values_ref, outs, terms_ref = rest[:pieces], rest[pieces], rest[pieces + 1 : -1], rest[-1]
    lines = len(outs) * rhs
    edge = values_ref.shape[1]
    count = terms_ref.shape[0] // lines

    def one_chunk(piece_ref, first, chunk, step, carry):
        for n in range(0, chunk, 2):
            here = step * chunk + n
            index = first + here
            pulled = [
                values_ref[pl.ds(pl.multiple_of(row_ref[index + q] * lines, lines), lines), :]
                for q in range(2)
            ]
            both = jnp.dot(
                jnp.concatenate(pulled, axis=0).astype(jnp.bfloat16),
                jnp.concatenate([piece_ref[here + q] for q in range(2)], axis=1),
                preferred_element_type=jnp.float32,
            )
            for q in range(2):
                to = pl.multiple_of((index + q) * lines, lines)
                part = both[q * lines : (q + 1) * lines, q * edge : (q + 1) * edge]
                terms_ref[pl.ds(to, lines), :] = part * scale_ref[index + q]
        return carry

    over_chunks(pieces, one_chunk)
    half = count // 2
    for place, out_ref in enumerate(outs):
        terms = [terms_ref[pl.ds(place * rhs + k, count, stride=lines), :] for k in range(rhs)]
        exponents = exponent_rows([jnp.abs(term) for term in terms])
        out_ref[rhs * half :, :] = exponents
        for k in range(rhs):
            number = to_int(terms[k], pow2(15 - exponents[k : k + 1]))
            out_ref[k * half : (k + 1) * half, :] = pack(number[:half], number[half:])


def adjoint_terms(row_list, scales, pieces, values, outs, rhs):
    count = sum(piece.shape[0] for piece in pieces)
    edge = values.shape[1]
    lines = outs * rhs
    words = rhs * count // 2 + SUBLANES
    return pl.pallas_call(
        functools.partial(adjoint_kernel, len(pieces), rhs),
        in_specs=[pl.BlockSpec(memory_space=pltpu.SMEM)] * 2 + in_vmem(len(pieces) + 1),
        out_specs=in_vmem(outs),
        out_shape=[jax.ShapeDtypeStruct((words, edge), jnp.int32)] * outs,
        scratch_shapes=[pltpu.VMEM((count * lines, edge), jnp.float32)],
        compiler_params=params(15),
        cost_estimate=cost(count * edge**2 * 2 * lines, count * edge**2 * 2),
        name="adjoint",
    )(row_list, scales, *pieces, values)


def gather_cells_kernel(slots, hot_ref, *rest):
    terms, (field_ref, word_ref, split_ref) = rest[:slots], rest[slots:]
    rhs, weeks, rows, lon = field_ref.shape
    count = hot_ref.shape[1] // slots
    half = count // 2
    wide = rhs * LANES
    for slot in range(slots):
        for k in range(rhs):
            scale = word_scale(terms[slot], rhs * half, k)[:1]
            word = terms[slot][k * half : (k + 1) * half, :]
            for base, number in ((0, high_of(word)), (half, low_of(word))):
                coarse = (number + 128) >> 8
                fine = number - (coarse << 8)
                at = slot * count + base
                split_ref[at : at + half, k * LANES : (k + 1) * LANES] = (
                    (coarse << 8).astype(jnp.float32) * scale
                ).astype(jnp.bfloat16)
                split_ref[at : at + half, wide + k * LANES : wide + (k + 1) * LANES] = (
                    fine.astype(jnp.float32) * scale
                ).astype(jnp.bfloat16)
    peaks = [jnp.zeros((SUBLANES, lon), jnp.float32)] * rhs
    parts = lon // LANES
    for week in range(weeks):
        at = week * parts * rows
        both = jnp.dot(
            hot_ref[at : at + parts * rows, :],
            split_ref[...],
            preferred_element_type=jnp.float32,
        )
        cells = both[:, :wide] + both[:, wide:]
        for k in range(rhs):
            for part in range(parts):
                field_ref[k, week, :, part * LANES : (part + 1) * LANES] = cells[
                    part * rows : (part + 1) * rows, k * LANES : (k + 1) * LANES
                ]
            for start in range(0, rows, SUBLANES):
                peaks[k] = jnp.maximum(
                    peaks[k], jnp.abs(field_ref[k, week, start : start + SUBLANES, :])
                )
    pack_field(field_ref, word_ref, peaks)


def gather_cells(hot_turned, terms, rhs, weeks, rows, lon):
    slots = len(terms)
    return pl.pallas_call(
        functools.partial(gather_cells_kernel, slots),
        in_specs=in_vmem(1 + slots),
        out_specs=in_vmem(2),
        out_shape=[
            jax.ShapeDtypeStruct((rhs, weeks, rows, lon), jnp.float32),
            jax.ShapeDtypeStruct(words_shape(rhs, weeks, rows, lon), jnp.int32),
        ],
        scratch_shapes=[pltpu.VMEM((hot_turned.shape[1], 2 * rhs * LANES), jnp.bfloat16)],
        compiler_params=params(12),
        cost_estimate=cost(rhs * hot_turned.size * 4 * LANES, rhs * weeks * rows * lon * 10),
        name="gather_cells",
    )(hot_turned, *terms)


def pull_back_kernel(
    side_ref, own_ref, pair_ref, cross_ref, weights_ref, count_ref, word_ref, window_ref, field_ref
):
    rhs, weeks, rows, lon = own_ref.shape
    parts = lon // LANES
    body = rhs * weeks * rows // 2
    for k in range(rhs):
        scales = [field_scale(ref, body, k, parts) for ref in (pair_ref, cross_ref)]
        for week in range(weeks):
            field_ref[k, week] = lat_mix(
                side_ref, weights_ref, window_ref, k, week, pair_ref, own_ref, cross_ref, scales
            )
    pack_field(field_ref, word_ref, lon_field(field_ref, count_ref, field_ref))


def pull_back(side, own, pair, cross, weights, counts):
    rhs, weeks, rows, lon = own.shape
    return pl.pallas_call(
        pull_back_kernel,
        in_specs=[pl.BlockSpec(memory_space=pltpu.SMEM)] + in_vmem(5),
        out_specs=pl.BlockSpec(memory_space=pltpu.VMEM),
        out_shape=jax.ShapeDtypeStruct(pair.shape, jnp.int32),
        scratch_shapes=[
            pltpu.VMEM((3 * rows, lon), jnp.float32),
            pltpu.VMEM((rhs, weeks, rows, lon), jnp.float32),
        ],
        compiler_params=params(8),
        cost_estimate=cost(rhs * weeks * rows * lon * 300, rhs * weeks * rows * lon * 10),
        name="pull_back",
    )(side, own, pair, cross, weights, counts)


def gram_kernel(places, count, rhs, order_ref, sums_before, residual_ref, direction_ref, *rest):
    words, (image_ref, gram_ref, sums_ref) = rest[:count], rest[-3:]
    rhs_count, weeks, rows, lon = direction_ref.shape
    half = rows // 2
    body, parts = rhs * weeks * half, lon // LANES
    old_places, new_places = places[:-count], places[-count:]
    for word_ref, place in zip(words, new_places):
        for k in range(rhs):
            index = order_ref[place] + k
            scale = field_scale(word_ref, body, k, parts)

            def one_week(week, carry):
                for start in range(0, half, SUBLANES):
                    word = words_at(word_ref, body, (k * weeks + week) * half + start, parts)
                    for base, number in ((start, high_of(word)), (half + start, low_of(word))):
                        image_ref[index, week, base : base + SUBLANES, :] = (
                            direction_ref[index, week, base : base + SUBLANES, :]
                            + number.astype(jnp.float32) * scale
                        )
                return carry

            lax.fori_loop(0, weeks, one_week, 0)

    sums_ref[...] = jnp.zeros_like(sums_ref)
    row_groups = rows // SUBLANES

    def tile(blocks):
        def one_week(week, sums):
            sums = list(sums)
            for row in range(0, rows, SUBLANES):
                for lane in range(0, lon, LANES):
                    spot = (week, slice(row, row + SUBLANES), slice(lane, lane + LANES))
                    place = 0
                    for _, lefts, rights, _ in blocks:
                        right = [ref[(k, *spot)] for ref, k, _ in rights]
                        for ref, k, _ in lefts:
                            left = ref[(k, *spot)]
                            for b in range(len(rights)):
                                sums[place] = sums[place] + left * right[b]
                                place += 1
            return tuple(sums)

        zero = jnp.zeros((SUBLANES, LANES), jnp.float32)
        total = sum(len(lefts) * len(rights) for _, lefts, rights, _ in blocks)
        sums = list(lax.fori_loop(0, weeks, one_week, (zero,) * total))
        for index, lefts, rights, mirror in blocks:
            for _, _, row in lefts:
                for _, _, column in rights:
                    lanes = jnp.sum(sums.pop(0), axis=0, keepdims=True)
                    for row_at, column_at in ((row, column), (column, row))[: 1 + mirror]:
                        at = (index * rhs_count + row_at) * rhs_count + column_at
                        sums_ref[pl.ds(at, 1), :] = lanes

    def listed(places):
        found = [order_ref[place] + k for place in places for k in range(rhs)]
        return [(image_ref, index, index) for index in found]

    residuals = [(residual_ref, k, k) for k in range(rhs_count)]
    directions = [(direction_ref, k, k) for k in range(rhs_count)]
    images = listed(new_places)
    if not old_places:
        for a in range(rhs_count):
            tile([(0, residuals[a : a + 1], residuals[a:], True)])
    for b in range(0, len(images), 2):
        right = images[b : b + 2]
        left = images[: b + len(right)] + listed(old_places)
        tile([(1, directions, right, False), (2, residuals, right, False), (3, left, right, True)])

    gram_ref[...] = sums_before[...] + lax.dot_general(
        jnp.ones((SUBLANES, LANES), jnp.float32),
        sums_ref[...],
        (((1,), (1,)), ((), ())),
        precision=HIGHEST,
        preferred_element_type=jnp.float32,
    )


def grams(order, places, sums, residual, direction, words, rhs, images):
    rhs_count, weeks, rows, lon = direction.shape
    total = 4 * rhs_count**2
    count = len(words)
    return pl.pallas_call(
        functools.partial(gram_kernel, places, count, rhs),
        in_specs=[pl.BlockSpec(memory_space=pltpu.SMEM)] + in_vmem(3 + count + len(images)),
        out_specs=in_vmem(2),
        out_shape=[
            jax.ShapeDtypeStruct(direction.shape, jnp.float32),
            jax.ShapeDtypeStruct((SUBLANES, total), jnp.float32),
        ],
        scratch_shapes=[pltpu.VMEM((total, LANES), jnp.float32)],
        input_output_aliases={4 + count: 0} if images else {},
        compiler_params=params(14),
        cost_estimate=cost(8 * rhs_count * direction.size, 16 * direction.size),
        name="grams",
    )(order, sums, residual, direction, *words, *images)


def small_product(left, right):
    total = jnp.zeros((SUBLANES, LANES), jnp.float32)
    for j in range(SUBLANES):
        column = jnp.broadcast_to(left[:, j : j + 1], (SUBLANES, LANES))
        total = total + column * jnp.broadcast_to(right[j : j + 1, :], (SUBLANES, LANES))
    return total


def small_transpose(value):
    rest = jnp.zeros((LANES - SUBLANES, LANES), jnp.float32)
    return jnp.concatenate([value, rest], axis=0).T[:SUBLANES]


def small_solves(systems):
    line = lax.broadcasted_iota(jnp.int32, (SUBLANES, LANES), 0)
    lane = lax.broadcasted_iota(jnp.int32, (SUBLANES, LANES), 1)
    states = [matrix + pltpu.roll(right, SUBLANES, 1) for matrix, right in systems]
    for j in range(SUBLANES):
        for index, both in enumerate(states):
            column = jnp.broadcast_to(both[:, j : j + 1], (SUBLANES, LANES))
            pivot = jnp.broadcast_to(both[j : j + 1, :], (SUBLANES, LANES))
            scaled = pivot / jnp.broadcast_to(both[j : j + 1, j : j + 1], (SUBLANES, LANES))
            states[index] = jnp.where(line == j, scaled, both - column * scaled)
    return [
        jnp.where(lane < SUBLANES, pltpu.roll(both, LANES - SUBLANES, 1), 0.0) for both in states
    ]


def solve_steps(sums_ref):
    total = sums_ref.shape[1]
    size = SUBLANES
    place = lax.broadcasted_iota(jnp.int32, (size, total), 1)
    line = lax.broadcasted_iota(jnp.int32, (size, total), 0)
    spot = lax.broadcasted_iota(jnp.int32, (total, LANES), 0)
    lane = lax.broadcasted_iota(jnp.int32, (total, LANES), 1)
    sums = sums_ref[...]

    def matrix(index, turned=False):
        row, column = place % size, spot // size % size
        if not turned:
            row, column = place // size % size, spot % size
        here = (place // size**2 == index) & (row == line)
        return jnp.dot(
            jnp.where(here, sums, 0.0),
            jnp.where(column == lane, 1.0, 0.0),
            precision=HIGHEST,
            preferred_element_type=jnp.float32,
        )

    gram_old, gram_image = matrix(0), matrix(3)
    curvature = 0.5 * (matrix(1) + matrix(1, True))
    mixed, mixed_turned = matrix(2), matrix(2, True)
    diagonal = lax.broadcasted_iota(jnp.int32, (size, LANES), 0)
    identity = jnp.where(diagonal == lax.broadcasted_iota(jnp.int32, (size, LANES), 1), 1.0, 0.0)
    step, old_inverse = small_solves([(curvature, gram_old), (gram_old, identity)])
    step_turned = small_transpose(step)
    rest = small_product(gram_image, step) - mixed_turned
    gram_new = gram_old - small_product(mixed, step) + small_product(step_turned, rest)
    return step_turned, small_product(gram_new, old_inverse)


def spread_coefficients(turned):
    size = SUBLANES
    wide = 4 * size**2
    lane = lax.broadcasted_iota(jnp.int32, (size, wide), 1)
    line = lax.broadcasted_iota(jnp.int32, (size, wide), 0)
    spread = jnp.zeros((size, wide), jnp.float32)
    for b in range(size):
        column = jnp.broadcast_to(turned[:, b : b + 1], (size, wide))
        spread = spread + jnp.where(lane // size % size == b, column, 0.0)
    high = spread.astype(jnp.bfloat16).astype(jnp.float32)
    spread = jnp.where(lane < 2 * size**2, high, spread - high)
    own = (lane % size == line) & (lane < 3 * size**2)
    rows = [
        jnp.where(own, jnp.broadcast_to(spread[a : a + 1], (size, wide)), 0.0) for a in range(size)
    ]
    return jnp.concatenate(rows, axis=0)


def split_rows(ref, row):
    value = jnp.concatenate([ref[b, 0, row : row + SUBLANES, :] for b in range(ref.shape[0])], axis=0)
    high = value.astype(jnp.bfloat16)
    low = (value - high.astype(jnp.float32)).astype(jnp.bfloat16)
    return jnp.concatenate([high, low, high], axis=0)


def update_kernel(
    sums_ref, solution_ref, residual_ref, direction_ref, image_ref, sol_out, res_out, dir_out, coef_ref
):
    rhs_count, _, rows, lon = direction_ref.shape
    size = rhs_count * SUBLANES

    @pl.when(pl.program_id(0) == 0)
    def _():
        step_turned, turn_turned = solve_steps(sums_ref)
        coefs = [spread_coefficients(step_turned), spread_coefficients(turn_turned)]
        coef_ref[...] = jnp.concatenate(coefs, axis=0).astype(jnp.bfloat16)

    for row in range(0, rows, SUBLANES):
        coefs = coef_ref[:, : 3 * size]
        moves = jnp.dot(coefs, split_rows(direction_ref, row), preferred_element_type=jnp.float32)
        drops = jnp.dot(coefs[:size], split_rows(image_ref, row), preferred_element_type=jnp.float32)
        for a in range(rhs_count):
            at = a * SUBLANES
            spot = (a, 0, slice(row, row + SUBLANES), slice(None))
            sol_out[spot] = solution_ref[spot] + moves[at : at + SUBLANES]
            left = residual_ref[spot] - drops[at : at + SUBLANES]
            res_out[spot] = left
            dir_out[spot] = left + moves[size + at : size + at + SUBLANES]


def update(sums, solution, residual, direction, image):
    rhs_count, weeks, rows, lon = direction.shape
    field = pl.BlockSpec((rhs_count, 1, rows, lon), lambda w: (0, w, 0, 0))
    shape = jax.ShapeDtypeStruct(direction.shape, jnp.float32)
    return pl.pallas_call(
        update_kernel,
        grid=(weeks,),
        in_specs=[whole(sums.shape)] + [field] * 4,
        out_specs=[field] * 3,
        scratch_shapes=[pltpu.VMEM((2 * rhs_count * SUBLANES, 4 * rhs_count * SUBLANES), jnp.bfloat16)],
        out_shape=[shape] * 3,
        compiler_params=params(16),
        cost_estimate=cost(6 * rhs_count * direction.size, 28 * direction.size),
        name="update",
    )(sums, solution, residual, direction, image)


def crossed(value, axis, by):
    if by == 0:
        return value
    return lax.ppermute(value, axis, [(i, i ^ by) for i in range(lax.axis_size(axis))])


def far_first(size):
    return [1 << bit for bit in reversed(range(size.bit_length() - 1))]


def neighbours(value, axis):
    size = lax.axis_size(axis)
    outer = [(i, i + 1) for i in range(1, size - 1, 2)]
    outer += [(after, before) for before, after in outer]
    return crossed(value, axis, 1), lax.ppermute(value, axis, outer)


def summed_over(value, axis):
    bits = far_first(lax.axis_size(axis))[::-1]
    before = value
    for step in [bits[:1]] + [bits[at : at + 2] for at in range(1, len(bits), 2)]:
        before = value
        for reach in step[:1]:
            value = value + crossed(before, axis, reach)
        for reach in step[1:]:
            far = crossed(before, axis, reach) + crossed(before, axis, reach | step[0])
            value = value + far
    return value, before


def lat_windows(lat_width, band, rows):
    decay = rows / 2.0
    total = lat_width.shape[0]
    offsets = jnp.abs(jnp.arange(-rows, rows + 1)).astype(jnp.float32)
    limits = lat_width.astype(jnp.float32)
    normal = jnp.sqrt(
        jnp.sum(
            jnp.where(
                offsets[None, :] <= limits[:, None], jnp.exp(-2.0 * offsets / decay)[None, :], 0.0
            ),
            axis=1,
        )
    )
    padded_limits = jnp.pad(limits, (rows, rows), constant_values=-1.0)
    padded_normal = jnp.pad(normal, (rows, rows), constant_values=1.0)
    near_limits = lax.dynamic_slice_in_dim(padded_limits, band * rows, 3 * rows)
    near_normal = lax.dynamic_slice_in_dim(padded_normal, band * rows, 3 * rows)
    distance = jnp.abs(
        jnp.arange(rows)[:, None] + rows - jnp.arange(3 * rows)[None, :]
    ).astype(jnp.float32)
    fade = jnp.exp(-distance / decay)
    own_limits, own_normal = near_limits[rows : 2 * rows, None], near_normal[rows : 2 * rows, None]
    spread = jnp.where(distance <= own_limits, fade, 0.0) / own_normal
    pulled = jnp.where(distance <= near_limits[None, :], fade, 0.0) / near_normal[None, :]
    return spread, pulled


def shards(
    footprints,
    block_rows,
    block_cols,
    block_scale,
    lat_width,
    lon_width,
    obs_weight,
    solution,
    residual,
    direction,
):
    rhs_count, weeks, rows, lon = direction.shape
    blocks = footprints[0, 0]
    count, edge, _ = blocks.shape
    row_list = block_rows[0, 0]
    scales = jnp.exp2(-block_scale[0, 0].astype(jnp.float32))
    row_blocks = obs_weight.shape[0] // edge
    slots = lax.axis_size("obs")
    rhs = rhs_count // slots
    slab, band = lax.axis_index("obs"), lax.axis_index("lat")
    parts = lon // edge
    cols = weeks * rows * parts

    groups = chunk_of(rhs, BACK_GROUPS)
    each = rhs // groups
    order = (slab ^ jnp.arange(slots, dtype=jnp.int32)) * rhs
    own_width = lax.dynamic_slice_in_dim(lon_width, band * rows, rows)
    counts = jnp.broadcast_to(own_width[:, None] + 1, (rows, lon))

    lists = jnp.concatenate([crossed(block_cols, "obs", d) for d in range(slots)], axis=0)[:, 0]
    line, part = lists // parts, lists % parts
    places = ((line // rows) * parts + part) * rows + line % rows

    lon_own, words = spread_lon(
        lax.dynamic_slice_in_dim(direction, slab * rhs, rhs, 0), counts
    )
    halo = neighbours(words, "lat")
    hot = (places[:, :, None] == jnp.arange(cols)[None, None, :]).astype(jnp.bfloat16)
    hot_turned = (jnp.arange(cols)[:, None] == places.reshape(1, -1)).astype(jnp.bfloat16)
    lat_spread, lat_pulled = lat_windows(lat_width, band, rows)
    side = (band % 2).astype(jnp.int32).reshape(1)

    picks = spread_lat(side, lon_own, *halo, lat_spread, hot)
    cells = [crossed(picks[d], "obs", d) for d in range(slots)]
    kept = count // KEPT_OF * KEPT if count % KEPT_OF == 0 else 0
    stays = [preload(blocks, 0, kept, picks[0])] if kept else []
    near = preload(blocks, kept, count - kept, picks[0])
    sums, partial = summed_over(
        forward(row_list, scales, [*stays, near], cells, row_blocks), "lat"
    )
    near = preload(blocks, kept, count - kept, partial)
    weighted = sums.reshape(row_blocks, slots * rhs, edge) * obs_weight.reshape(row_blocks, 1, edge)
    terms = adjoint_terms(
        row_list, scales, [*stays, near], weighted.reshape(-1, edge), slots * groups, each
    )
    sent = [[crossed(terms[d * groups + g], "obs", d) for d in range(slots)] for g in range(groups)]
    own = []
    for group in range(groups):
        field, words = gather_cells(hot_turned, sent[group], each, weeks, rows, lon)
        own.append(pull_back(side, field, *neighbours(words, "lat"), lat_pulled, counts))

    starts = (order[:, None] + jnp.arange(groups, dtype=jnp.int32) * each).reshape(-1)
    products = jnp.zeros((SUBLANES, 4 * rhs_count**2), jnp.float32)
    images, places = [], ()

    def add_products(slot):
        nonlocal products, places, images
        words = [arrived[group][slot] for group in range(groups)]
        places += tuple(slot * groups + group for group in range(groups))
        *images, products = grams(
            starts, places, products, residual, direction, words, each, images
        )

    arrived = [{0: words} for words in own]
    for group in range(groups):
        for reach in far_first(slots):
            arrived[group][reach] = crossed(own[group], "obs", reach)
    add_products(0)
    first_products = products
    for reach in far_first(slots)[1:]:
        for group in range(groups):
            for bits in [bits for bits in arrived[group] if bits > reach and not bits % (2 * reach)]:
                words = arrived[group][bits]
                if group == groups - 1:
                    words, _ = lax.optimization_barrier((words, first_products))
                arrived[group][bits | reach] = crossed(words, "obs", reach)
    for slot in range(1, slots):
        add_products(slot)
    products, _ = summed_over(products, "lat")
    return tuple(update(products, solution, residual, direction, *images))


def solution(mesh):
    return jax.shard_map(
        shards,
        mesh=mesh,
        in_specs=(
            P("obs", "lat", None, None, None),
            P("obs", "lat", None),
            P("obs", "lat", None),
            P("obs", "lat", None),
            P(),
            P(),
            P("obs"),
            P(None, None, "lat", None),
            P(None, None, "lat", None),
            P(None, None, "lat", None),
        ),
        out_specs=(
            P(None, None, "lat", None),
            P(None, None, "lat", None),
            P(None, None, "lat", None),
        ),
        check_vma=False,
    )
```
